32 devices in a mesh: dp: 2 (over x), fsdp: 16 (over z, y, core).
Axes of the slice: x: 2, y: 2, z: 4, core: 2. Of those that a mesh axis runs over, the one named last changes fastest.
Arguments:
- patches: bfloat16 [32, 512, 768], P(('dp', 'fsdp')), may hold values from -6 to 6
- counts: int32 [32], P(('dp', 'fsdp')), may hold values from 128 to 512, as said below
- cotangent: bfloat16 [32, 512, 768], P(('dp', 'fsdp')), may hold values from -6 to 6
- w_attn: float32 [4, 768, 768], P(None, 'fsdp')
- w_in: float32 [2, 768, 2048], P(None, 'fsdp'), may hold values from -0.21875 to 0.21875
- w_down: float32 [2048, 768], P('fsdp'), may hold values from -0.125 to 0.125
- gains: float32 [2, 768], P(None, 'fsdp')
- m_attn: float32 [4, 768, 768], P(None, 'fsdp'), may hold values from -0.00024414062 to 0.00024414062
- m_in: float32 [2, 768, 2048], P(None, 'fsdp'), may hold values from -0.00024414062 to 0.00024414062
- m_down: float32 [2048, 768], P('fsdp'), may hold values from -0.00024414062 to 0.00024414062
- m_gains: float32 [2, 768], P(None, 'fsdp'), may hold values from -0.0007324219 to 0.0007324219
- v_attn: float32 [4, 768, 768], P(None, 'fsdp'), may hold values from 1.4125442e-10 to 5.650177e-10
- v_in: float32 [2, 768, 2048], P(None, 'fsdp'), may hold values from 1.4125443e-11 to 5.6501772e-11
- v_down: float32 [2048, 768], P('fsdp'), may hold values from 1.4125442e-10 to 5.650177e-10
- v_gains: float32 [2, 768], P(None, 'fsdp'), may hold values from 7.062721e-11 to 2.8250885e-10
Outputs:
- output: bfloat16 [32, 512, 768], P(('dp', 'fsdp'))
- input_grad: bfloat16 [32, 512, 768], P(('dp', 'fsdp'))
- grad_norm: float32 [], replicated
- new_attn: float32 [4, 768, 768], P(None, 'fsdp')
- new_in: float32 [2, 768, 2048], P(None, 'fsdp')
- new_down: float32 [2048, 768], P('fsdp')
- new_gains: float32 [2, 768], P(None, 'fsdp')
- first_attn: float32 [4, 768, 768], P(None, 'fsdp')
- first_in: float32 [2, 768, 2048], P(None, 'fsdp')
- first_down: float32 [2048, 768], P('fsdp')
- first_gains: float32 [2, 768], P(None, 'fsdp')
- second_attn: float32 [4, 768, 768], P(None, 'fsdp')
- second_in: float32 [2, 768, 2048], P(None, 'fsdp')
- second_down: float32 [2048, 768], P('fsdp')
- second_gains: float32 [2, 768], P(None, 'fsdp')
The draws below stay inside these ranges and needn't reach their ends.
Inputs may be any that keep to these rules, and one draw needn't show every extreme that they name: Image i's valid patches are its first counts[i] slots, the others padding; in every draw some image has all 512 slots valid.
All inputs are finite; a program needn't handle non-finite values.
Results may differ from the reference program's by a relative error of at most 0.02.
The reference program's roundings to bfloat16 on the way count: a program that leaves them out, or rounds other values in their place, can miss the bound.
Values may be sent and summed in bfloat16 or wider, within the bound.
No kernel may reach another device: no remote copies, remote signals or barrier semaphores. Data moves between devices by JAX's collectives and lax.ppermute only.
A program may use at most 192 MiB of HBM per device.

```python
import math
import jax
import jax.numpy as jnp
from jax import lax

D = 768
H = 12
HD = 64
FF = 2048
S = 512
STEP = 10
IMAGES = 32


def draw_counts(key, part):
    key = jax.random.fold_in(key, 11)
    first_key, second_key = jax.random.split(key)
    drawn = jax.random.randint(first_key, (IMAGES,), S // 4, S + 1)
    full_at = jax.random.randint(second_key, (), 0, IMAGES)
    return jnp.where(jnp.arange(IMAGES) == full_at, S, drawn).astype(jnp.int32)


def draw_w_attn(key, part):
    key = jax.random.fold_in(key, 7)
    scales = jnp.array([(8.0 * D) ** (-0.5), (8.0 * D) ** (-0.5), (1.0 * D) ** (-0.5), (D / 4.0) ** (-0.5)], jnp.float32)
    base = jax.random.truncated_normal(key, -4.0, 4.0, (4, D, D), jnp.float32)
    return base * scales[:, None, None]


def draw_gains(key, part):
    key = jax.random.fold_in(key, 5)
    ramp = 1.0 + 0.8 * jnp.arange(D, dtype=jnp.float32) / (D - 1)
    jitter = jax.random.uniform(key, (2, D), jnp.float32, 0.7, 1.3)
    return ramp[None, :] * jitter


def block_levels(own_key, extent, pieces, least, high):
    level = 1.0
    for dim, parts in pieces:
        heights = jax.random.uniform(jax.random.fold_in(jax.random.fold_in(own_key, 6), dim), (parts,), jnp.float32, least / len(pieces), high / len(pieces))
        level = level * jnp.repeat(jnp.exp(heights), extent[dim] // parts).reshape((-1,) + (1,) * (len(extent) - 1 - dim))
    return level


def centred(own_key, extent, scale, reach, cuts=(), held_as=jnp.bfloat16):
    values = scale * jax.random.normal(own_key, extent, jnp.float32)
    if cuts:
        values = values * block_levels(own_key, extent, cuts, -0.22, 0.18)
    return jnp.clip(values, -reach, reach).astype(held_as)


def setup_inputs(seed: int = 0) -> dict:
    key_of = jax.random.split(jax.random.key(seed), 16)
    return {
        "patches": centred(key_of[0], (IMAGES, S, D), 1.0, 6.0, ((0, 32),)),
        "counts": draw_counts(jax.random.fold_in(key_of[15], 71), 0),
        "cotangent": centred(key_of[2], (IMAGES, S, D), 1.0, 6.0, ((0, 32),)),
        "w_attn": draw_w_attn(jax.random.fold_in(key_of[15], 71), 0),
        "w_in": centred(key_of[4], (2, D, FF), D ** -0.5, 0.21875, ((1, 16),), jnp.float32),
        "w_down": centred(key_of[5], (FF, D), FF ** -0.5, 0.125, ((0, 16),), jnp.float32),
        "gains": draw_gains(jax.random.fold_in(key_of[15], 71), 0),
        "m_attn": centred(key_of[7], (4, D, D), (0.11 / (4*D*D + 3*D*FF + 2*D) ** 0.5), 0.00024414062, ((1, 16),), jnp.float32),
        "m_in": centred(key_of[8], (2, D, FF), (0.11 / (4*D*D + 3*D*FF + 2*D) ** 0.5), 0.00024414062, ((1, 16),), jnp.float32),
        "m_down": centred(key_of[9], (FF, D), (0.11 / (4*D*D + 3*D*FF + 2*D) ** 0.5), 0.00024414062, ((0, 16),), jnp.float32),
        "m_gains": centred(key_of[10], (2, D), (0.33 / (4*D*D + 3*D*FF + 2*D) ** 0.5), 0.0007324219, ((1, 16),), jnp.float32),
        "v_attn": jnp.clip(jnp.exp(math.log(5.650176992944012e-10) - 1.3862944 * jax.random.uniform(key_of[11], (4, D, D), jnp.float32) ** block_levels(key_of[11], (4, D, D), ((1, 16),), -0.2, 0.2)), 1.412544248236003e-10, 5.650176992944012e-10),
        "v_in": jnp.clip(jnp.exp(math.log(5.6501772011108287e-11) - 1.3862944 * jax.random.uniform(key_of[12], (2, D, FF), jnp.float32) ** block_levels(key_of[12], (2, D, FF), ((1, 16),), -0.2, 0.2)), 1.4125443002777072e-11, 5.6501772011108287e-11),
        "v_down": jnp.clip(jnp.exp(math.log(5.650176992944012e-10) - 1.3862944 * jax.random.uniform(key_of[13], (FF, D), jnp.float32) ** block_levels(key_of[13], (FF, D), ((0, 16),), -0.2, 0.2)), 1.412544248236003e-10, 5.650176992944012e-10),
        "v_gains": jnp.clip(jnp.exp(math.log(2.825088496472006e-10) - 1.3862944 * jax.random.uniform(key_of[14], (2, D), jnp.float32) ** block_levels(key_of[14], (2, D), ((1, 16),), -0.2, 0.2)), 7.062721241180014e-11, 2.825088496472006e-10),
    }


@jax.custom_vjp
def low(v):
    return lax.optimization_barrier(v.astype(jnp.bfloat16)).astype(jnp.float32)

@jax.custom_vjp
def low_back(v):
    return v

def low_keep(v):
    return (low(v), None)

def low_pass(kept, grad):
    return (grad,)

def back_keep(v):
    return (v, None)

def back_low(kept, grad):
    return (low(grad),)
low.defvjp(low_keep, low_pass)
low_back.defvjp(back_keep, back_low)
NORM_EPS = 1e-06
MASKED = -1000000000.0
BETA_ONE = 0.9
BETA_TWO = 0.999
ADAM_EPS = 1e-08
CLIP_AT = 1.0
MATRIX_RATE = 0.04
MATRIX_DECAY = 0.1
GAIN_RATE = 0.8

def product(left, right):
    return jnp.dot(left, right, precision=lax.Precision.HIGHEST)

def rms_scale(values, gain):
    return values * lax.rsqrt(lax.optimization_barrier(jnp.mean(values * values, -1, keepdims=True)) + NORM_EPS) * gain

def layer(image, count, attn, inner, down, gain):
    length = image.shape[0]
    valid = jnp.arange(length) < count
    row_mask = valid.astype(image.dtype)[:, None]
    normed = low(rms_scale(image, gain[0]))
    queries = low(low_back(product(normed, attn[0]))).reshape(length, H, HD)
    keys = low(low_back(product(normed, attn[1]))).reshape(length, H, HD)
    values = low(low_back(product(normed, attn[2]))).reshape(length, H, HD)
    scores = low_back(jnp.einsum('qhd,khd->hqk', queries, keys, precision=lax.Precision.HIGHEST))
    scores = jnp.where(valid[None, None, :], scores, MASKED)
    probs = jax.nn.softmax(scores, axis=-1)
    context = jnp.einsum('hqk,khd->qhd', low(probs), values, precision=lax.Precision.HIGHEST)
    context = low(low_back(context.reshape(length, H * HD)))
    attended = image + low_back(product(context, attn[3]))
    normed_two = low(rms_scale(attended, gain[1]))
    gate = low_back(product(normed_two, inner[0]))
    up_part = low_back(product(normed_two, inner[1]))
    hidden = low(jax.nn.gelu(gate, approximate=True) * up_part)
    return row_mask * (attended + product(hidden, down))

def adamw(param, first, second, grad, rate, decay):
    first = BETA_ONE * first + (1.0 - BETA_ONE) * grad
    second = BETA_TWO * second + (1.0 - BETA_TWO) * grad * grad
    update = first / (1.0 - BETA_ONE ** STEP) / (jnp.sqrt(second / (1.0 - BETA_TWO ** STEP)) + ADAM_EPS)
    return (param - rate * (update + decay * param), first, second)

def reference(patches, counts, cotangent, w_attn, w_in, w_down, gains, m_attn, m_in, m_down, m_gains, v_attn, v_in, v_down, v_gains):
    images = patches.astype(jnp.float32)

    def forward_all(inputs, attn, inner, down, gain):
        attn, inner, down, gain = (low(attn), low(inner), low(down), low(gain))

        def per_image(item):
            return layer(item[0], item[1], attn, inner, down, gain)
        return lax.map(jax.checkpoint(per_image), (inputs, counts))
    result, pull = jax.vjp(forward_all, images, w_attn, w_in, w_down, gains)
    d_images, g_attn, g_in, g_down, g_gains = pull(cotangent.astype(jnp.float32))
    grads = (g_attn, g_in, g_down, g_gains)
    grad_norm = jnp.sqrt(sum((jnp.sum(grad * grad) for grad in grads)))
    factor = jnp.minimum(1.0, CLIP_AT / (grad_norm + 1e-06))
    params = (w_attn, w_in, w_down, gains)
    firsts = (m_attn, m_in, m_down, m_gains)
    seconds = (v_attn, v_in, v_down, v_gains)
    rates = (MATRIX_RATE, MATRIX_RATE, MATRIX_RATE, GAIN_RATE)
    decays = (MATRIX_DECAY, MATRIX_DECAY, MATRIX_DECAY, 0.0)
    updated = [adamw(params[n], firsts[n], seconds[n], grads[n] * factor, rates[n], decays[n]) for n in range(4)]
    return (result.astype(jnp.bfloat16), d_images.astype(jnp.bfloat16), grad_norm, updated[0][0], updated[1][0], updated[2][0], updated[3][0], updated[0][1], updated[1][1], updated[2][1], updated[3][1], updated[0][2], updated[1][2], updated[2][2], updated[3][2])
```

```python
import functools

import jax
import jax.numpy as jnp
from jax import lax
from jax.experimental import pallas as pl
from jax.experimental.pallas import tpu as pltpu
from jax.sharding import PartitionSpec as P

HD = 64
STEP = 10


NORM_EPS = 1e-06
MASKED = -1000000000.0
BETA_ONE = 0.9
BETA_TWO = 0.999
ADAM_EPS = 1e-08
CLIP_AT = 1.0
MATRIX_RATE = 0.04
MATRIX_DECAY = 0.1
GAIN_RATE = 0.8


def rms_scale(values, gain):
    return values * lax.rsqrt(jnp.mean(values * values, -1, keepdims=True) + NORM_EPS) * gain


def gated_unit(gate, up_part):
    return jax.nn.gelu(gate, approximate=True) * up_part


def split_heads(block, head_size):
    return block.reshape(block.shape[0], block.shape[1] // head_size, head_size)


def head_scores(queries, keys, valid):
    scores = jnp.einsum("qhd,khd->hqk", queries, keys, preferred_element_type=jnp.float32)
    return jnp.where(valid[None, None, :], scores, MASKED)


def attend_forward(qkv, valid, head_size):
    length, width_all = (qkv.shape[1], qkv.shape[2])
    width = 2 * head_size

    def one_pair(index):
        parts = lax.dynamic_slice_in_dim(qkv, index * width, width, 2)
        queries = split_heads(parts[0], head_size)
        keys = split_heads(parts[1], head_size)
        values = split_heads(parts[2], head_size)
        scores = head_scores(queries, keys, valid)
        top = jnp.max(scores, -1, keepdims=True)
        expd = jnp.exp(scores - top)
        total = jnp.sum(expd, -1, keepdims=True)
        probs = (expd / total).astype(jnp.bfloat16)
        context = jnp.einsum("hqk,khd->qhd", probs, values, preferred_element_type=jnp.float32)
        return (context.reshape(length, width), top + jnp.log(total))

    contexts, logsums = lax.map(one_pair, jnp.arange(width_all // width))
    context = jnp.swapaxes(contexts, 0, 1).reshape(length, width_all).astype(jnp.bfloat16)
    return (context, logsums)


def attend_backward(qkv, d_context, logsums, valid, head_size):
    length, width_all = (qkv.shape[1], qkv.shape[2])
    width = 2 * head_size

    def one_pair(item):
        index, logsum = item
        parts = lax.dynamic_slice_in_dim(qkv, index * width, width, 2)
        queries = split_heads(parts[0], head_size)
        keys = split_heads(parts[1], head_size)
        values = split_heads(parts[2], head_size)
        d_out = split_heads(lax.dynamic_slice_in_dim(d_context, index * width, width, 1), head_size)
        probs = jnp.exp(head_scores(queries, keys, valid) - logsum)
        d_probs = jnp.einsum("qhd,khd->hqk", d_out, values, preferred_element_type=jnp.float32)
        d_values = jnp.einsum(
            "hqk,qhd->khd", probs.astype(jnp.bfloat16), d_out, preferred_element_type=jnp.float32
        )
        d_scores = (probs * (d_probs - jnp.sum(probs * d_probs, -1, keepdims=True))).astype(
            jnp.bfloat16
        )
        d_queries = jnp.einsum("hqk,khd->qhd", d_scores, keys, preferred_element_type=jnp.float32)
        d_keys = jnp.einsum("hqk,qhd->khd", d_scores, queries, preferred_element_type=jnp.float32)
        return jnp.stack((d_queries, d_keys, d_values)).reshape(3, length, width)

    pieces = lax.map(one_pair, (jnp.arange(width_all // width), logsums))
    return jnp.transpose(pieces, (1, 2, 0, 3)).reshape(3, length, width_all).astype(jnp.bfloat16)


def adamw(param, first, second, grad, rate, decay):
    first = BETA_ONE * first + (1.0 - BETA_ONE) * grad
    second = BETA_TWO * second + (1.0 - BETA_TWO) * grad * grad
    update = first / (1.0 - BETA_ONE**STEP) / (jnp.sqrt(second / (1.0 - BETA_TWO**STEP)) + ADAM_EPS)
    return (param - rate * (update + decay * param), first, second)


EVERY = ("dp", "fsdp")


class Grid:
    def __init__(self, dp, fsdp):
        self.dp, self.fsdp = dp, fsdp
        self.nz = fsdp // 4
        power = self.nz & (self.nz - 1) == 0
        self.cube = dp == 2 and fsdp % 4 == 0 and self.nz % 2 == 0 and power

    def move(self, step):
        pairs = []
        for source in range(self.dp * self.fsdp):
            x, rest = divmod(source, self.fsdp)
            z, rest = divmod(rest, 4)
            y, core = divmod(rest, 2)
            x, z, y, core = step(x, z, y, core)
            pairs.append((source, x * self.fsdp + (z * 2 + y) * 2 + core))
        return pairs

    def flip_x(self, v):
        return lax.ppermute(v, EVERY, self.move(lambda x, z, y, c: (1 - x, z, y, c)))

    def flip_y(self, v):
        return lax.ppermute(v, EVERY, self.move(lambda x, z, y, c: (x, z, 1 - y, c)))

    def flip_core(self, v):
        return lax.ppermute(v, EVERY, self.move(lambda x, z, y, c: (x, z, y, 1 - c)))

    def shift_z(self, v, by):
        return lax.ppermute(v, EVERY, self.move(lambda x, z, y, c: (x, (z + by) % self.nz, y, c)))

    def swap_z(self, v, bit):
        return lax.ppermute(v, EVERY, self.move(lambda x, z, y, c: (x, z ^ bit, y, c)))

    def place(self):
        x, f = lax.axis_index("dp"), lax.axis_index("fsdp")
        return x, f // 4, f // 2 % 2, f % 2


def spread(grid, part):
    half = grid.nz // 2
    column = jnp.stack([part] + [grid.shift_z(part, k) for k in range(1, grid.nz)])
    side = grid.flip_x(column)
    across = grid.flip_y(column)
    corner_low = grid.flip_x(across[:half])
    corner_high = grid.flip_y(side[half:])
    mine = [column, side, across, corner_low, corner_high]
    return mine + [grid.flip_core(piece) for piece in mine]


def piece_places(grid):
    nz, half = grid.nz, grid.nz // 2
    spots = [(0, 0, 0, nz), (1, 0, 0, nz), (0, 1, 0, nz), (1, 1, 0, half), (1, 1, half, nz - half)]
    return [(dx, dy, dc, low, n) for dc in (0, 1) for dx, dy, low, n in spots]


def assemble(grid, pieces):
    rows, columns = pieces[0].shape[1:]
    places = piece_places(grid)

    def body(*refs):
        ins, out, sem = refs[: len(pieces)], refs[len(pieces)], refs[len(pieces) + 1]
        x, z, y, c = grid.place()
        for ref, (dx, dy, dc, low, n) in zip(ins, places):
            for level in range(n):
                owner_z = lax.rem(z - (low + level) + grid.nz, grid.nz)
                owner = (owner_z * 2 + lax.rem(y + dy, 2)) * 2 + lax.rem(c + dc, 2)
                pltpu.make_async_copy(ref.at[level], out.at[lax.rem(x + dx, 2), owner], sem).start()
        pltpu.make_async_copy(out, out, sem).wait()

    return pl.pallas_call(
        body,
        out_shape=jax.ShapeDtypeStruct((2, grid.fsdp, rows, columns), pieces[0].dtype),
        in_specs=[pl.BlockSpec(memory_space=pl.ANY)] * len(pieces),
        out_specs=pl.BlockSpec(memory_space=pl.ANY),
        scratch_shapes=[pltpu.SemaphoreType.DMA],
        name="assemble",
    )(*pieces)


def reduce_group(grid, grads):
    if not grid.cube:
        owned = lax.psum_scatter(grads.astype(jnp.float32), "fsdp", scatter_dimension=1)
        return lax.psum(owned.astype(jnp.bfloat16), "dp")
    x, z, y, c = grid.place()
    half = grid.nz // 2
    grads = grads.reshape((2, grid.nz, 2, 2) + grads.shape[2:])
    got = grid.flip_core(lax.dynamic_index_in_dim(grads, 1 - c, 3, False))
    keep = lax.dynamic_index_in_dim(grads, c, 3, False)

    def block(h, at_y, low, n):
        total = 0.0
        for array in (keep, got):
            part = lax.dynamic_index_in_dim(array, h, 0, False)[low : low + n]
            total = total + lax.dynamic_index_in_dim(part, at_y, 1, False).astype(jnp.float32)
        return total

    def low(v):
        return v.astype(jnp.bfloat16)

    nz = grid.nz
    in_x = grid.flip_x(low(block(1 - x, 1 - y, 0, half)))
    in_y = grid.flip_y(low(block(1 - x, 1 - y, half, nz - half)))
    to_x = jnp.concatenate(
        [block(1 - x, y, 0, half), block(1 - x, y, half, nz - half) + in_y.astype(jnp.float32)]
    )
    to_y = jnp.concatenate(
        [block(x, 1 - y, 0, half) + in_x.astype(jnp.float32), block(x, 1 - y, half, nz - half)]
    )
    got_x, got_y = grid.flip_x(low(to_x)), grid.flip_y(low(to_y))
    column = low(block(x, y, 0, nz) + got_x.astype(jnp.float32) + got_y.astype(jnp.float32))
    total = lax.dynamic_index_in_dim(column, z, 0, False).astype(jnp.float32)
    for k in range(1, nz):
        out = lax.dynamic_index_in_dim(column, lax.rem(z + k, nz), 0, False)
        total = total + grid.shift_z(out, k).astype(jnp.float32)
    return low(total)


def both_halves(grid, total):
    x = lax.axis_index("dp")
    other = grid.flip_x(total)
    return jnp.stack([jnp.where(x == 0, total, other), jnp.where(x == 0, other, total)])


def total_of(grid, value):
    if not grid.cube:
        return lax.psum(value, "fsdp")
    value = grid.flip_core(value) + value
    value = grid.flip_x(value) + value
    value = grid.flip_y(value) + value
    bit = 1
    while bit < grid.nz:
        value = grid.swap_z(value, bit) + value
        bit *= 2
    return value


def split_columns(v):
    return jnp.moveaxis(v.reshape(v.shape[:-1] + (2, v.shape[-1] // 2)), -2, 0)


def join_columns(v):
    moved = jnp.moveaxis(v, 0, -2)
    return moved.reshape(moved.shape[:-2] + (2 * v.shape[-1],))


def on_device(grid,
    patches,
    counts,
    cotangent,
    w_attn,
    w_in,
    w_down,
    gains,
    m_attn,
    m_in,
    m_down,
    m_gains,
    v_attn,
    v_in,
    v_down,
    v_gains,
):
    head_size = HD
    inputs = patches[0].astype(jnp.float32)
    length = inputs.shape[0]
    valid = jnp.arange(length) < counts[0]
    row_mask = valid.astype(jnp.float32)[:, None]
    low_attn = w_attn.astype(jnp.bfloat16)
    low_in = w_in.astype(jnp.bfloat16)
    low_down = w_down.astype(jnp.bfloat16)
    low_gains = gains.astype(jnp.bfloat16)
    x = lax.axis_index("dp")
    rows = low_attn.shape[1]
    wide = low_down.shape[0]
    ups = low_in.shape[2] // 2
    columns = inputs.shape[1] // 2
    gain_rows = jnp.pad(low_gains, ((0, 14), (0, 2 * columns - rows)))
    first_part = jnp.concatenate([low_attn[0], low_attn[1], low_attn[2], gain_rows], 0)
    second_part = jnp.concatenate([low_attn[3], low_down], 0)
    third_part = jnp.concatenate([low_in[0], low_in[1]], 0)
    first_part, second_part, third_part = (
        split_columns(p) for p in (first_part, second_part, third_part)
    )
    if grid.cube:
        first_pieces = spread(grid, lax.dynamic_index_in_dim(first_part, x, 0, False))
        second_part, first_pieces[0] = lax.optimization_barrier((second_part, first_pieces[0]))
        second_pieces = spread(grid, lax.dynamic_index_in_dim(second_part, x, 0, False))
        third_part, second_pieces[0] = lax.optimization_barrier((third_part, second_pieces[0]))
        third_pieces = spread(grid, lax.dynamic_index_in_dim(third_part, x, 0, False))
        first_full = assemble(grid, first_pieces)
        second_full = assemble(grid, second_pieces)
        third_full = assemble(grid, third_pieces)
    else:
        first_full, second_full, third_full = (
            lax.all_gather(p, "fsdp", axis=1) for p in (first_part, second_part, third_part)
        )

    def whole(full, low, n):
        return join_columns(full[:, :, low : low + n].reshape(2, grid.fsdp * n, full.shape[3]))

    qkv_full = [whole(first_full, j * rows, rows) for j in range(3)]
    attn_full = jnp.stack(qkv_full + [whole(second_full, 0, rows)])
    down_full = whole(second_full, rows, wide)
    in_full = jnp.stack([whole(third_full, j * rows, rows) for j in range(2)])
    gain_full = jnp.swapaxes(first_full[0, :, 3 * rows : 3 * rows + 2, :rows], 0, 1).reshape(2, -1)
    normed = rms_scale(inputs, gain_full[0].astype(jnp.float32)).astype(jnp.bfloat16)
    qkv = jnp.einsum(
        "sd,jde->jse", normed, attn_full[:3], preferred_element_type=jnp.float32
    ).astype(jnp.bfloat16)
    context, logsums = attend_forward(qkv, valid, head_size)
    attended = inputs + jnp.dot(context, attn_full[3], preferred_element_type=jnp.float32)
    normed_two = rms_scale(attended, gain_full[1].astype(jnp.float32)).astype(jnp.bfloat16)
    gate_up = jnp.einsum("sd,jdf->jsf", normed_two, in_full, preferred_element_type=jnp.float32)
    hidden = gated_unit(gate_up[0], gate_up[1]).astype(jnp.bfloat16)
    result = row_mask * (attended + jnp.dot(hidden, down_full, preferred_element_type=jnp.float32))
    output = result.astype(jnp.bfloat16)[None]
    attn_back, in_back, down_back, gain_back = attn_full, in_full, down_full, gain_full
    d_result = (row_mask * cotangent[0].astype(jnp.float32)).astype(jnp.bfloat16)
    g_down = jnp.einsum("sf,sd->fd", hidden, d_result, preferred_element_type=jnp.float32)
    d_hidden = jnp.einsum("sd,fd->sf", d_result, down_back, preferred_element_type=jnp.float32)
    unused, pull_gate = jax.vjp(gated_unit, gate_up[0], gate_up[1])
    d_gate, d_up = pull_gate(d_hidden)
    d_gate_up = jnp.stack((d_gate, d_up)).astype(jnp.bfloat16)
    g_in = jnp.einsum("sd,jsf->jdf", normed_two, d_gate_up, preferred_element_type=jnp.float32)
    d_normed_two = jnp.einsum("jsf,jdf->sd", d_gate_up, in_back, preferred_element_type=jnp.float32)
    unused, pull_two = jax.vjp(rms_scale, attended, gain_back[1].astype(jnp.float32))
    d_norm_two, g_gain_two = pull_two(d_normed_two)
    d_attended = d_result.astype(jnp.float32) + d_norm_two
    d_attended_low = d_attended.astype(jnp.bfloat16)
    g_out = jnp.einsum("sd,se->de", context, d_attended_low, preferred_element_type=jnp.float32)
    d_context = jnp.einsum(
        "se,de->sd", d_attended_low, attn_back[3], preferred_element_type=jnp.float32
    ).astype(jnp.bfloat16)
    d_qkv = attend_backward(qkv, d_context, logsums, valid, head_size)
    g_qkv = jnp.einsum("sd,jse->jde", normed, d_qkv, preferred_element_type=jnp.float32)
    d_normed = jnp.einsum("jse,jde->sd", d_qkv, attn_back[:3], preferred_element_type=jnp.float32)
    unused, pull_one = jax.vjp(rms_scale, inputs, gain_back[0].astype(jnp.float32))
    d_norm_one, g_gain_one = pull_one(d_normed)
    input_grad = (d_attended + d_norm_one).astype(jnp.bfloat16)[None]
    g_gains = jnp.stack((g_gain_one, g_gain_two))
    params = (w_attn, w_in, w_down, gains)
    firsts = (m_attn, m_in, m_down, m_gains)
    seconds = (v_attn, v_in, v_down, v_gains)
    rates = (MATRIX_RATE, MATRIX_RATE, MATRIX_RATE, GAIN_RATE)
    decays = (MATRIX_DECAY, MATRIX_DECAY, MATRIX_DECAY, 0.0)
    def parts(g, n):
        return split_columns(g.astype(jnp.bfloat16).reshape(grid.fsdp, n, g.shape[1]))

    gain_slab = jnp.swapaxes(g_gains.astype(jnp.bfloat16).reshape(2, grid.fsdp, rows), 0, 1)
    gain_slab = jnp.pad(gain_slab, ((0, 0), (0, 14), (0, columns - rows)))
    gain_slab = jnp.stack([gain_slab, jnp.zeros_like(gain_slab)])
    first = jnp.concatenate([parts(g_qkv[j], rows) for j in range(3)] + [gain_slab], 2)
    second = jnp.concatenate([parts(g_out, rows), parts(g_down, wide)], 2)
    third = jnp.concatenate([parts(g_in[j], rows) for j in range(2)], 2)
    third = reduce_group(grid, third)
    second = reduce_group(grid, second)
    first = reduce_group(grid, first)
    squares = sum((jnp.sum(jnp.square(g.astype(jnp.float32))) for g in (first, second, third)))
    grad_norm = jnp.sqrt(total_of(grid, squares))
    if grid.cube:
        first, second, third = (both_halves(grid, g) for g in (first, second, third))
    first, second, third = (join_columns(g).astype(jnp.float32) for g in (first, second, third))
    owned = (
        jnp.stack([first[j * rows : (j + 1) * rows] for j in range(3)] + [second[:rows]]),
        jnp.stack([third[j * rows : (j + 1) * rows] for j in range(2)]),
        second[rows:],
        first[3 * rows : 3 * rows + 2, :rows],
    )
    factor = jnp.minimum(1.0, CLIP_AT / (grad_norm + 1e-06))
    updated = [
        adamw(params[n], firsts[n], seconds[n], owned[n] * factor, rates[n], decays[n])
        for n in range(4)
    ]
    return (
        output,
        input_grad,
        grad_norm,
        updated[0][0],
        updated[1][0],
        updated[2][0],
        updated[3][0],
        updated[0][1],
        updated[1][1],
        updated[2][1],
        updated[3][1],
        updated[0][2],
        updated[1][2],
        updated[2][2],
        updated[3][2],
    )


def solution(mesh):
    placed = (
        P(("dp", "fsdp"), None, None),
        P(("dp", "fsdp")),
        P(("dp", "fsdp"), None, None),
        P(None, "fsdp", None),
        P(None, "fsdp", None),
        P("fsdp", None),
        P(None, "fsdp"),
        P(None, "fsdp", None),
        P(None, "fsdp", None),
        P("fsdp", None),
        P(None, "fsdp"),
        P(None, "fsdp", None),
        P(None, "fsdp", None),
        P("fsdp", None),
        P(None, "fsdp"),
    )
    grid = Grid(mesh.shape["dp"], mesh.shape["fsdp"])
    return jax.shard_map(
        functools.partial(on_device, grid),
        mesh=mesh,
        in_specs=placed,
        out_specs=(
            P(("dp", "fsdp"), None, None),
            P(("dp", "fsdp"), None, None),
            P(),
            P(None, "fsdp", None),
            P(None, "fsdp", None),
            P("fsdp", None),
            P(None, "fsdp"),
            P(None, "fsdp", None),
            P(None, "fsdp", None),
            P("fsdp", None),
            P(None, "fsdp"),
            P(None, "fsdp", None),
            P(None, "fsdp", None),
            P("fsdp", None),
            P(None, "fsdp"),
        ),
        check_vma=False,
    )
```

```python
import functools
import math

import jax
import jax.numpy as jnp
from jax import lax
from jax.experimental import pallas as pl
from jax.experimental.pallas import tpu as pltpu
from jax.sharding import PartitionSpec as P

HD = 64
STEP = 10


NORM_EPS = 1e-06
MASKED = -1000000000.0
BETA_ONE = 0.9
BETA_TWO = 0.999
ADAM_EPS = 1e-08
CLIP_AT = 1.0
MATRIX_RATE = 0.04
MATRIX_DECAY = 0.1
GAIN_RATE = 0.8

EVERY = ("dp", "fsdp")
LOW = jnp.bfloat16
WIDE = jnp.float32
SLAB = 16
VMEM_LIMIT = 56 * 1024 * 1024
ANYWHERE = pl.BlockSpec(memory_space=pl.ANY)


class Grid:
    def __init__(self, dp, fsdp):
        self.dp, self.fsdp = dp, fsdp
        self.nz = fsdp // 4
        power = self.nz & (self.nz - 1) == 0
        self.cube = dp == 2 and fsdp % 4 == 0 and self.nz % 2 == 0 and power

    def move(self, step):
        pairs = []
        for source in range(self.dp * self.fsdp):
            x, rest = divmod(source, self.fsdp)
            z, rest = divmod(rest, 4)
            y, core = divmod(rest, 2)
            x, z, y, core = step(x, z, y, core)
            pairs.append((source, x * self.fsdp + (z * 2 + y) * 2 + core))
        return pairs

    def flip_x(self, v):
        return lax.ppermute(v, EVERY, self.move(lambda x, z, y, c: (1 - x, z, y, c)))

    def flip_y(self, v):
        return lax.ppermute(v, EVERY, self.move(lambda x, z, y, c: (x, z, 1 - y, c)))

    def flip_core(self, v):
        return lax.ppermute(v, EVERY, self.move(lambda x, z, y, c: (x, z, y, 1 - c)))

    def shift_z(self, v, by):
        return lax.ppermute(v, EVERY, self.move(lambda x, z, y, c: (x, (z + by) % self.nz, y, c)))

    def swap_z(self, v, bit):
        return lax.ppermute(v, EVERY, self.move(lambda x, z, y, c: (x, z ^ bit, y, c)))

    def place(self):
        x, f = lax.axis_index("dp"), lax.axis_index("fsdp")
        return x, f // 4, lax.rem(f // 2, 2), lax.rem(f, 2)


def spread(grid, part):
    half = grid.nz // 2
    column = jnp.stack([part] + [grid.shift_z(part, k) for k in range(1, grid.nz)])
    side = grid.flip_x(column)
    across = grid.flip_y(column)
    corner_low = grid.flip_x(across[:half])
    corner_high = grid.flip_y(side[half:])
    mine = [column, side, across, corner_low, corner_high]
    return mine + [grid.flip_core(piece) for piece in mine]


def piece_places(grid):
    nz, half = grid.nz, grid.nz // 2
    spots = [(0, 0, 0, nz), (1, 0, 0, nz), (0, 1, 0, nz), (1, 1, 0, half), (1, 1, half, nz - half)]
    return [(dx, dy, dc, low, n) for dc in (0, 1) for dx, dy, low, n in spots]


def gather_groups(grid, groups):
    if not grid.cube:
        return [lax.all_gather(split_columns(g), "fsdp", axis=1) for g in groups]
    x = lax.axis_index("dp")
    parts = [lax.dynamic_index_in_dim(split_columns(g), x, 0, False) for g in groups]
    pieces = []
    for n, part in enumerate(parts):
        if n:
            part, pieces[-1][0] = lax.optimization_barrier((part, pieces[-1][0]))
        pieces.append(spread(grid, part))
    return pieces


def reduce_group(grid, keep, sent):
    x, z, y, c = grid.place()
    nz, half = grid.nz, grid.nz // 2
    got = grid.flip_core(sent)
    keep, got = (v.reshape((2, nz, 2) + v.shape[2:]) for v in (keep, got))

    def block(h, at_y, low, n):
        total = 0.0
        for array in (keep, got):
            part = lax.dynamic_index_in_dim(array, h, 0, False)[low : low + n]
            total = total + lax.dynamic_index_in_dim(part, at_y, 1, False).astype(WIDE)
        return total

    def low(v):
        return v.astype(LOW)

    in_x = grid.flip_x(low(block(1 - x, 1 - y, 0, half)))
    in_y = grid.flip_y(low(block(1 - x, 1 - y, half, nz - half)))
    to_x = jnp.concatenate(
        [block(1 - x, y, 0, half), block(1 - x, y, half, nz - half) + in_y.astype(WIDE)]
    )
    to_y = jnp.concatenate(
        [block(x, 1 - y, 0, half) + in_x.astype(WIDE), block(x, 1 - y, half, nz - half)]
    )
    got_x, got_y = grid.flip_x(low(to_x)), grid.flip_y(low(to_y))
    column = low(block(x, y, 0, nz) + got_x.astype(WIDE) + got_y.astype(WIDE))
    total = lax.dynamic_index_in_dim(column, z, 0, False).astype(WIDE)
    for k in range(1, nz):
        out = lax.dynamic_index_in_dim(column, lax.rem(z + k, nz), 0, False)
        total = total + grid.shift_z(out, k).astype(WIDE)
    return low(total)


def both_halves(grid, total):
    x = lax.axis_index("dp")
    other = grid.flip_x(total)
    first = jnp.where(x == 0, total, other)
    return jnp.concatenate([first, jnp.where(x == 0, other, total)], -1)


def total_of(grid, value):
    if not grid.cube:
        return lax.psum(value, "fsdp")
    value = grid.flip_core(value) + value
    value = grid.flip_x(value) + value
    value = grid.flip_y(value) + value
    bit = 1
    while bit < grid.nz:
        value = grid.swap_z(value, bit) + value
        bit *= 2
    return value


def split_columns(v):
    return jnp.stack(jnp.split(v, 2, -1))


def params(semantics=None):
    return pltpu.CompilerParams(vmem_limit_bytes=VMEM_LIMIT, dimension_semantics=semantics)


def cost(flops, moved, hard=0):
    return pl.CostEstimate(flops=int(flops), bytes_accessed=int(moved), transcendentals=int(hard))


def dot(a, b):
    return jnp.dot(a, b, preferred_element_type=WIDE)


def dot_nt(a, b):
    return lax.dot_general(a, b, (((1,), (1,)), ((), ())), preferred_element_type=WIDE)


def dot_tn(a, b):
    return lax.dot_general(a, b, (((0,), (0,)), ((), ())), preferred_element_type=WIDE)


class Source:
    def __init__(self, grid, arrays):
        self.grid, self.arrays = grid, arrays
        self.specs = [ANYWHERE] * len(arrays)

    def copy(self, refs, low, rows, target, sem):
        grid = self.grid
        x, z, y, c = grid.place()
        for ref, (dx, dy, dc, first, n) in zip(refs, piece_places(grid)):
            half = lax.rem(x + dx, 2)
            for level in range(n):
                owner_z = lax.rem(z - (first + level) + grid.nz, grid.nz)
                shard = (owner_z * 2 + lax.rem(y + dy, 2)) * 2 + lax.rem(c + dc, 2)
                source = ref.at[level, pl.ds(low, rows)]
                pltpu.make_async_copy(source, target(half, shard), sem).start()


def wait_all(ref, sem):
    pltpu.make_async_copy(ref, ref, sem).wait()


def shard_target(matrix, rows):
    n = matrix.shape[-1] // 2

    def target(half, shard):
        return matrix.at[
            pl.ds(pl.multiple_of(shard * rows, 16), rows), pl.ds(pl.multiple_of(half * n, 128), n)
        ]

    return target


def start_load(source, refs, low, rows, matrix, sem, whole=0):
    if source.grid.cube:
        source.copy(refs, low, rows, shard_target(matrix, rows), sem)
    else:
        pltpu.make_async_copy(refs[whole], matrix, sem).start()


def store_grad(grid, refs, index, low, rows, value):
    lead, columns = index
    if not grid.cube:
        refs[0][lead, :, low : low + rows, columns] = value.astype(LOW).reshape(grid.fsdp, rows, -1)
        return
    c = lax.rem(lax.axis_index("fsdp"), 2)
    value = value.astype(LOW).reshape(grid.fsdp // 2, 2, rows, value.shape[-1])
    even, odd = value[:, 0], value[:, 1]
    refs[0][lead, :, low : low + rows, columns] = jnp.where(c == 0, even, odd)
    refs[1][lead, :, low : low + rows, columns] = jnp.where(c == 0, odd, even)


def grad_shapes(grid, rows, columns):
    if not grid.cube:
        return [jax.ShapeDtypeStruct((2, grid.fsdp, rows, columns // 2), LOW)]
    return [jax.ShapeDtypeStruct((2, grid.fsdp // 2, rows, columns // 2), LOW)] * 2


def norm_rows(values):
    return lax.rsqrt(jnp.mean(values * values, -1, keepdims=True) + NORM_EPS)


def norm_back(values, scale, gain, grad):
    y = values * scale
    c = grad * gain
    back = scale * (c - y * jnp.mean(c * y, -1, keepdims=True))
    return back, jnp.sum(grad * y, 0, keepdims=True)


def project_in(grid, source, image, gains):
    length, width = image.shape
    rows = width // grid.fsdp
    count = len(source.arrays)

    def body(*refs):
        image_ref, gains_ref, pieces = refs[0], refs[1], refs[2 : 2 + count]
        normed_ref, qkv_ref, gains_out, weights, slabs, sems = refs[2 + count :]
        for j in range(3):
            start_load(source, pieces, j * rows, rows, weights.at[j], sems.at[j], j)
        if grid.cube:
            source.copy(pieces, 3 * rows, SLAB, lambda h, f: slabs.at[h, f], sems.at[3])
        values = image_ref[...].astype(WIDE)
        scaled = values * norm_rows(values)
        if grid.cube:
            wait_all(slabs, sems.at[3])
            found = jnp.sum(slabs[...].astype(WIDE), 1)
            gain = jnp.concatenate([found[0], found[1]], -1)
        else:
            gain = gains_ref[...].astype(WIDE)
        gains_out[...] = gain
        normed = (scaled * gain[0:1]).astype(LOW)
        normed_ref[...] = normed
        for j in range(3):
            wait_all(weights.at[j], sems.at[j])
            qkv_ref[j] = dot(normed, weights[j]).astype(LOW)

    vmem = pl.BlockSpec(memory_space=pltpu.VMEM)
    return pl.pallas_call(
        body,
        out_shape=[
            jax.ShapeDtypeStruct((length, width), LOW),
            jax.ShapeDtypeStruct((3, length, width), LOW),
            jax.ShapeDtypeStruct((SLAB, width), WIDE),
        ],
        in_specs=[vmem, vmem] + source.specs,
        out_specs=[vmem] * 3,
        scratch_shapes=[
            pltpu.VMEM((3, width, width), LOW),
            pltpu.VMEM((2, grid.fsdp, SLAB, width // 2), LOW),
            pltpu.SemaphoreType.DMA((4,)),
        ],
        compiler_params=params(),
        cost_estimate=cost(6 * length * width * width, 8 * width * width + 10 * length * width),
        name="project_in",
    )(image, gains, *source.arrays)


def attend(qkv, counts):
    length, width = qkv.shape[1:]
    pair = 2 * HD

    def body(counts_ref, qkv_ref, context_ref):
        seen = lax.broadcasted_iota(jnp.int32, (1, length), 1) < counts_ref[0]
        first = lax.broadcasted_iota(jnp.int32, (1, pair), 1) < HD
        q, k, v = qkv_ref[0], qkv_ref[1], qkv_ref[2]
        found = []
        for head in range(2):
            own = first if head == 0 else jnp.logical_not(first)
            scores = dot_nt(jnp.where(own, q, jnp.zeros_like(q)), k)
            scores = jnp.where(seen, scores, MASKED)
            probs = jnp.exp(scores - jnp.max(scores, -1, keepdims=True))
            summed = dot(probs.astype(LOW), jnp.where(own, v, jnp.ones_like(v)))
            found.append(summed / pltpu.roll(summed, HD, 1))
        context_ref[...] = jnp.where(first, found[0], found[1]).astype(LOW)

    return pl.pallas_call(
        body,
        grid=(width // pair,),
        out_shape=jax.ShapeDtypeStruct((length, width), LOW),
        in_specs=[
            pl.BlockSpec(memory_space=pltpu.SMEM),
            pl.BlockSpec((3, length, pair), lambda i: (0, 0, i)),
        ],
        out_specs=pl.BlockSpec((length, pair), lambda i: (0, i)),
        compiler_params=params(("arbitrary",)),
        cost_estimate=cost(
            4 * length * length * width, 8 * length * width, length * length * width // HD
        ),
        name="attend",
    )(counts, qkv)


def attend_back(qkv, d_context, counts):
    length, width = qkv.shape[1:]
    pair = 2 * HD

    def body(counts_ref, qkv_ref, d_ref, out_ref):
        seen = lax.broadcasted_iota(jnp.int32, (length, 1), 0) < counts_ref[0]
        first = lax.broadcasted_iota(jnp.int32, (1, pair), 1) < HD
        q, k, v, d = qkv_ref[0], qkv_ref[1], qkv_ref[2], d_ref[...]
        found = []
        for head in range(2):
            own = first if head == 0 else jnp.logical_not(first)
            scores = dot_nt(k, jnp.where(own, q, jnp.zeros_like(q)))
            scores = jnp.where(seen, scores, MASKED)
            probs = jnp.exp(scores - jnp.max(scores, 0, keepdims=True))
            probs = probs * (1.0 / jnp.sum(probs, 0, keepdims=True))
            d_probs = dot_nt(v, jnp.where(own, d, jnp.zeros_like(d)))
            weighed = probs * d_probs
            d_scores = (weighed - probs * jnp.sum(weighed, 0, keepdims=True)).astype(LOW)
            found.append((dot_tn(d_scores, k), dot(d_scores, q), dot(probs.astype(LOW), d)))
        for j in range(3):
            out_ref[j] = jnp.where(first, found[0][j], found[1][j]).astype(LOW)

    return pl.pallas_call(
        body,
        grid=(width // pair,),
        out_shape=jax.ShapeDtypeStruct((3, length, width), LOW),
        in_specs=[
            pl.BlockSpec(memory_space=pltpu.SMEM),
            pl.BlockSpec((3, length, pair), lambda i: (0, 0, i)),
            pl.BlockSpec((length, pair), lambda i: (0, i)),
        ],
        out_specs=pl.BlockSpec((3, length, pair), lambda i: (0, 0, i)),
        compiler_params=params(("arbitrary",)),
        cost_estimate=cost(
            10 * length * length * width, 14 * length * width, length * length * width // HD
        ),
        name="attend_back",
    )(counts, qkv, d_context)


def feed_forward(grid, second, third, image, context, cotangent, counts, gains):
    length, width = image.shape
    rows = width // grid.fsdp
    down_rows = second.down_rows
    hidden_width = down_rows * grid.fsdp
    steps = 4
    chunk = hidden_width // steps
    n_second, n_third = len(second.arrays), len(third.arrays)
    n_refs = len(grad_shapes(grid, rows, width))

    def body(*refs):
        counts_ref, image_ref, context_ref, cotangent_ref, gains_ref = refs[:5]
        seconds, refs = refs[5 : 5 + n_second], refs[5 + n_second :]
        thirds, refs = refs[:n_third], refs[n_third:]
        output_ref, d_attended_ref, d_context_ref, d_gain_ref = refs[:4]
        out_grads, refs = refs[4 : 4 + n_refs], refs[4 + n_refs :]
        in_grads, refs = refs[:n_refs], refs[n_refs:]
        w_out, w_down, w_gate, w_up, attended, normed, normed_t, e_ref, total, d_normed, sems = refs
        step = pl.program_id(0)
        seen = lax.broadcasted_iota(jnp.int32, (length, 1), 0) < counts_ref[0]

        @pl.when(step == 0)
        def _():
            start_load(second, seconds, 0, rows, w_out, sems.at[0], 0)
            start_load(third, thirds, 0, rows, w_gate, sems.at[1], 0)
            start_load(third, thirds, rows, rows, w_up, sems.at[2], 1)
            start_load(second, seconds, rows, down_rows, w_down, sems.at[3], 1)
            e = cotangent_ref[...]
            e_ref[...] = jnp.where(seen, e, jnp.zeros_like(e))
            wait_all(w_out, sems.at[0])
            values = image_ref[...].astype(WIDE) + dot(context_ref[...], w_out[...])
            attended[...] = values
            low = (values * norm_rows(values) * gains_ref[1:2]).astype(LOW)
            normed[...] = low
            normed_t[...] = low.T
            total[...] = values
            d_normed[...] = jnp.zeros_like(d_normed)
            wait_all(w_gate, sems.at[1])
            wait_all(w_up, sems.at[2])
            wait_all(w_down, sems.at[3])

        columns = pl.ds(pl.multiple_of(step * chunk, chunk), chunk)
        gate_w, up_w, down_w = w_gate[:, columns], w_up[:, columns], w_down[columns]
        e = e_ref[...]
        gate, up = dot(normed[...], gate_w), dot(normed[...], up_w)
        square = gate * gate
        bend = jnp.tanh(0.7978845608 * (gate + 0.044715 * square * gate))
        half_up = 0.5 * (1.0 + bend)
        gelu = gate * half_up
        slope = half_up + 0.5 * gate * (1.0 - bend * bend) * (
            0.7978845608 * (1.0 + 3.0 * 0.044715 * square)
        )
        hidden = (gelu * up).astype(LOW)
        total[...] += dot(hidden, down_w)
        d_hidden = dot_nt(e, down_w)
        d_gate = (d_hidden * up * slope).astype(LOW)
        d_up = (d_hidden * gelu).astype(LOW)
        g_down = dot_tn(hidden, e)
        shards = chunk // down_rows
        if grid.cube:
            c = lax.rem(lax.axis_index("fsdp"), 2)
            g_down = g_down.astype(LOW).reshape(shards // 2, 2, down_rows, width)
            even, odd = g_down[:, 0], g_down[:, 1]
            g_down = [jnp.where(c == 0, even, odd), jnp.where(c == 0, odd, even)]
            lead = pl.ds(step * (shards // 2), shards // 2)
        else:
            g_down = [g_down.astype(LOW).reshape(shards, down_rows, width)]
            lead = pl.ds(step * shards, shards)
        for ref, value in zip(out_grads, g_down):
            for h in range(2):
                ref[h, lead, rows:] = value[:, :, h * (width // 2) : (h + 1) * (width // 2)]
        everything = (0, slice(None))
        store_grad(grid, in_grads, everything, 0, rows, dot(normed_t[...], d_gate))
        store_grad(grid, in_grads, everything, rows, rows, dot(normed_t[...], d_up))
        d_normed[...] += dot_nt(d_gate, gate_w) + dot_nt(d_up, up_w)

        @pl.when(step == steps - 1)
        def _():
            output_ref[...] = jnp.where(seen, total[...], 0.0).astype(LOW)
            values = attended[...]
            back, d_gain = norm_back(values, norm_rows(values), gains_ref[1:2], d_normed[...])
            d_gain_ref[...] = jnp.broadcast_to(d_gain, d_gain_ref.shape)
            d_attended = e_ref[...].astype(WIDE) + back
            d_attended_ref[...] = d_attended
            low = d_attended.astype(LOW)
            d_context_ref[...] = dot_nt(low, w_out[...]).astype(LOW)
            g_out = dot_tn(context_ref[...], low)
            for h in range(2):
                part = g_out[:, h * (width // 2) : (h + 1) * (width // 2)]
                store_grad(grid, out_grads, (h, slice(None)), 0, rows, part)

    vmem = pl.BlockSpec(memory_space=pltpu.VMEM)
    per_half = steps // 2
    out_grads = grad_shapes(grid, rows + down_rows, width)
    in_grads = grad_shapes(grid, 2 * rows, hidden_width)
    block = (1,) + in_grads[0].shape[1:3] + (chunk,)
    in_block = pl.BlockSpec(block, lambda i: (i // per_half, 0, 0, lax.rem(i, per_half)))
    results = pl.pallas_call(
        body,
        grid=(steps,),
        out_shape=[
            jax.ShapeDtypeStruct((length, width), LOW),
            jax.ShapeDtypeStruct((length, width), WIDE),
            jax.ShapeDtypeStruct((length, width), LOW),
            jax.ShapeDtypeStruct((8, width), WIDE),
        ]
        + out_grads
        + in_grads,
        in_specs=[pl.BlockSpec(memory_space=pltpu.SMEM)] + [vmem] * 4 + second.specs + third.specs,
        out_specs=[vmem] * (4 + n_refs) + [in_block] * n_refs,
        scratch_shapes=[
            pltpu.VMEM((width, width), LOW),
            pltpu.VMEM((hidden_width, width), LOW),
            pltpu.VMEM((width, hidden_width), LOW),
            pltpu.VMEM((width, hidden_width), LOW),
            pltpu.VMEM((length, width), WIDE),
            pltpu.VMEM((length, width), LOW),
            pltpu.VMEM((width, length), LOW),
            pltpu.VMEM((length, width), LOW),
            pltpu.VMEM((length, width), WIDE),
            pltpu.VMEM((length, width), WIDE),
            pltpu.SemaphoreType.DMA((4,)),
        ],
        compiler_params=params(("arbitrary",)),
        cost_estimate=cost(
            6 * length * width * (3 * hidden_width + width),
            8 * width * (3 * hidden_width + width),
            length * hidden_width,
        ),
        name="feed_forward",
    )(counts, image, context, cotangent, gains, *second.arrays, *third.arrays)
    return results[:4], results[4 : 4 + n_refs], results[4 + n_refs :]


def project_back(grid, source, image, normed, d_qkv, d_attended, gains, d_gain_two):
    length, width = image.shape
    rows = width // grid.fsdp
    count = len(source.arrays)
    n_refs = len(grad_shapes(grid, rows, width))

    def body(*refs):
        image_ref, normed_ref, d_qkv_ref, d_attended_ref, gains_ref, d_gain_ref = refs[:6]
        pieces, refs = refs[6 : 6 + count], refs[6 + count :]
        input_grad_ref, grads, weights, sems = refs[0], refs[1 : 1 + n_refs], refs[-2], refs[-1]
        for j in range(3):
            start_load(source, pieces, j * rows, rows, weights.at[j], sems.at[j], j)
        normed_t = normed_ref[...].T
        for j in range(3):
            g = dot(normed_t, d_qkv_ref[j])
            for h in range(2):
                part = g[:, h * (width // 2) : (h + 1) * (width // 2)]
                store_grad(grid, grads, (h, slice(None)), j * rows, rows, part)
        d_normed = jnp.zeros((length, width), WIDE)
        for j in range(3):
            wait_all(weights.at[j], sems.at[j])
            d_normed = d_normed + dot_nt(d_qkv_ref[j], weights[j])
        values = image_ref[...].astype(WIDE)
        back, d_gain = norm_back(values, norm_rows(values), gains_ref[0:1], d_normed)
        input_grad_ref[...] = (d_attended_ref[...] + back).astype(LOW)
        slab = jnp.concatenate(
            [d_gain, d_gain_ref[0:1], jnp.zeros((SLAB - 2, width), WIDE)], 0
        ).astype(LOW)
        for h in range(2):
            part = slab[:, h * (width // 2) : (h + 1) * (width // 2)]
            for ref in grads:
                ref[h, :, 3 * rows :] = jnp.broadcast_to(part[None], (ref.shape[1],) + part.shape)

    vmem = pl.BlockSpec(memory_space=pltpu.VMEM)
    results = pl.pallas_call(
        body,
        out_shape=[jax.ShapeDtypeStruct((length, width), LOW)]
        + grad_shapes(grid, 3 * rows + SLAB, width),
        in_specs=[vmem] * 6 + source.specs,
        out_specs=[vmem] * (1 + n_refs),
        scratch_shapes=[
            pltpu.VMEM((3, width, width), LOW),
            pltpu.SemaphoreType.DMA((3,)),
        ],
        compiler_params=params(),
        cost_estimate=cost(12 * length * width * width, 18 * width * width + 14 * length * width),
        name="project_back",
    )(image, normed, d_qkv, d_attended, gains, d_gain_two, *source.arrays)
    return results[0], results[1:]


def adamw(param, first, second, grad, rate, decay):
    first = BETA_ONE * first + (1.0 - BETA_ONE) * grad
    second = BETA_TWO * second + (1.0 - BETA_TWO) * grad * grad
    update = first / (1.0 - BETA_ONE**STEP) / (jnp.sqrt(second / (1.0 - BETA_TWO**STEP)) + ADAM_EPS)
    return (param - rate * (update + decay * param), first, second)


def on_device(
    grid,
    patches,
    counts,
    cotangent,
    w_attn,
    w_in,
    w_down,
    gains,
    m_attn,
    m_in,
    m_down,
    m_gains,
    v_attn,
    v_in,
    v_down,
    v_gains,
):
    image, e = patches[0], cotangent[0]
    width = image.shape[1]
    rows, down_rows = w_attn.shape[1], w_down.shape[0]
    shard = lax.axis_index("fsdp")
    low_attn, low_in, low_down, low_gains = (
        w.astype(LOW) for w in (w_attn, w_in, w_down, gains)
    )
    owned = lax.broadcasted_iota(jnp.int32, (1, width), 1) // rows == shard
    slab = jnp.where(owned, jnp.tile(low_gains, (1, grid.fsdp)), jnp.zeros((), LOW))
    slab = jnp.pad(slab, ((0, SLAB - 2), (0, 0)))
    groups = gather_groups(
        grid,
        [
            jnp.concatenate([low_attn[0], low_attn[1], low_attn[2], slab], 0),
            jnp.concatenate([low_attn[3], low_down], 0),
            jnp.concatenate([low_in[0], low_in[1]], 0),
        ],
    )
    whole_gains = jnp.zeros((SLAB, width), WIDE)
    if not grid.cube:

        def whole(full, low, n):
            full = full[:, :, low : low + n].reshape(2, grid.fsdp * n, full.shape[3])
            return jnp.concatenate([full[0], full[1]], -1)

        first_full, second_full, third_full = groups
        slabs = jnp.sum(first_full[:, :, 3 * rows :].astype(WIDE), 1)
        whole_gains = jnp.concatenate([slabs[0], slabs[1]], -1)
        groups = [
            [whole(first_full, j * rows, rows) for j in range(3)],
            [whole(second_full, 0, rows), whole(second_full, rows, down_rows)],
            [whole(third_full, j * rows, rows) for j in range(2)],
        ]
    first, second, third = (Source(grid, g) for g in groups)
    second.down_rows = down_rows

    normed, qkv, full_gains = project_in(grid, first, image, whole_gains)
    context = attend(qkv, counts)
    (output, d_attended, d_context, d_gain_two), out_grads, in_grads = feed_forward(
        grid, second, third, image, context, e, counts, full_gains
    )
    d_qkv = attend_back(qkv, d_context, counts)
    input_grad, qkv_grads = project_back(
        grid, first, image, normed, d_qkv, d_attended, full_gains, d_gain_two
    )

    if grid.cube:
        third, second, first = (
            reduce_group(grid, *g) for g in (in_grads, out_grads, qkv_grads)
        )
        x = lax.axis_index("dp")
        half = width // 2
        mine = lax.dynamic_slice_in_dim(owned, x * half, half, 1)
    else:

        def reduce_whole(g):
            total = lax.psum_scatter(g.astype(WIDE), "fsdp", scatter_dimension=1)
            total = lax.psum(total.astype(LOW), "dp")
            return jnp.concatenate([total[0], total[1]], -1)

        third, second, first = (reduce_whole(g[0]) for g in (in_grads, out_grads, qkv_grads))
        mine = owned

    def squares(v):
        return jnp.sum(jnp.square(v.astype(WIDE)))

    squared = squares(first[: 3 * rows]) + squares(second) + squares(third)
    squared = squared + squares(jnp.where(mine, first[3 * rows :], jnp.zeros((), LOW)))
    grad_norm = jnp.sqrt(total_of(grid, squared))
    if grid.cube:
        first, second, third = (both_halves(grid, g) for g in (first, second, third))
    first, second, third = (g.astype(WIDE) for g in (first, second, third))
    own_gains = lax.dynamic_slice_in_dim(first[3 * rows : 3 * rows + 2], shard * rows, rows, 1)
    factor = jnp.minimum(1.0, CLIP_AT / (grad_norm + 1e-06))
    owned_grads = (
        jnp.stack([first[j * rows : (j + 1) * rows] for j in range(3)] + [second[:rows]]),
        jnp.stack([third[:rows], third[rows:]]),
        second[rows:],
        own_gains,
    )
    weights = (w_attn, w_in, w_down, gains)
    firsts = (m_attn, m_in, m_down, m_gains)
    seconds = (v_attn, v_in, v_down, v_gains)
    rates = (MATRIX_RATE, MATRIX_RATE, MATRIX_RATE, GAIN_RATE)
    decays = (MATRIX_DECAY, MATRIX_DECAY, MATRIX_DECAY, 0.0)
    updated = [
        adamw(weights[n], firsts[n], seconds[n], owned_grads[n] * factor, rates[n], decays[n])
        for n in range(4)
    ]
    return (
        output[None],
        input_grad[None],
        grad_norm,
        updated[0][0],
        updated[1][0],
        updated[2][0],
        updated[3][0],
        updated[0][1],
        updated[1][1],
        updated[2][1],
        updated[3][1],
        updated[0][2],
        updated[1][2],
        updated[2][2],
        updated[3][2],
    )


def solution(mesh):
    placed = (
        P(("dp", "fsdp"), None, None),
        P(("dp", "fsdp")),
        P(("dp", "fsdp"), None, None),
        P(None, "fsdp", None),
        P(None, "fsdp", None),
        P("fsdp", None),
        P(None, "fsdp"),
        P(None, "fsdp", None),
        P(None, "fsdp", None),
        P("fsdp", None),
        P(None, "fsdp"),
        P(None, "fsdp", None),
        P(None, "fsdp", None),
        P("fsdp", None),
        P(None, "fsdp"),
    )
    grid = Grid(mesh.shape["dp"], mesh.shape["fsdp"])
    return jax.shard_map(
        functools.partial(on_device, grid),
        mesh=mesh,
        in_specs=placed,
        out_specs=(
            P(("dp", "fsdp"), None, None),
            P(("dp", "fsdp"), None, None),
            P(),
            P(None, "fsdp", None),
            P(None, "fsdp", None),
            P("fsdp", None),
            P(None, "fsdp"),
            P(None, "fsdp", None),
            P(None, "fsdp", None),
            P("fsdp", None),
            P(None, "fsdp"),
            P(None, "fsdp", None),
            P(None, "fsdp", None),
            P("fsdp", None),
            P(None, "fsdp"),
        ),
        check_vma=False,
    )
```

```python
import functools
import math

import jax
import jax.numpy as jnp
from jax import lax
from jax.experimental import pallas as pl
from jax.experimental.pallas import tpu as pltpu
from jax.sharding import PartitionSpec as P

HD = 64
STEP = 10


NORM_EPS = 1e-06
MASKED = -1000000000.0
BETA_ONE = 0.9
BETA_TWO = 0.999
ADAM_EPS = 1e-08
CLIP_AT = 1.0
MATRIX_RATE = 0.04
MATRIX_DECAY = 0.1
GAIN_RATE = 0.8

EVERY = ("dp", "fsdp")
LOW = jnp.bfloat16
WIDE = jnp.float32
SLAB = 16
VMEM_LIMIT = 56 * 1024 * 1024
ANYWHERE = pl.BlockSpec(memory_space=pl.ANY)


class Grid:
    def __init__(self, dp, fsdp):
        self.dp, self.fsdp = dp, fsdp
        self.nz = fsdp // 4
        power = self.nz & (self.nz - 1) == 0
        self.cube = dp == 2 and fsdp % 4 == 0 and self.nz % 2 == 0 and power

    def move(self, step):
        pairs = []
        for source in range(self.dp * self.fsdp):
            x, rest = divmod(source, self.fsdp)
            z, rest = divmod(rest, 4)
            y, core = divmod(rest, 2)
            x, z, y, core = step(x, z, y, core)
            pairs.append((source, x * self.fsdp + (z * 2 + y) * 2 + core))
        return pairs

    def flip_x(self, v):
        return lax.ppermute(v, EVERY, self.move(lambda x, z, y, c: (1 - x, z, y, c)))

    def flip_y(self, v):
        return lax.ppermute(v, EVERY, self.move(lambda x, z, y, c: (x, z, 1 - y, c)))

    def flip_xy(self, v):
        return lax.ppermute(v, EVERY, self.move(lambda x, z, y, c: (1 - x, z, 1 - y, c)))

    def flip_core(self, v):
        return lax.ppermute(v, EVERY, self.move(lambda x, z, y, c: (x, z, y, 1 - c)))

    def swap_z(self, v, bit):
        return lax.ppermute(v, EVERY, self.move(lambda x, z, y, c: (x, z ^ bit, y, c)))

    def place(self):
        x, f = lax.axis_index("dp"), lax.axis_index("fsdp")
        return x, f // 4, lax.rem(f // 2, 2), lax.rem(f, 2)


def after(first, then):
    return lax.optimization_barrier((first, then))


class Spread:
    def __init__(self, grid, part):
        self.grid, self.part = grid, part
        self.half = grid.nz // 2

    def send_levels(self):
        self.levels = [self.grid.swap_z(self.part, k) for k in range(1, self.grid.nz)]

    def load_column(self):
        self.column = jnp.stack([self.part] + self.levels)

    def send_sides(self):
        self.side = self.grid.flip_x(self.column)
        self.across = self.grid.flip_y(self.column)

    def send_corners(self):
        self.low = self.grid.flip_x(self.across[: self.half])
        self.high = self.grid.flip_y(self.side[self.half :])
        self.most = jnp.concatenate([self.column, self.side, self.across])
        self.other_most = self.grid.flip_core(self.most)

    def finish(self):
        self.rest = jnp.concatenate([self.low, self.high])
        self.other_rest = self.grid.flip_core(self.rest)

    @property
    def pieces(self):
        return [self.most, self.rest, self.other_most, self.other_rest]


def piece_places(grid):
    nz = grid.nz
    most = [(x, y, level) for x, y in ((0, 0), (1, 0), (0, 1)) for level in range(nz)]
    rest = [(1, 1, level) for level in range(nz)]
    return [[(x, y, core, n) for x, y, n in spots] for core in (0, 1) for spots in (most, rest)]


class Reduce:
    def __init__(self, grid, keep, sent):
        self.grid, self.keep, self.sent = grid, keep, sent
        self.half = grid.nz // 2
        self.in_x = self.in_y = None

    def send_core(self):
        self.got = self.grid.flip_core(self.sent)

    def block(self, h, at_y, low=0, n=None):
        n = self.grid.nz if n is None else n
        total = 0.0
        for array in (self.keep, self.got):
            array = array.reshape((2, self.grid.nz, 2) + array.shape[2:])
            part = lax.dynamic_index_in_dim(array, h, 0, False)[low : low + n]
            total = total + lax.dynamic_index_in_dim(part, at_y, 1, False).astype(WIDE)
        return total

    def load_corners(self):
        x, z, y, c = self.grid.place()
        low = self.block(1 - x, 1 - y, 0, self.half)
        high = self.block(1 - x, 1 - y, self.half, self.grid.nz - self.half)
        return low.astype(LOW), high.astype(LOW)

    def send_corners(self, corners):
        self.in_x, self.in_y = self.grid.flip_x(corners[0]), self.grid.flip_y(corners[1])

    def load_sides(self):
        x, z, y, c = self.grid.place()
        half, rest = self.half, self.grid.nz - self.half
        if self.in_x is None:
            to_x, to_y = self.block(1 - x, y), self.block(x, 1 - y)
            return [v.astype(LOW) for v in (to_x, to_y, self.block(1 - x, 1 - y))]
        high = self.block(1 - x, y, half, rest) + self.in_y.astype(WIDE)
        low = self.block(x, 1 - y, 0, half) + self.in_x.astype(WIDE)
        to_x = jnp.concatenate([self.block(1 - x, y, 0, half), high])
        to_y = jnp.concatenate([low, self.block(x, 1 - y, half, rest)])
        return [to_x.astype(LOW), to_y.astype(LOW)]

    def send_sides(self, sides):
        sends = (self.grid.flip_x, self.grid.flip_y, self.grid.flip_xy)
        self.sides = [send(v) for send, v in zip(sends, sides)]

    def load_levels(self):
        x, z, y, c = self.grid.place()
        column = self.block(x, y) + sum(v.astype(WIDE) for v in self.sides)
        column = column.astype(LOW)
        self.own = lax.dynamic_index_in_dim(column, z, 0, False)
        self.leave = [
            lax.dynamic_index_in_dim(column, z ^ k, 0, False) for k in range(1, self.grid.nz)
        ]

    def send_levels(self):
        self.arrive = [self.grid.swap_z(v, k) for k, v in enumerate(self.leave, 1)]

    def load_total(self):
        self.total = sum((v.astype(WIDE) for v in self.arrive), self.own.astype(WIDE)).astype(LOW)

    def send_total(self):
        self.other = self.grid.flip_x(self.total)


def total_of(grid, value):
    if not grid.cube:
        return lax.psum(value, "fsdp")
    value = value + grid.flip_core(value)
    value = value + grid.flip_x(value)
    value = value + grid.flip_y(value)
    bit = 1
    while bit < grid.nz:
        value = value + grid.swap_z(value, bit)
        bit *= 2
    return value


def split_columns(v):
    return jnp.stack(jnp.split(v, 2, -1))


def params(semantics=None):
    return pltpu.CompilerParams(vmem_limit_bytes=VMEM_LIMIT, dimension_semantics=semantics)


def cost(microseconds):
    return pl.CostEstimate(flops=int(microseconds * 1e6), bytes_accessed=0, transcendentals=0)


def dot(a, b):
    return jnp.dot(a, b, preferred_element_type=WIDE)


def dot_nt(a, b):
    return lax.dot_general(a, b, (((1,), (1,)), ((), ())), preferred_element_type=WIDE)


def dot_tn(a, b):
    return lax.dot_general(a, b, (((0,), (0,)), ((), ())), preferred_element_type=WIDE)


class Source:
    def __init__(self, grid, arrays, whole=False):
        self.grid, self.arrays, self.whole = grid, arrays, whole
        self.specs = [ANYWHERE] * len(arrays)

    def copy(self, refs, low, rows, target, sem):
        grid = self.grid
        x, z, y, c = grid.place()
        for ref, spots in zip(refs, piece_places(grid)):
            for entry, (dx, dy, dc, level) in enumerate(spots):
                half = lax.rem(x + dx, 2)
                shard = ((z ^ level) * 2 + lax.rem(y + dy, 2)) * 2 + lax.rem(c + dc, 2)
                source = ref.at[entry, pl.ds(low, rows)]
                pltpu.make_async_copy(source, target(half, shard), sem).start()


def wait_all(ref, sem):
    pltpu.make_async_copy(ref, ref, sem).wait()


def shard_target(matrix, rows):
    n = matrix.shape[-1] // 2

    def target(half, shard):
        return matrix.at[
            pl.ds(pl.multiple_of(shard * rows, 16), rows), pl.ds(pl.multiple_of(half * n, 128), n)
        ]

    return target


def start_load(source, refs, low, rows, matrix, sem, whole=0):
    if not source.whole:
        source.copy(refs, low, rows, shard_target(matrix, rows), sem)
    else:
        pltpu.make_async_copy(refs[whole], matrix, sem).start()


def load_rows(grid, refs, which, low, target, sem):
    source = refs[0].at[:, pl.ds(low, target.shape[1])] if grid.cube else refs[which]
    pltpu.make_async_copy(source, target, sem).start()


def store_grad(grid, refs, index, low, rows, value):
    lead, columns = index
    if not grid.cube:
        refs[0][lead, :, low : low + rows, columns] = value.astype(LOW).reshape(grid.fsdp, rows, -1)
        return
    c = lax.rem(lax.axis_index("fsdp"), 2)
    value = value.astype(LOW).reshape(grid.fsdp // 2, 2, rows, value.shape[-1])
    even, odd = value[:, 0], value[:, 1]
    refs[0][lead, :, low : low + rows, columns] = jnp.where(c == 0, even, odd)
    refs[1][lead, :, low : low + rows, columns] = jnp.where(c == 0, odd, even)


def grad_shapes(grid, rows, columns):
    if not grid.cube:
        return [jax.ShapeDtypeStruct((2, grid.fsdp, rows, columns // 2), LOW)]
    return [jax.ShapeDtypeStruct((2, grid.fsdp // 2, rows, columns // 2), LOW)] * 2


def norm_rows(values):
    return lax.rsqrt(jnp.mean(values * values, -1, keepdims=True) + NORM_EPS)


def norm_back(values, scale, gain, grad):
    y = values * scale
    c = grad * gain
    back = scale * (c - y * jnp.mean(c * y, -1, keepdims=True))
    return back, jnp.sum(grad * y, 0, keepdims=True)


def project_in(grid, source, image, gains):
    length, width = image.shape
    rows = width // grid.fsdp
    count = len(source.arrays)

    def body(*refs):
        image_ref, gains_ref, pieces = refs[0], refs[1], refs[2 : 2 + count]
        normed_ref, qkv_ref, gains_out, weights, slabs, sems = refs[2 + count :]
        for j in range(3):
            start_load(source, pieces, j * rows, rows, weights.at[j], sems.at[j], j)
        if grid.cube:
            source.copy(pieces, 3 * rows, SLAB, lambda h, f: slabs.at[h, f], sems.at[3])
        values = image_ref[...].astype(WIDE)
        scaled = values * norm_rows(values)
        if grid.cube:
            wait_all(slabs, sems.at[3])
            found = jnp.sum(slabs[...].astype(WIDE), 1)
            gain = jnp.concatenate([found[0], found[1]], -1)
        else:
            gain = gains_ref[...].astype(WIDE)
        gains_out[...] = gain
        normed = (scaled * gain[0:1]).astype(LOW)
        normed_ref[...] = normed
        for j in range(3):
            wait_all(weights.at[j], sems.at[j])
            qkv_ref[j] = dot(normed, weights[j]).astype(LOW)

    vmem = pl.BlockSpec(memory_space=pltpu.VMEM)
    return pl.pallas_call(
        body,
        out_shape=[
            jax.ShapeDtypeStruct((length, width), LOW),
            jax.ShapeDtypeStruct((3, length, width), LOW),
            jax.ShapeDtypeStruct((SLAB, width), WIDE),
        ],
        in_specs=[vmem, vmem] + source.specs,
        out_specs=[vmem] * 3,
        scratch_shapes=[
            pltpu.VMEM((3, width, width), LOW),
            pltpu.VMEM((2, grid.fsdp, SLAB, width // 2), LOW),
            pltpu.SemaphoreType.DMA((4,)),
        ],
        compiler_params=params(),
        cost_estimate=cost(8),
        name="project_in",
    )(image, gains, *source.arrays)


def attend(qkv, counts):
    length, width = qkv.shape[1:]
    pair = 2 * HD

    def body(counts_ref, qkv_ref, context_ref):
        seen = lax.broadcasted_iota(jnp.int32, (1, length), 1) < counts_ref[0]
        first = lax.broadcasted_iota(jnp.int32, (1, pair), 1) < HD
        q, k, v = qkv_ref[0], qkv_ref[1], qkv_ref[2]
        found = []
        for head in range(2):
            own = first if head == 0 else jnp.logical_not(first)
            scores = dot_nt(jnp.where(own, q, jnp.zeros_like(q)), k)
            scores = jnp.where(seen, scores, MASKED)
            probs = jnp.exp(scores - jnp.max(scores, -1, keepdims=True))
            summed = dot(probs.astype(LOW), jnp.where(own, v, jnp.ones_like(v)))
            found.append(summed / pltpu.roll(summed, HD, 1))
        context_ref[...] = jnp.where(first, found[0], found[1]).astype(LOW)

    return pl.pallas_call(
        body,
        grid=(width // pair,),
        out_shape=jax.ShapeDtypeStruct((length, width), LOW),
        in_specs=[
            pl.BlockSpec(memory_space=pltpu.SMEM),
            pl.BlockSpec((3, length, pair), lambda i: (0, 0, i)),
        ],
        out_specs=pl.BlockSpec((length, pair), lambda i: (0, i)),
        compiler_params=params(("arbitrary",)),
        cost_estimate=cost(9),
        name="attend",
    )(counts, qkv)


def attend_back(qkv, d_context, counts, low, steps):
    length = qkv.shape[1]
    pair = 2 * HD
    width = steps * pair

    def body(counts_ref, qkv_ref, d_ref, out_ref):
        seen = lax.broadcasted_iota(jnp.int32, (length, 1), 0) < counts_ref[0]
        first = lax.broadcasted_iota(jnp.int32, (1, pair), 1) < HD
        q, k, v, d = qkv_ref[0], qkv_ref[1], qkv_ref[2], d_ref[...]
        found = []
        for head in range(2):
            own = first if head == 0 else jnp.logical_not(first)
            scores = dot_nt(k, jnp.where(own, q, jnp.zeros_like(q)))
            scores = jnp.where(seen, scores, MASKED)
            probs = jnp.exp(scores - jnp.max(scores, 0, keepdims=True))
            probs = probs * (1.0 / jnp.sum(probs, 0, keepdims=True))
            d_probs = dot_nt(v, jnp.where(own, d, jnp.zeros_like(d)))
            weighed = probs * d_probs
            d_scores = (weighed - probs * jnp.sum(weighed, 0, keepdims=True)).astype(LOW)
            found.append((dot_tn(d_scores, k), dot(d_scores, q), dot(probs.astype(LOW), d)))
        for j in range(3):
            out_ref[j] = jnp.where(first, found[0][j], found[1][j]).astype(LOW)

    return pl.pallas_call(
        body,
        grid=(width // pair,),
        out_shape=jax.ShapeDtypeStruct((3, length, width), LOW),
        in_specs=[
            pl.BlockSpec(memory_space=pltpu.SMEM),
            pl.BlockSpec((3, length, pair), lambda i: (0, 0, low + i)),
            pl.BlockSpec((length, pair), lambda i: (0, low + i)),
        ],
        out_specs=pl.BlockSpec((3, length, pair), lambda i: (0, 0, i)),
        compiler_params=params(("arbitrary",)),
        cost_estimate=cost(2.3 * steps + 2),
        name="attend_back",
    )(counts, qkv, d_context)


def feed_forward(grid, second, third, image, context, cotangent, counts, gains):
    length, width = image.shape
    rows = width // grid.fsdp
    down_rows = second.down_rows
    hidden_width = down_rows * grid.fsdp
    steps = 4
    chunk = hidden_width // steps
    n_second, n_third = len(second.arrays), len(third.arrays)
    n_refs = len(grad_shapes(grid, rows, width))

    def body(*refs):
        counts_ref, image_ref, context_ref, cotangent_ref, gains_ref = refs[:5]
        seconds, refs = refs[5 : 5 + n_second], refs[5 + n_second :]
        thirds, refs = refs[:n_third], refs[n_third:]
        output_ref, attended, d_normed, hidden_ref = refs[:4]
        in_grads, refs = refs[4 : 4 + n_refs], refs[4 + n_refs :]
        w_out, w_down, w_gate, w_up, normed, normed_t, e_ref, total, sems = refs
        step = pl.program_id(0)
        seen = lax.broadcasted_iota(jnp.int32, (length, 1), 0) < counts_ref[0]

        @pl.when(step == 0)
        def _():
            start_load(second, seconds, 0, rows, w_out, sems.at[0], 0)
            load_rows(grid, thirds, 0, 0, w_gate, sems.at[1])
            load_rows(grid, thirds, 1, rows, w_up, sems.at[2])
            start_load(second, seconds, rows, down_rows, w_down, sems.at[3], 1)
            e = cotangent_ref[...]
            e_ref[...] = jnp.where(seen, e, jnp.zeros_like(e))
            wait_all(w_out, sems.at[0])
            values = image_ref[...].astype(WIDE) + dot(context_ref[...], w_out[...])
            attended[...] = values
            low = (values * norm_rows(values) * gains_ref[1:2]).astype(LOW)
            normed[...] = low
            normed_t[...] = low.T
            total[...] = values
            d_normed[...] = jnp.zeros_like(d_normed)
            wait_all(w_gate, sems.at[1])
            wait_all(w_up, sems.at[2])
            wait_all(w_down, sems.at[3])

        columns = pl.ds(pl.multiple_of(step * chunk, chunk), chunk)
        gate_w, up_w = (w[:, :, columns].reshape(width, chunk) for w in (w_gate, w_up))
        down_w = w_down[columns]
        e = e_ref[...]
        gate, up = dot(normed[...], gate_w), dot(normed[...], up_w)
        square = gate * gate
        bend = jnp.tanh(0.7978845608 * (gate + 0.044715 * square * gate))
        half_up = 0.5 * (1.0 + bend)
        gelu = gate * half_up
        slope = half_up + 0.5 * gate * (1.0 - bend * bend) * (
            0.7978845608 * (1.0 + 3.0 * 0.044715 * square)
        )
        hidden = (gelu * up).astype(LOW)
        hidden_ref[...] = hidden
        total[...] += dot(hidden, down_w)
        d_hidden = dot_nt(e, down_w)
        d_gate = (d_hidden * up * slope).astype(LOW)
        d_up = (d_hidden * gelu).astype(LOW)
        everything = (0, slice(None))
        store_grad(grid, in_grads, everything, 0, rows, dot(normed_t[...], d_gate))
        store_grad(grid, in_grads, everything, rows, rows, dot(normed_t[...], d_up))
        d_normed[...] += dot_nt(d_gate, gate_w) + dot_nt(d_up, up_w)

        @pl.when(step == steps - 1)
        def _():
            output_ref[...] = jnp.where(seen, total[...], 0.0).astype(LOW)

    vmem = pl.BlockSpec(memory_space=pltpu.VMEM)
    per_half = steps // 2
    in_grads = grad_shapes(grid, 2 * rows, hidden_width)
    block = (1,) + in_grads[0].shape[1:3] + (chunk,)
    in_block = pl.BlockSpec(block, lambda i: (i // per_half, 0, 0, lax.rem(i, per_half)))
    results = pl.pallas_call(
        body,
        grid=(steps,),
        out_shape=[
            jax.ShapeDtypeStruct((length, width), LOW),
            jax.ShapeDtypeStruct((length, width), WIDE),
            jax.ShapeDtypeStruct((length, width), WIDE),
            jax.ShapeDtypeStruct((length, hidden_width), LOW),
        ]
        + in_grads,
        in_specs=[pl.BlockSpec(memory_space=pltpu.SMEM)] + [vmem] * 4 + second.specs + third.specs,
        out_specs=[vmem] * 3
        + [pl.BlockSpec((length, chunk), lambda i: (0, i))]
        + [in_block] * n_refs,
        scratch_shapes=[
            pltpu.VMEM((width, width), LOW),
            pltpu.VMEM((hidden_width, width), LOW),
            pltpu.VMEM((grid.fsdp, rows, hidden_width), LOW),
            pltpu.VMEM((grid.fsdp, rows, hidden_width), LOW),
            pltpu.VMEM((length, width), LOW),
            pltpu.VMEM((width, length), LOW),
            pltpu.VMEM((length, width), LOW),
            pltpu.VMEM((length, width), WIDE),
            pltpu.SemaphoreType.DMA((4,)),
        ],
        compiler_params=params(("arbitrary",)),
        cost_estimate=cost(25),
        name="feed_forward",
    )(counts, image, context, cotangent, gains, *second.arrays, *third.arrays)
    return results[:4], results[4:]


def feed_forward_back(grid, second, context, cotangent, counts, gains, attended, d_normed, hidden):
    length, width = context.shape
    rows, down_rows = width // grid.fsdp, second.down_rows
    n_second = len(second.arrays)

    def body(*refs):
        counts_ref, context_ref, cotangent_ref, gains_ref = refs[:4]
        attended_ref, d_normed_ref, hidden_ref = refs[4:7]
        seconds, refs = refs[7 : 7 + n_second], refs[7 + n_second :]
        d_attended_ref, d_context_ref, d_gain_ref, grads, w_out, sem = refs
        start_load(second, seconds, 0, rows, w_out, sem, 0)
        seen = lax.broadcasted_iota(jnp.int32, (length, 1), 0) < counts_ref[0]
        e = cotangent_ref[...]
        e = jnp.where(seen, e, jnp.zeros_like(e))
        values = attended_ref[...]
        back, d_gain = norm_back(values, norm_rows(values), gains_ref[1:2], d_normed_ref[...])
        d_gain_ref[...] = jnp.broadcast_to(d_gain, d_gain_ref.shape)
        d_attended = e.astype(WIDE) + back
        d_attended_ref[...] = d_attended
        low = d_attended.astype(LOW)
        wait_all(w_out, sem)
        d_context_ref[...] = dot_nt(low, w_out[...]).astype(LOW)
        g_out = dot_tn(context_ref[...], low).astype(LOW)
        grads[:, :rows] = g_out.reshape(grid.fsdp, rows, width)
        g_down = dot_tn(hidden_ref[...], e).astype(LOW)
        grads[:, rows:] = g_down.reshape(grid.fsdp, down_rows, width)

    vmem = pl.BlockSpec(memory_space=pltpu.VMEM)
    return pl.pallas_call(
        body,
        out_shape=[
            jax.ShapeDtypeStruct((length, width), WIDE),
            jax.ShapeDtypeStruct((length, width), LOW),
            jax.ShapeDtypeStruct((8, width), WIDE),
            jax.ShapeDtypeStruct((grid.fsdp, rows + down_rows, width), LOW),
        ],
        in_specs=[pl.BlockSpec(memory_space=pltpu.SMEM)] + [vmem] * 6 + second.specs,
        out_specs=[vmem] * 4,
        scratch_shapes=[pltpu.VMEM((width, width), LOW), pltpu.SemaphoreType.DMA],
        compiler_params=params(),
        cost_estimate=cost(10),
        name="feed_forward_back",
    )(counts, context, cotangent, gains, attended, d_normed, hidden, *second.arrays)


def project_back(grid, source, image, normed, d_qkv, d_attended, gains, d_gain_two):
    length, width = image.shape
    rows = width // grid.fsdp
    count, parts = len(source.arrays), len(d_qkv)
    shapes = grad_shapes(grid, 3 * rows + SLAB, width)

    def body(*refs):
        image_ref, normed_ref, d_attended_ref, gains_ref, d_gain_ref = refs[:5]
        d_refs, refs = refs[5 : 5 + parts], refs[5 + parts :]
        pieces, refs = refs[:count], refs[count:]
        input_grad_ref, grads, (weights, sems) = refs[0], refs[1 : 1 + len(shapes)], refs[-2:]
        for j in range(3):
            start_load(source, pieces, j * rows, rows, weights.at[j], sems.at[j], j)
        normed_t = normed_ref[...].T
        d_parts = [jnp.concatenate([d_ref[j] for d_ref in d_refs], -1) for j in range(3)]
        for j in range(3):
            g = dot(normed_t, d_parts[j])
            for h in range(2):
                part = g[:, h * (width // 2) : (h + 1) * (width // 2)]
                store_grad(grid, grads, (h, slice(None)), j * rows, rows, part)
        d_normed = jnp.zeros((length, width), WIDE)
        for j in range(3):
            wait_all(weights.at[j], sems.at[j])
            d_normed = d_normed + dot_nt(d_parts[j], weights[j])
        values = image_ref[...].astype(WIDE)
        back, d_gain = norm_back(values, norm_rows(values), gains_ref[0:1], d_normed)
        input_grad_ref[...] = (d_attended_ref[...] + back).astype(LOW)
        slab = jnp.concatenate(
            [d_gain, d_gain_ref[0:1], jnp.zeros((SLAB - 2, width), WIDE)], 0
        ).astype(LOW)
        for h in range(2):
            part = slab[:, h * (width // 2) : (h + 1) * (width // 2)]
            for ref in grads:
                ref[h, :, 3 * rows :] = jnp.broadcast_to(part[None], (ref.shape[1],) + part.shape)

    vmem = pl.BlockSpec(memory_space=pltpu.VMEM)
    results = pl.pallas_call(
        body,
        out_shape=[jax.ShapeDtypeStruct((length, width), LOW)] + shapes,
        in_specs=[vmem] * (5 + parts) + source.specs,
        out_specs=[vmem] * (1 + len(shapes)),
        scratch_shapes=[
            pltpu.VMEM((3, width, width), LOW),
            pltpu.SemaphoreType.DMA((3,)),
        ],
        compiler_params=params(),
        cost_estimate=cost(11),
        name="project_back",
    )(image, normed, d_attended, gains, d_gain_two, *d_qkv, *source.arrays)
    return results[0], results[1:]


def adamw(param, first, second, grad, rate, decay):
    first = BETA_ONE * first + (1.0 - BETA_ONE) * grad
    second = BETA_TWO * second + (1.0 - BETA_TWO) * grad * grad
    update = first / (1.0 - BETA_ONE**STEP) / (jnp.sqrt(second / (1.0 - BETA_TWO**STEP)) + ADAM_EPS)
    return (param - rate * (update + decay * param), first, second)


def update(grad_norm, weights, firsts, seconds, first, second, third, own_gains):
    rows = weights[0].shape[1]
    rates = (MATRIX_RATE, MATRIX_RATE, MATRIX_RATE, GAIN_RATE)
    decays = (MATRIX_DECAY, MATRIX_DECAY, MATRIX_DECAY, 0.0)

    def body(*refs):
        norm_ref, first_ref, second_ref, third_ref, gains_ref = refs[:5]
        weight_refs, first_refs, second_refs = refs[5:9], refs[9:13], refs[13:17]
        outs = refs[17:]
        factor = jnp.minimum(1.0, CLIP_AT / (norm_ref[0] + 1e-06))

        def one(n, index, grad):
            taken = [r[n][index] for r in (weight_refs, first_refs, second_refs)]
            results = adamw(*taken, grad.astype(WIDE) * factor, rates[n], decays[n])
            for k, value in enumerate(results):
                outs[4 * k + n][index] = value

        for j in range(3):
            one(0, j, first_ref[0, j * rows : (j + 1) * rows])
        one(0, 3, second_ref[:rows])
        for j in range(2):
            one(1, j, third_ref[0, j * rows : (j + 1) * rows])
        one(2, slice(None), second_ref[rows:])
        one(3, slice(None), gains_ref[...])

    def halves(shape):
        block = shape[:-1] + (shape[-1] // 2,)
        return pl.BlockSpec(block, lambda i: (0,) * (len(shape) - 1) + (i,))

    whole = pl.BlockSpec(own_gains.shape, lambda i: (0, 0))
    own = [halves(w.shape) for w in weights[:3]] + [whole]
    outer = [pl.BlockSpec((1,) + v.shape[1:], lambda i: (i, 0, 0)) for v in (first, third)]
    results = pl.pallas_call(
        body,
        grid=(2,),
        out_shape=[jax.ShapeDtypeStruct(w.shape, WIDE) for w in weights] * 3,
        in_specs=[pl.BlockSpec(memory_space=pltpu.SMEM), outer[0], halves(second.shape), outer[1]]
        + [whole]
        + own * 3,
        out_specs=own * 3,
        compiler_params=params(("arbitrary",)),
        cost_estimate=cost(4),
        name="update",
    )(grad_norm.reshape(1), first, second, third, own_gains, *weights, *firsts, *seconds)
    return results


def on_device(
    grid,
    patches,
    counts,
    cotangent,
    w_attn,
    w_in,
    w_down,
    gains,
    m_attn,
    m_in,
    m_down,
    m_gains,
    v_attn,
    v_in,
    v_down,
    v_gains,
):
    image, e = patches[0], cotangent[0]
    width = image.shape[1]
    rows, down_rows = w_attn.shape[1], w_down.shape[0]
    shard = lax.axis_index("fsdp")
    low_attn, low_in, low_down, low_gains = (
        w.astype(LOW) for w in (w_attn, w_in, w_down, gains)
    )
    owned = lax.broadcasted_iota(jnp.int32, (1, width), 1) // rows == shard
    slab = jnp.where(owned, jnp.tile(low_gains, (1, grid.fsdp)), jnp.zeros((), LOW))
    slab = jnp.pad(slab, ((0, SLAB - 2), (0, 0)))
    groups = [
        split_columns(g)
        for g in (
            jnp.concatenate([low_attn[0], low_attn[1], low_attn[2], slab], 0),
            jnp.concatenate([low_attn[3], low_down], 0),
        )
    ]
    pairs = width // (2 * HD)
    in_full = lax.all_gather(low_in.reshape(2 * rows, -1), "fsdp")
    in_full = [in_full] if grid.cube else [in_full[:, :rows], in_full[:, rows:]]
    third = Source(grid, in_full, True)

    if grid.cube:
        x = lax.axis_index("dp")
        parts = [lax.dynamic_index_in_dim(g, x, 0, False) for g in groups]
        one, two = Spread(grid, parts[0]), Spread(grid, parts[1])
        one.send_levels()
        one.levels, two.part = after(one.levels, two.part)
        one.load_column()
        one.send_sides()
        two.send_levels()
        (one.side, one.across), two.levels = after((one.side, one.across), two.levels)
        one.send_corners()
        two.load_column()
        two.send_sides()
        one.finish()
        first = Source(grid, one.pieces)
        normed, qkv, full_gains = project_in(grid, first, image, jnp.zeros((SLAB, width), WIDE))
        qkv, two.side, two.across = lax.optimization_barrier((qkv, two.side, two.across))
        two.send_corners()
        context = attend(qkv, counts)
        context, two.low, two.high = lax.optimization_barrier((context, two.low, two.high))
        two.finish()
        second = Source(grid, two.pieces)
        second.down_rows = down_rows

        (output, attended, d_normed, hidden), in_grads = feed_forward(
            grid, second, third, image, context, e, counts, full_gains
        )
        three = Reduce(grid, *in_grads)
        three.send_core()
        d_attended, d_context, d_gain_two, out_grads = feed_forward_back(
            grid, second, context, e, counts, full_gains, attended, d_normed, hidden
        )
        out_total = lax.psum_scatter(out_grads, "fsdp", scatter_dimension=0)
        three.got, d_context = after(three.got, d_context)
        corners, d_context = after(three.load_corners(), d_context)
        three.send_corners(corners)
        low = pairs // 2
        d_qkv = [attend_back(qkv, d_context, counts, 0, low)]
        d_qkv, three.in_x, three.in_y = lax.optimization_barrier((d_qkv, three.in_x, three.in_y))
        sides, d_context = after(three.load_sides(), d_context)
        three.send_sides(sides)
        d_qkv.append(attend_back(qkv, d_context, counts, low, pairs - low))
        input_grad, grads = project_back(
            grid, first, image, normed, d_qkv, d_attended, full_gains, d_gain_two
        )
        one = Reduce(grid, *grads)
        three.sides, one.sent = after(three.sides, one.sent)
        one.send_core()
        three.load_levels()
        three.leave, one.got = after(three.leave, one.got)
        three.send_levels()
        one.send_sides(one.load_sides())
        one.sides, three.arrive, out_total = lax.optimization_barrier(
            (one.sides, three.arrive, out_total)
        )
        one.load_levels()
        one.send_levels()
        three.load_total()
        three.send_total()
        out_other = grid.flip_x(out_total)
        one.load_total()
        one.send_total()
        second = (out_total.astype(WIDE) + out_other.astype(WIDE)).astype(LOW)
        first, third = (
            jnp.stack([jnp.where(x == 0, g.total, g.other), jnp.where(x == 0, g.other, g.total)])
            for g in (one, three)
        )
        mine = lax.dynamic_slice_in_dim(owned, x * (width // 2), width // 2, 1)
        counted = (one.total, three.total)
    else:
        groups = [lax.all_gather(g, "fsdp", axis=1) for g in groups]

        def whole(full, low, n):
            full = full[:, :, low : low + n].reshape(2, grid.fsdp * n, full.shape[3])
            return jnp.concatenate([full[0], full[1]], -1)

        slabs = jnp.sum(groups[0][:, :, 3 * rows :].astype(WIDE), 1)
        first = Source(grid, [whole(groups[0], j * rows, rows) for j in range(3)], True)
        second = Source(
            grid, [whole(groups[1], 0, rows), whole(groups[1], rows, down_rows)], True
        )
        second.down_rows = down_rows
        normed, qkv, full_gains = project_in(
            grid, first, image, jnp.concatenate([slabs[0], slabs[1]], -1)
        )
        context = attend(qkv, counts)
        (output, attended, d_normed, hidden), in_grads = feed_forward(
            grid, second, third, image, context, e, counts, full_gains
        )
        d_attended, d_context, d_gain_two, out_grads = feed_forward_back(
            grid, second, context, e, counts, full_gains, attended, d_normed, hidden
        )
        d_qkv = [attend_back(qkv, d_context, counts, 0, pairs)]
        input_grad, grads = project_back(
            grid, first, image, normed, d_qkv, d_attended, full_gains, d_gain_two
        )

        def reduce_whole(g, dim):
            total = lax.psum_scatter(g.astype(WIDE), "fsdp", scatter_dimension=dim)
            return lax.psum(total.astype(LOW), "dp")

        first, third = reduce_whole(grads[0], 1), reduce_whole(in_grads[0], 1)
        second = reduce_whole(out_grads, 0)
        mine = owned.reshape(2, 1, width // 2)
        counted = (first, third)

    def squares(v):
        return jnp.sum(jnp.square(v.astype(WIDE)))

    squared = squares(counted[0][..., : 3 * rows, :]) + squares(counted[1])
    squared = squared + squares(jnp.where(mine, counted[0][..., 3 * rows :, :], jnp.zeros((), LOW)))
    squared = squared + squares(second) * (0.5 if grid.cube else 1.0)
    grad_norm = jnp.sqrt(total_of(grid, squared))
    own_gains = jnp.concatenate([first[0, 3 * rows : 3 * rows + 2], first[1, 3 * rows : 3 * rows + 2]], -1)
    own_gains = lax.dynamic_slice_in_dim(own_gains, shard * rows, rows, 1)
    updated = update(
        grad_norm,
        (w_attn, w_in, w_down, gains),
        (m_attn, m_in, m_down, m_gains),
        (v_attn, v_in, v_down, v_gains),
        first,
        second,
        third,
        own_gains,
    )
    return (output[None], input_grad[None], grad_norm, *updated)


def solution(mesh):
    placed = (
        P(("dp", "fsdp"), None, None),
        P(("dp", "fsdp")),
        P(("dp", "fsdp"), None, None),
        P(None, "fsdp", None),
        P(None, "fsdp", None),
        P("fsdp", None),
        P(None, "fsdp"),
        P(None, "fsdp", None),
        P(None, "fsdp", None),
        P("fsdp", None),
        P(None, "fsdp"),
        P(None, "fsdp", None),
        P(None, "fsdp", None),
        P("fsdp", None),
        P(None, "fsdp"),
    )
    grid = Grid(mesh.shape["dp"], mesh.shape["fsdp"])
    return jax.shard_map(
        functools.partial(on_device, grid),
        mesh=mesh,
        in_specs=placed,
        out_specs=(
            P(("dp", "fsdp"), None, None),
            P(("dp", "fsdp"), None, None),
            P(),
            P(None, "fsdp", None),
            P(None, "fsdp", None),
            P("fsdp", None),
            P(None, "fsdp"),
            P(None, "fsdp", None),
            P(None, "fsdp", None),
            P("fsdp", None),
            P(None, "fsdp"),
            P(None, "fsdp", None),
            P(None, "fsdp", None),
            P("fsdp", None),
            P(None, "fsdp"),
        ),
        check_vma=False,
    )
```

```python
import functools
import math

import jax
import jax.numpy as jnp
from jax import lax
from jax.experimental import pallas as pl
from jax.experimental.pallas import tpu as pltpu
from jax.sharding import PartitionSpec as P

HD = 64
STEP = 10


NORM_EPS = 1e-06
MASKED = -1000000000.0
BETA_ONE = 0.9
BETA_TWO = 0.999
ADAM_EPS = 1e-08
CLIP_AT = 1.0
MATRIX_RATE = 0.04
MATRIX_DECAY = 0.1
GAIN_RATE = 0.8

EVERY = ("dp", "fsdp")
LOW = jnp.bfloat16
WIDE = jnp.float32
SLAB = 16
MIB = 1024 * 1024
ANYWHERE = pl.BlockSpec(memory_space=pl.ANY)


class Grid:
    def __init__(self, dp, fsdp):
        self.dp, self.fsdp = dp, fsdp
        self.nz = fsdp // 4
        power = self.nz & (self.nz - 1) == 0
        self.cube = dp == 2 and fsdp % 4 == 0 and self.nz % 2 == 0 and power

    def move(self, step):
        pairs = []
        for source in range(self.dp * self.fsdp):
            x, rest = divmod(source, self.fsdp)
            z, rest = divmod(rest, 4)
            y, core = divmod(rest, 2)
            x, z, y, core = step(x, z, y, core)
            pairs.append((source, x * self.fsdp + (z * 2 + y) * 2 + core))
        return pairs

    def flip_x(self, v):
        return lax.ppermute(v, EVERY, self.move(lambda x, z, y, c: (1 - x, z, y, c)))

    def flip_y(self, v):
        return lax.ppermute(v, EVERY, self.move(lambda x, z, y, c: (x, z, 1 - y, c)))

    def flip_xy(self, v):
        return lax.ppermute(v, EVERY, self.move(lambda x, z, y, c: (1 - x, z, 1 - y, c)))

    def flip_core(self, v):
        return lax.ppermute(v, EVERY, self.move(lambda x, z, y, c: (x, z, y, 1 - c)))

    def swap_z(self, v, bit):
        return lax.ppermute(v, EVERY, self.move(lambda x, z, y, c: (x, z ^ bit, y, c)))

    def place(self):
        x, f = lax.axis_index("dp"), lax.axis_index("fsdp")
        return x, f // 4, lax.rem(f // 2, 2), lax.rem(f, 2)


def after(first, then):
    return lax.optimization_barrier((first, then))


class Spread:
    def __init__(self, grid, part):
        self.grid, self.part = grid, part
        self.half = grid.nz // 2

    def send_levels(self):
        self.levels = [self.grid.swap_z(self.part, k) for k in range(1, self.grid.nz)]

    def load_column(self):
        self.column = jnp.stack([self.part] + self.levels)

    def send_sides(self):
        self.side = self.grid.flip_x(self.column)
        self.across = self.grid.flip_y(self.column)

    def send_corners(self):
        self.low = self.grid.flip_x(self.across[: self.half])
        self.high = self.grid.flip_y(self.side[self.half :])
        self.most = jnp.concatenate([self.column, self.side, self.across])
        self.other_most = self.grid.flip_core(self.most)

    def finish(self):
        self.rest = jnp.concatenate([self.low, self.high])
        self.other_rest = self.grid.flip_core(self.rest)

    @property
    def pieces(self):
        return [self.most, self.rest, self.other_most, self.other_rest]


def piece_places(grid):
    nz = grid.nz
    most = [(x, y, level) for x, y in ((0, 0), (1, 0), (0, 1)) for level in range(nz)]
    rest = [(1, 1, level) for level in range(nz)]
    return [[(x, y, core, n) for x, y, n in spots] for core in (0, 1) for spots in (most, rest)]


class Reduce:
    def __init__(self, grid, keep, sent):
        self.grid, self.keep, self.sent = grid, keep, sent

    def send_core(self):
        self.got = self.grid.flip_core(self.sent)

    def block(self, h, at_y):
        total = 0.0
        for array in (self.keep, self.got):
            array = array.reshape((2, self.grid.nz, 2) + array.shape[2:])
            part = lax.dynamic_index_in_dim(array, h, 0, False)
            total = total + lax.dynamic_index_in_dim(part, at_y, 1, False).astype(WIDE)
        return total

    def load_sides(self):
        x, z, y, c = self.grid.place()
        places = ((1 - x, y), (x, 1 - y), (1 - x, 1 - y))
        return [self.block(h, at_y).astype(LOW) for h, at_y in places]

    def send_sides(self, sides):
        sends = (self.grid.flip_x, self.grid.flip_y, self.grid.flip_xy)
        self.sides = [send(v) for send, v in zip(sends, sides)]

    def load_levels(self):
        x, z, y, c = self.grid.place()
        column = self.block(x, y) + sum(v.astype(WIDE) for v in self.sides)
        column = column.astype(LOW)
        self.own = lax.dynamic_index_in_dim(column, z, 0, False)
        self.leave = [
            lax.dynamic_index_in_dim(column, z ^ k, 0, False) for k in range(1, self.grid.nz)
        ]

    def send_levels(self):
        self.arrive = [self.grid.swap_z(v, k) for k, v in enumerate(self.leave, 1)]

    def load_total(self):
        self.total = sum((v.astype(WIDE) for v in self.arrive), self.own.astype(WIDE)).astype(LOW)

    def send_total(self):
        self.other = self.grid.flip_x(self.total)


class Fold:
    def __init__(self, grid, parts):
        self.grid, self.parts = grid, parts

    def by_bits(self, dim):
        count = self.parts[0].shape[dim].bit_length() - 1
        self.parts = [v.reshape(v.shape[:dim] + (2,) * count + v.shape[dim + 1 :]) for v in self.parts]
        return count

    def leave(self, dim, mine):
        leave = sum(lax.dynamic_index_in_dim(v, 1 - mine, dim, False).astype(WIDE) for v in self.parts)
        self.parts = [lax.dynamic_index_in_dim(v, mine, dim, False) for v in self.parts]
        return leave.astype(LOW)

    def total(self):
        return sum(v.astype(WIDE) for v in self.parts).astype(LOW)


def total_of(grid, value):
    if not grid.cube:
        return lax.psum(value, "fsdp")
    value = value + grid.flip_core(value)
    value = value + grid.flip_x(value)
    value = value + grid.flip_y(value)
    bit = 1
    while bit < grid.nz:
        value = value + grid.swap_z(value, bit)
        bit *= 2
    return value


def split_columns(v):
    return jnp.stack(jnp.split(v, 2, -1))


def params(mib, semantics=None):
    return pltpu.CompilerParams(vmem_limit_bytes=mib * MIB, dimension_semantics=semantics)


def cost(microseconds):
    return pl.CostEstimate(flops=int(microseconds * 1e6), bytes_accessed=0, transcendentals=0)


def dot(a, b):
    return jnp.dot(a, b, preferred_element_type=WIDE)


def dot_nt(a, b):
    return lax.dot_general(a, b, (((1,), (1,)), ((), ())), preferred_element_type=WIDE)


def dot_tn(a, b):
    return lax.dot_general(a, b, (((0,), (0,)), ((), ())), preferred_element_type=WIDE)


class Source:
    def __init__(self, grid, arrays, whole=False):
        self.grid, self.arrays, self.whole = grid, arrays, whole
        self.specs = [ANYWHERE] * len(arrays)

    def copy(self, refs, low, rows, target, sem):
        grid = self.grid
        x, z, y, c = grid.place()
        for ref, spots in zip(refs, piece_places(grid)):
            for entry, (dx, dy, dc, level) in enumerate(spots):
                half = lax.rem(x + dx, 2)
                shard = ((z ^ level) * 2 + lax.rem(y + dy, 2)) * 2 + lax.rem(c + dc, 2)
                source = ref.at[entry, pl.ds(low, rows)]
                pltpu.make_async_copy(source, target(half, shard), sem).start()


def wait_all(ref, sem):
    pltpu.make_async_copy(ref, ref, sem).wait()


def shard_target(matrix, rows):
    n = matrix.shape[-1] // 2

    def target(half, shard):
        return matrix.at[
            pl.ds(pl.multiple_of(shard * rows, 16), rows), pl.ds(pl.multiple_of(half * n, 128), n)
        ]

    return target


def start_load(source, refs, low, rows, matrix, sem, whole=0):
    if not source.whole:
        source.copy(refs, low, rows, shard_target(matrix, rows), sem)
    else:
        pltpu.make_async_copy(refs[whole], matrix, sem).start()


def load_rows(grid, refs, which, low, target, sem):
    source = refs[0].at[:, pl.ds(low, target.shape[1])] if grid.cube else refs[which]
    pltpu.make_async_copy(source, target, sem).start()


def store_grad(grid, refs, index, low, rows, value):
    lead, columns = index
    if not grid.cube:
        refs[0][lead, :, low : low + rows, columns] = value.astype(LOW).reshape(grid.fsdp, rows, -1)
        return
    c = lax.rem(lax.axis_index("fsdp"), 2)
    value = value.astype(LOW).reshape(grid.fsdp // 2, 2, rows, value.shape[-1])
    even, odd = value[:, 0], value[:, 1]
    refs[0][lead, :, low : low + rows, columns] = jnp.where(c == 0, even, odd)
    refs[1][lead, :, low : low + rows, columns] = jnp.where(c == 0, odd, even)


def grad_shapes(grid, rows, columns):
    if not grid.cube:
        return [jax.ShapeDtypeStruct((2, grid.fsdp, rows, columns // 2), LOW)]
    return [jax.ShapeDtypeStruct((2, grid.fsdp // 2, rows, columns // 2), LOW)] * 2


def norm_rows(values):
    return lax.rsqrt(jnp.mean(values * values, -1, keepdims=True) + NORM_EPS)


def norm_back(values, scale, gain, grad):
    y = values * scale
    c = grad * gain
    back = scale * (c - y * jnp.mean(c * y, -1, keepdims=True))
    return back, jnp.sum(grad * y, 0, keepdims=True)


def project_in(grid, source, image, gains):
    length, width = image.shape
    rows = width // grid.fsdp
    count = len(source.arrays)

    def body(*refs):
        image_ref, gains_ref, pieces = refs[0], refs[1], refs[2 : 2 + count]
        normed_ref, qkv_ref, gains_out, weights, slabs, sems = refs[2 + count :]
        for j in range(3):
            start_load(source, pieces, j * rows, rows, weights.at[j], sems.at[j], j)
        if grid.cube:
            source.copy(pieces, 3 * rows, SLAB, lambda h, f: slabs.at[h, f], sems.at[3])
        values = image_ref[...].astype(WIDE)
        scaled = values * norm_rows(values)
        if grid.cube:
            wait_all(slabs, sems.at[3])
            found = jnp.sum(slabs[...].astype(WIDE), 1)
            gain = jnp.concatenate([found[0], found[1]], -1)
        else:
            gain = gains_ref[...].astype(WIDE)
        gains_out[...] = gain
        normed = (scaled * gain[0:1]).astype(LOW)
        normed_ref[...] = normed
        for j in range(3):
            wait_all(weights.at[j], sems.at[j])
            qkv_ref[j] = dot(normed, weights[j]).astype(LOW)

    vmem = pl.BlockSpec(memory_space=pltpu.VMEM)
    return pl.pallas_call(
        body,
        out_shape=[
            jax.ShapeDtypeStruct((length, width), LOW),
            jax.ShapeDtypeStruct((3, length, width), LOW),
            jax.ShapeDtypeStruct((SLAB, width), WIDE),
        ],
        in_specs=[vmem, vmem] + source.specs,
        out_specs=[vmem] * 3,
        scratch_shapes=[
            pltpu.VMEM((3, width, width), LOW),
            pltpu.VMEM((2, grid.fsdp, SLAB, width // 2), LOW),
            pltpu.SemaphoreType.DMA((4,)),
        ],
        compiler_params=params(12),
        cost_estimate=cost(8),
        name="project_in",
    )(image, gains, *source.arrays)


def attend(qkv, counts):
    length, width = qkv.shape[1:]
    pair = 2 * HD

    def body(counts_ref, qkv_ref, context_ref):
        seen = lax.broadcasted_iota(jnp.int32, (1, length), 1) < counts_ref[0]
        first = lax.broadcasted_iota(jnp.int32, (1, pair), 1) < HD
        q, k, v = qkv_ref[0], qkv_ref[1], qkv_ref[2]
        found = []
        for head in range(2):
            own = first if head == 0 else jnp.logical_not(first)
            scores = dot_nt(jnp.where(own, q, jnp.zeros_like(q)), k)
            scores = jnp.where(seen, scores, MASKED)
            probs = jnp.exp(scores - jnp.max(scores, -1, keepdims=True))
            summed = dot(probs.astype(LOW), jnp.where(own, v, jnp.ones_like(v)))
            found.append(summed / pltpu.roll(summed, HD, 1))
        context_ref[...] = jnp.where(first, found[0], found[1]).astype(LOW)

    return pl.pallas_call(
        body,
        grid=(width // pair,),
        out_shape=jax.ShapeDtypeStruct((length, width), LOW),
        in_specs=[
            pl.BlockSpec(memory_space=pltpu.SMEM),
            pl.BlockSpec((3, length, pair), lambda i: (0, 0, i)),
        ],
        out_specs=pl.BlockSpec((length, pair), lambda i: (0, i)),
        compiler_params=params(8, ("arbitrary",)),
        cost_estimate=cost(9),
        name="attend",
    )(counts, qkv)


def attend_back(qkv, d_context, counts, low, steps):
    length = qkv.shape[1]
    pair = 2 * HD
    width = steps * pair

    def body(counts_ref, qkv_ref, d_ref, out_ref):
        seen = lax.broadcasted_iota(jnp.int32, (length, 1), 0) < counts_ref[0]
        first = lax.broadcasted_iota(jnp.int32, (1, pair), 1) < HD
        q, k, v, d = qkv_ref[0], qkv_ref[1], qkv_ref[2], d_ref[...]
        found = []
        for head in range(2):
            own = first if head == 0 else jnp.logical_not(first)
            scores = dot_nt(k, jnp.where(own, q, jnp.zeros_like(q)))
            scores = jnp.where(seen, scores, MASKED)
            probs = jnp.exp(scores - jnp.max(scores, 0, keepdims=True))
            probs = probs * (1.0 / jnp.sum(probs, 0, keepdims=True))
            d_probs = dot_nt(v, jnp.where(own, d, jnp.zeros_like(d)))
            weighed = probs * d_probs
            d_scores = (weighed - probs * jnp.sum(weighed, 0, keepdims=True)).astype(LOW)
            found.append((dot_tn(d_scores, k), dot(d_scores, q), dot(probs.astype(LOW), d)))
        for j in range(3):
            out_ref[j] = jnp.where(first, found[0][j], found[1][j]).astype(LOW)

    return pl.pallas_call(
        body,
        grid=(width // pair,),
        out_shape=jax.ShapeDtypeStruct((3, length, width), LOW),
        in_specs=[
            pl.BlockSpec(memory_space=pltpu.SMEM),
            pl.BlockSpec((3, length, pair), lambda i: (0, 0, low + i)),
            pl.BlockSpec((length, pair), lambda i: (0, low + i)),
        ],
        out_specs=pl.BlockSpec((3, length, pair), lambda i: (0, 0, i)),
        compiler_params=params(8, ("arbitrary",)),
        cost_estimate=cost(2.3 * steps + 2),
        name="attend_back",
    )(counts, qkv, d_context)


def feed_forward(grid, second, third, image, context, cotangent, counts, gains):
    length, width = image.shape
    rows = width // grid.fsdp
    down_rows = second.down_rows
    hidden_width = down_rows * grid.fsdp
    steps = 4
    chunk = hidden_width // steps
    n_second, n_third = len(second.arrays), len(third.arrays)
    n_refs = len(grad_shapes(grid, rows, width))

    def body(*refs):
        counts_ref, image_ref, context_ref, cotangent_ref, gains_ref = refs[:5]
        seconds, refs = refs[5 : 5 + n_second], refs[5 + n_second :]
        thirds, refs = refs[:n_third], refs[n_third:]
        output_ref, d_attended_ref, d_context_ref, d_gain_ref = refs[:4]
        out_grads, refs = refs[4 : 4 + n_refs], refs[4 + n_refs :]
        in_grads, refs = refs[:n_refs], refs[n_refs:]
        w_out, w_down, w_gate, w_up, attended, normed, normed_t, e_ref, total, d_normed, sems = refs
        step = pl.program_id(0)
        seen = lax.broadcasted_iota(jnp.int32, (length, 1), 0) < counts_ref[0]

        @pl.when(step == 0)
        def _():
            start_load(second, seconds, 0, rows, w_out, sems.at[0], 0)
            load_rows(grid, thirds, 0, 0, w_gate, sems.at[1])
            load_rows(grid, thirds, 1, rows, w_up, sems.at[2])
            start_load(second, seconds, rows, down_rows, w_down, sems.at[3], 1)
            e = cotangent_ref[...]
            e_ref[...] = jnp.where(seen, e, jnp.zeros_like(e))
            wait_all(w_out, sems.at[0])
            values = image_ref[...].astype(WIDE) + dot(context_ref[...], w_out[...])
            attended[...] = values
            low = (values * norm_rows(values) * gains_ref[1:2]).astype(LOW)
            normed[...] = low
            normed_t[...] = low.T
            total[...] = values
            d_normed[...] = jnp.zeros_like(d_normed)
            wait_all(w_gate, sems.at[1])
            wait_all(w_up, sems.at[2])
            wait_all(w_down, sems.at[3])

        columns = pl.ds(pl.multiple_of(step * chunk, chunk), chunk)
        gate_w, up_w = (w[:, :, columns].reshape(width, chunk) for w in (w_gate, w_up))
        down_w = w_down[columns]
        e = e_ref[...]
        gate, up = dot(normed[...], gate_w), dot(normed[...], up_w)
        square = gate * gate
        bend = jnp.tanh(0.7978845608 * (gate + 0.044715 * square * gate))
        half_up = 0.5 * (1.0 + bend)
        gelu = gate * half_up
        slope = half_up + 0.5 * gate * (1.0 - bend * bend) * (
            0.7978845608 * (1.0 + 3.0 * 0.044715 * square)
        )
        hidden = (gelu * up).astype(LOW)
        total[...] += dot(hidden, down_w)
        d_hidden = dot_nt(e, down_w)
        d_gate = (d_hidden * up * slope).astype(LOW)
        d_up = (d_hidden * gelu).astype(LOW)
        g_down = dot_tn(hidden, e)
        shards = chunk // down_rows
        if grid.cube:
            c = lax.rem(lax.axis_index("fsdp"), 2)
            g_down = g_down.astype(LOW).reshape(shards // 2, 2, down_rows, width)
            even, odd = g_down[:, 0], g_down[:, 1]
            g_down = [jnp.where(c == 0, even, odd), jnp.where(c == 0, odd, even)]
            lead = pl.ds(step * (shards // 2), shards // 2)
        else:
            g_down = [g_down.astype(LOW).reshape(shards, down_rows, width)]
            lead = pl.ds(step * shards, shards)
        for ref, value in zip(out_grads, g_down):
            for h in range(2):
                ref[h, lead, rows:] = value[:, :, h * (width // 2) : (h + 1) * (width // 2)]
        everything = (0, slice(None))
        store_grad(grid, in_grads, everything, 0, rows, dot(normed_t[...], d_gate))
        store_grad(grid, in_grads, everything, rows, rows, dot(normed_t[...], d_up))
        d_normed[...] += dot_nt(d_gate, gate_w) + dot_nt(d_up, up_w)

        @pl.when(step == steps - 1)
        def _():
            output_ref[...] = jnp.where(seen, total[...], 0.0).astype(LOW)
            values = attended[...]
            back, d_gain = norm_back(values, norm_rows(values), gains_ref[1:2], d_normed[...])
            d_gain_ref[...] = jnp.broadcast_to(d_gain, d_gain_ref.shape)
            d_attended = e_ref[...].astype(WIDE) + back
            d_attended_ref[...] = d_attended
            low = d_attended.astype(LOW)
            d_context_ref[...] = dot_nt(low, w_out[...]).astype(LOW)
            g_out = dot_tn(context_ref[...], low)
            for h in range(2):
                part = g_out[:, h * (width // 2) : (h + 1) * (width // 2)]
                store_grad(grid, out_grads, (h, slice(None)), 0, rows, part)

    vmem = pl.BlockSpec(memory_space=pltpu.VMEM)
    per_half = steps // 2
    out_grads = grad_shapes(grid, rows + down_rows, width)
    in_grads = grad_shapes(grid, 2 * rows, hidden_width)
    block = (1,) + in_grads[0].shape[1:3] + (chunk,)
    in_block = pl.BlockSpec(block, lambda i: (i // per_half, 0, 0, lax.rem(i, per_half)))
    results = pl.pallas_call(
        body,
        grid=(steps,),
        out_shape=[
            jax.ShapeDtypeStruct((length, width), LOW),
            jax.ShapeDtypeStruct((length, width), WIDE),
            jax.ShapeDtypeStruct((length, width), LOW),
            jax.ShapeDtypeStruct((8, width), WIDE),
        ]
        + out_grads
        + in_grads,
        in_specs=[pl.BlockSpec(memory_space=pltpu.SMEM)] + [vmem] * 4 + second.specs + third.specs,
        out_specs=[vmem] * (4 + n_refs) + [in_block] * n_refs,
        scratch_shapes=[
            pltpu.VMEM((width, width), LOW),
            pltpu.VMEM((hidden_width, width), LOW),
            pltpu.VMEM((grid.fsdp, rows, hidden_width), LOW),
            pltpu.VMEM((grid.fsdp, rows, hidden_width), LOW),
            pltpu.VMEM((length, width), WIDE),
            pltpu.VMEM((length, width), LOW),
            pltpu.VMEM((width, length), LOW),
            pltpu.VMEM((length, width), LOW),
            pltpu.VMEM((length, width), WIDE),
            pltpu.VMEM((length, width), WIDE),
            pltpu.SemaphoreType.DMA((4,)),
        ],
        compiler_params=params(56, ("arbitrary",)),
        cost_estimate=cost(28),
        name="feed_forward",
    )(counts, image, context, cotangent, gains, *second.arrays, *third.arrays)
    return results[:4], results[4 : 4 + n_refs], results[4 + n_refs :]


def project_back(grid, source, image, normed, d_qkv, d_attended, gains, d_gain_two):
    length, width = image.shape
    rows = width // grid.fsdp
    count, parts = len(source.arrays), len(d_qkv)
    shapes = grad_shapes(grid, 3 * rows + SLAB, width)

    def body(*refs):
        image_ref, normed_ref, d_attended_ref, gains_ref, d_gain_ref = refs[:5]
        d_refs, refs = refs[5 : 5 + parts], refs[5 + parts :]
        pieces, refs = refs[:count], refs[count:]
        input_grad_ref, grads, (weights, sems) = refs[0], refs[1 : 1 + len(shapes)], refs[-2:]
        for j in range(3):
            start_load(source, pieces, j * rows, rows, weights.at[j], sems.at[j], j)
        normed_t = normed_ref[...].T
        d_parts = [jnp.concatenate([d_ref[j] for d_ref in d_refs], -1) for j in range(3)]
        for j in range(3):
            g = dot(normed_t, d_parts[j])
            for h in range(2):
                part = g[:, h * (width // 2) : (h + 1) * (width // 2)]
                store_grad(grid, grads, (h, slice(None)), j * rows, rows, part)
        d_normed = jnp.zeros((length, width), WIDE)
        for j in range(3):
            wait_all(weights.at[j], sems.at[j])
            d_normed = d_normed + dot_nt(d_parts[j], weights[j])
        values = image_ref[...].astype(WIDE)
        back, d_gain = norm_back(values, norm_rows(values), gains_ref[0:1], d_normed)
        input_grad_ref[...] = (d_attended_ref[...] + back).astype(LOW)
        slab = jnp.concatenate(
            [d_gain, d_gain_ref[0:1], jnp.zeros((SLAB - 2, width), WIDE)], 0
        ).astype(LOW)
        for h in range(2):
            part = slab[:, h * (width // 2) : (h + 1) * (width // 2)]
            for ref in grads:
                ref[h, :, 3 * rows :] = jnp.broadcast_to(part[None], (ref.shape[1],) + part.shape)

    vmem = pl.BlockSpec(memory_space=pltpu.VMEM)
    results = pl.pallas_call(
        body,
        out_shape=[jax.ShapeDtypeStruct((length, width), LOW)] + shapes,
        in_specs=[vmem] * (5 + parts) + source.specs,
        out_specs=[vmem] * (1 + len(shapes)),
        scratch_shapes=[
            pltpu.VMEM((3, width, width), LOW),
            pltpu.SemaphoreType.DMA((3,)),
        ],
        compiler_params=params(12),
        cost_estimate=cost(11),
        name="project_back",
    )(image, normed, d_attended, gains, d_gain_two, *d_qkv, *source.arrays)
    return results[0], results[1:]


def fold_column(reduce):
    grid = reduce.grid
    rows, columns = reduce.keep.shape[2:]
    half = grid.nz // 2

    def level(i):
        return jnp.where(i < half, 2 * i + 1, 2 * (i - half))

    def body(place_ref, keep_ref, got_ref, *refs):
        sides, (leave_ref, rest_ref) = refs[:-2], refs[-2:]
        total = keep_ref[0, 0].astype(WIDE) + got_ref[0, 0].astype(WIDE)
        for ref in sides:
            total = total + ref[0].astype(WIDE)
        total = total.astype(LOW)

        @pl.when(pl.program_id(0) < half)
        def _():
            leave_ref[0] = total

        @pl.when(pl.program_id(0) >= half)
        def _():
            rest_ref[0] = total

    def own(i, place):
        return place[0], (place[1] ^ level(i)) * 2 + place[2], 0, 0

    block = (1, rows, columns)
    whole = pl.BlockSpec((1,) + block, own)
    side = pl.BlockSpec(block, lambda i, place: (place[1] ^ level(i), 0, 0))
    shape = jax.ShapeDtypeStruct((half, rows, columns), LOW)
    x, z, y, _ = grid.place()
    return pl.pallas_call(
        body,
        grid_spec=pltpu.PrefetchScalarGridSpec(
            num_scalar_prefetch=1,
            grid=(grid.nz,),
            in_specs=[whole, whole] + [side] * len(reduce.sides),
            out_specs=[
                pl.BlockSpec(block, lambda i, place: (jnp.minimum(i, half - 1), 0, 0)),
                pl.BlockSpec(block, lambda i, place: (jnp.maximum(i - half, 0), 0, 0)),
            ],
        ),
        out_shape=[shape, shape],
        compiler_params=params(16, ("arbitrary",)),
        cost_estimate=cost(6e7),
        name="fold_column",
    )(jnp.stack([x, z, y]).astype(jnp.int32), reduce.keep, reduce.got, *reduce.sides)


def adamw(param, first, second, grad, rate, decay):
    first = BETA_ONE * first + (1.0 - BETA_ONE) * grad
    second = BETA_TWO * second + (1.0 - BETA_TWO) * grad * grad
    update = first / (1.0 - BETA_ONE**STEP) / (jnp.sqrt(second / (1.0 - BETA_TWO**STEP)) + ADAM_EPS)
    return (param - rate * (update + decay * param), first, second)


def finish(grid, own, arrive, squared, slab_rows):
    rows, columns = own.shape
    per_shard = 2 * columns // grid.fsdp

    def body(*refs):
        squared_ref, total_ref, sum_ref = refs[0], refs[-2], refs[-1]
        total = refs[1][...].astype(WIDE)
        for ref in refs[2:-2]:
            total = total + ref[...].astype(WIDE)
        total = total.astype(LOW)
        total_ref[...] = total
        column = lax.broadcasted_iota(jnp.int32, (rows, columns), 1) + lax.axis_index("dp") * columns
        row = lax.broadcasted_iota(jnp.int32, (rows, columns), 0)
        first = lax.axis_index("fsdp") * per_shard
        mine = jnp.logical_and(column >= first, column < first + per_shard)
        counted = jnp.where(jnp.logical_or(row < rows - slab_rows, mine), total.astype(WIDE), 0.0)
        sum_ref[0] = squared_ref[0] + jnp.sum(counted * counted)

    vmem, smem = (pl.BlockSpec(memory_space=m) for m in (pltpu.VMEM, pltpu.SMEM))
    return pl.pallas_call(
        body,
        out_shape=[jax.ShapeDtypeStruct((rows, columns), LOW), jax.ShapeDtypeStruct((1,), WIDE)],
        in_specs=[smem] + [vmem] * (1 + len(arrive)),
        out_specs=[vmem, smem],
        compiler_params=params(8),
        cost_estimate=cost(1),
        name="finish",
    )(squared.reshape(1), own, *arrive)


def update(grid, grad_norm, x, weights, firsts, seconds, grads):
    rows = weights[0].shape[1]
    per_half = grid.fsdp // 2
    columns = weights[0].shape[2] // 2
    rates = (MATRIX_RATE, MATRIX_RATE, MATRIX_RATE, GAIN_RATE)
    decays = (MATRIX_DECAY, MATRIX_DECAY, MATRIX_DECAY, 0.0)

    def body(*refs):
        norm_ref, x_ref = refs[:2]
        weight_refs, first_refs, second_refs = refs[8:12], refs[12:16], refs[16:20]
        outs = refs[20:]
        half = pl.program_id(0)
        factor = jnp.minimum(1.0, CLIP_AT / (norm_ref[0] + 1e-06))
        group_one, group_two, group_three = (
            jnp.where(x_ref[0] == half, mine[...], other[...])
            for mine, other in zip(refs[2:8:2], refs[3:8:2])
        )

        def one(n, index, grad):
            taken = [r[n][index] for r in (weight_refs, first_refs, second_refs)]
            results = adamw(*taken, grad.astype(WIDE) * factor, rates[n], decays[n])
            for k, value in enumerate(results):
                outs[4 * k + n][index] = value

        for j in range(3):
            one(0, j, group_one[j * rows : (j + 1) * rows])
        one(0, 3, group_two[:rows])
        for j in range(2):
            one(1, j, group_three[j * rows : (j + 1) * rows])
        one(2, slice(None), group_two[rows:])
        shard = lax.axis_index("fsdp")

        @pl.when(shard // per_half == half)
        def _():
            shape = (columns, rows)
            place = lax.broadcasted_iota(jnp.int32, shape, 0) - lax.rem(shard, per_half) * rows
            pick = (place == lax.broadcasted_iota(jnp.int32, shape, 1)).astype(WIDE).astype(LOW)
            one(3, slice(None), dot(group_one[3 * rows :], pick)[:2])

    def halves(shape):
        block = shape[:-1] + (shape[-1] // 2,)
        return pl.BlockSpec(block, lambda i: (0,) * (len(shape) - 1) + (i,))

    smem, vmem = (pl.BlockSpec(memory_space=m) for m in (pltpu.SMEM, pltpu.VMEM))
    own = [halves(w.shape) for w in weights[:3]]
    own.append(pl.BlockSpec(weights[3].shape, lambda i: (0, 0)))
    return pl.pallas_call(
        body,
        grid=(2,),
        out_shape=[jax.ShapeDtypeStruct(w.shape, WIDE) for w in weights] * 3,
        in_specs=[smem, smem] + [vmem] * 6 + own * 3,
        out_specs=own * 3,
        compiler_params=params(56, ("arbitrary",)),
        cost_estimate=cost(4),
        name="update",
    )(grad_norm.reshape(1), x.reshape(1), *(v for g in grads for v in g), *weights, *firsts, *seconds)


def squares(v):
    return jnp.sum(jnp.square(v.astype(WIDE)))


def on_device(
    grid,
    patches,
    counts,
    cotangent,
    w_attn,
    w_in,
    w_down,
    gains,
    m_attn,
    m_in,
    m_down,
    m_gains,
    v_attn,
    v_in,
    v_down,
    v_gains,
):
    image, e = patches[0], cotangent[0]
    width = image.shape[1]
    rows, down_rows = w_attn.shape[1], w_down.shape[0]
    shard = lax.axis_index("fsdp")
    low_attn, low_in, low_down, low_gains = (
        w.astype(LOW) for w in (w_attn, w_in, w_down, gains)
    )
    owned = lax.broadcasted_iota(jnp.int32, (1, width), 1) // rows == shard
    slab = jnp.where(owned, jnp.tile(low_gains, (1, grid.fsdp)), jnp.zeros((), LOW))
    slab = jnp.pad(slab, ((0, SLAB - 2), (0, 0)))
    groups = [
        split_columns(g)
        for g in (
            jnp.concatenate([low_attn[0], low_attn[1], low_attn[2], slab], 0),
            jnp.concatenate([low_attn[3], low_down], 0),
        )
    ]
    pairs = width // (2 * HD)
    in_full = lax.all_gather(low_in.reshape(2 * rows, -1), "fsdp")
    in_full = [in_full] if grid.cube else [in_full[:, :rows], in_full[:, rows:]]
    third = Source(grid, in_full, True)

    if grid.cube:
        x = lax.axis_index("dp")
        parts = [lax.dynamic_index_in_dim(g, x, 0, False) for g in groups]
        one, two = Spread(grid, parts[0]), Spread(grid, parts[1])
        one.send_levels()
        one.levels, two.part = after(one.levels, two.part)
        one.load_column()
        one.send_sides()
        two.send_levels()
        (one.side, one.across), two.levels = after((one.side, one.across), two.levels)
        one.send_corners()
        two.load_column()
        two.send_sides()
        one.finish()
        first = Source(grid, one.pieces)
        normed, qkv, full_gains = project_in(grid, first, image, jnp.zeros((SLAB, width), WIDE))
        context = attend(qkv, counts)
        context, two.side, two.across = lax.optimization_barrier((context, two.side, two.across))
        two.send_corners()
        two.finish()
        second = Source(grid, two.pieces)
        second.down_rows = down_rows

        (output, d_attended, d_context, d_gain_two), out_grads, in_grads = feed_forward(
            grid, second, third, image, context, e, counts, full_gains
        )
        three = Reduce(grid, *in_grads)
        three.send_core()
        two_keep, two_sent = out_grads
        two_got = grid.flip_core(two_sent)
        cut = pairs // 3
        d_qkv = [attend_back(qkv, d_context, counts, 0, cut)]
        three.got, d_qkv = after(three.got, d_qkv)
        sides = three.load_sides()
        three.send_sides(sides)
        _, (two_got, d_context) = after(sides, (two_got, d_context))
        shape = (2, grid.nz, 2) + two_keep.shape[2:]
        two = Fold(grid, [two_keep.reshape(shape), two_got.reshape(shape)])
        bits = two.by_bits(1)
        x, z, y, c = grid.place()
        leave, d_context = after(two.leave(bits, lax.rem(z, 2)), d_context)
        arrived = grid.swap_z(leave, 1)
        d_qkv.append(attend_back(qkv, d_context, counts, cut, pairs - cut))
        input_grad, grads = project_back(
            grid, first, image, normed, d_qkv, d_attended, full_gains, d_gain_two
        )
        for bit in range(1, bits):
            grads, arrived = after(grads, arrived)
            two.parts.append(arrived)
            leave, three.sides = after(two.leave(bits - bit, lax.rem(z >> bit, 2)), three.sides)
            arrived = grid.swap_z(leave, 1 << bit)
        one = Reduce(grid, *grads)
        one.send_core()
        leave, rest = fold_column(three)
        in_three = grid.swap_z(leave, 1)
        leave, one.got = after(leave, one.got)
        sides = one.load_sides()
        one.send_sides(sides)
        _, (arrived, in_three) = after(sides, (arrived, in_three))
        two.parts.append(arrived)
        arrived = grid.flip_y(two.leave(1, y))
        three = Fold(grid, [rest, in_three])
        bits = three.by_bits(0)
        for bit in range(1, bits + 1):
            in_three = grid.swap_z(three.leave(bits - bit, 0), 1 << bit)
            three.parts.append(in_three)
        one.load_levels()
        one.send_levels()
        _, arrived = after(one.leave, arrived)
        two.parts.append(arrived)
        leave = two.leave(0, x)
        arrived = grid.flip_x(leave)
        two.parts.append(arrived)
        _, in_three = after(leave, in_three)
        three.parts[-1] = in_three
        three.total = three.total()
        three.other = grid.flip_x(three.total)
        two.total = two.total()
        two.other = grid.flip_x(two.total)
        squared = squares(three.total) + squares(two.total)
        squared, one.arrive = after(squared, one.arrive)
        one.total, squared = finish(grid, one.own, one.arrive, squared, SLAB)
        one.send_total()
        grad_norm = jnp.sqrt(total_of(grid, squared[0]))
        reduced = [(g.total, g.other) for g in (one, two, three)]
    else:
        groups = [lax.all_gather(g, "fsdp", axis=1) for g in groups]

        def whole(full, low, n):
            full = full[:, :, low : low + n].reshape(2, grid.fsdp * n, full.shape[3])
            return jnp.concatenate([full[0], full[1]], -1)

        slabs = jnp.sum(groups[0][:, :, 3 * rows :].astype(WIDE), 1)
        first = Source(grid, [whole(groups[0], j * rows, rows) for j in range(3)], True)
        second = Source(
            grid, [whole(groups[1], 0, rows), whole(groups[1], rows, down_rows)], True
        )
        second.down_rows = down_rows
        normed, qkv, full_gains = project_in(
            grid, first, image, jnp.concatenate([slabs[0], slabs[1]], -1)
        )
        context = attend(qkv, counts)
        (output, d_attended, d_context, d_gain_two), out_grads, in_grads = feed_forward(
            grid, second, third, image, context, e, counts, full_gains
        )
        d_qkv = [attend_back(qkv, d_context, counts, 0, pairs)]
        input_grad, grads = project_back(
            grid, first, image, normed, d_qkv, d_attended, full_gains, d_gain_two
        )

        reduced = []
        for (g,) in (grads, out_grads, in_grads):
            total = lax.psum_scatter(g.astype(WIDE), "fsdp", scatter_dimension=1)
            reduced.append(lax.psum(total.astype(LOW), "dp"))
        x = jnp.int32(0)
        mine = owned.reshape(2, 1, width // 2)
        slabs = jnp.where(mine, reduced[0][:, 3 * rows :], jnp.zeros((), LOW))
        squared = squares(reduced[0][:, : 3 * rows]) + squares(slabs)
        squared = squared + squares(reduced[1]) + squares(reduced[2])
        grad_norm = jnp.sqrt(total_of(grid, squared))

    updated = update(
        grid,
        grad_norm,
        x,
        (w_attn, w_in, w_down, gains),
        (m_attn, m_in, m_down, m_gains),
        (v_attn, v_in, v_down, v_gains),
        reduced,
    )
    return (output[None], input_grad[None], grad_norm, *updated)


def solution(mesh):
    placed = (
        P(("dp", "fsdp"), None, None),
        P(("dp", "fsdp")),
        P(("dp", "fsdp"), None, None),
        P(None, "fsdp", None),
        P(None, "fsdp", None),
        P("fsdp", None),
        P(None, "fsdp"),
        P(None, "fsdp", None),
        P(None, "fsdp", None),
        P("fsdp", None),
        P(None, "fsdp"),
        P(None, "fsdp", None),
        P(None, "fsdp", None),
        P("fsdp", None),
        P(None, "fsdp"),
    )
    grid = Grid(mesh.shape["dp"], mesh.shape["fsdp"])
    return jax.shard_map(
        functools.partial(on_device, grid),
        mesh=mesh,
        in_specs=placed,
        out_specs=(
            P(("dp", "fsdp"), None, None),
            P(("dp", "fsdp"), None, None),
            P(),
            P(None, "fsdp", None),
            P(None, "fsdp", None),
            P("fsdp", None),
            P(None, "fsdp"),
            P(None, "fsdp", None),
            P(None, "fsdp", None),
            P("fsdp", None),
            P(None, "fsdp"),
            P(None, "fsdp", None),
            P(None, "fsdp", None),
            P("fsdp", None),
            P(None, "fsdp"),
        ),
        check_vma=False,
    )
```

```python
import functools
import math

import jax
import jax.numpy as jnp
from jax import lax
from jax.experimental import pallas as pl
from jax.experimental.pallas import tpu as pltpu
from jax.sharding import PartitionSpec as P

HD = 64
STEP = 10


NORM_EPS = 1e-06
MASKED = -1000000000.0
BETA_ONE = 0.9
BETA_TWO = 0.999
ADAM_EPS = 1e-08
CLIP_AT = 1.0
MATRIX_RATE = 0.04
MATRIX_DECAY = 0.1
GAIN_RATE = 0.8

EVERY = ("dp", "fsdp")
LOW = jnp.bfloat16
WIDE = jnp.float32
SLAB = 16
MIB = 1024 * 1024
ANYWHERE = pl.BlockSpec(memory_space=pl.ANY)


class Grid:
    def __init__(self, dp, fsdp):
        self.dp, self.fsdp = dp, fsdp
        self.nz = fsdp // 4
        power = self.nz & (self.nz - 1) == 0
        self.cube = dp == 2 and fsdp % 4 == 0 and self.nz % 2 == 0 and power

    def move(self, step):
        pairs = []
        for source in range(self.dp * self.fsdp):
            x, rest = divmod(source, self.fsdp)
            z, rest = divmod(rest, 4)
            y, core = divmod(rest, 2)
            x, z, y, core = step(x, z, y, core)
            pairs.append((source, x * self.fsdp + (z * 2 + y) * 2 + core))
        return pairs

    def flip_x(self, v):
        return lax.ppermute(v, EVERY, self.move(lambda x, z, y, c: (1 - x, z, y, c)))

    def flip_y(self, v):
        return lax.ppermute(v, EVERY, self.move(lambda x, z, y, c: (x, z, 1 - y, c)))

    def flip_xy(self, v):
        return lax.ppermute(v, EVERY, self.move(lambda x, z, y, c: (1 - x, z, 1 - y, c)))

    def flip_core(self, v):
        return lax.ppermute(v, EVERY, self.move(lambda x, z, y, c: (x, z, y, 1 - c)))

    def swap_z(self, v, bit):
        return lax.ppermute(v, EVERY, self.move(lambda x, z, y, c: (x, z ^ bit, y, c)))

    def place(self):
        x, f = lax.axis_index("dp"), lax.axis_index("fsdp")
        return x, f // 4, lax.rem(f // 2, 2), lax.rem(f, 2)


def after(first, then):
    return lax.optimization_barrier((first, then))


class Spread:
    def __init__(self, grid, part):
        self.grid, self.part = grid, part
        self.half = grid.nz // 2

    def send_levels(self):
        self.levels = [self.grid.swap_z(self.part, k) for k in range(1, self.grid.nz)]

    def load_column(self):
        self.column = jnp.stack([self.part] + self.levels)

    def send_sides(self):
        self.side = self.grid.flip_x(self.column)
        self.across = self.grid.flip_y(self.column)

    def send_corners(self):
        self.low = self.grid.flip_x(self.across[: self.half])
        self.high = self.grid.flip_y(self.side[self.half :])
        self.most = jnp.concatenate([self.column, self.side, self.across])
        self.other_most = self.grid.flip_core(self.most)

    def finish(self):
        self.rest = jnp.concatenate([self.low, self.high])
        self.other_rest = self.grid.flip_core(self.rest)

    @property
    def pieces(self):
        return [self.most, self.rest, self.other_most, self.other_rest]


def piece_places(grid):
    nz = grid.nz
    most = [(x, y, level) for x, y in ((0, 0), (1, 0), (0, 1)) for level in range(nz)]
    rest = [(1, 1, level) for level in range(nz)]
    return [[(x, y, core, n) for x, y, n in spots] for core in (0, 1) for spots in (most, rest)]


class Reduce:
    def __init__(self, grid, keep, sent):
        self.grid, self.keep, self.sent = grid, keep, sent

    def send_core(self):
        self.got = self.grid.flip_core(self.sent)

    def block(self, h, at_y):
        total = 0.0
        for array in (self.keep, self.got):
            array = array.reshape((2, self.grid.nz, 2) + array.shape[2:])
            part = lax.dynamic_index_in_dim(array, h, 0, False)
            total = total + lax.dynamic_index_in_dim(part, at_y, 1, False).astype(WIDE)
        return total

    def load_sides(self):
        x, z, y, c = self.grid.place()
        places = ((1 - x, y), (x, 1 - y), (1 - x, 1 - y))
        return [self.block(h, at_y).astype(LOW) for h, at_y in places]

    def send_sides(self, sides):
        sends = (self.grid.flip_x, self.grid.flip_y, self.grid.flip_xy)
        self.sides = [send(v) for send, v in zip(sends, sides)]

    def load_levels(self):
        x, z, y, c = self.grid.place()
        column = self.block(x, y) + sum(v.astype(WIDE) for v in self.sides)
        column = column.astype(LOW)
        self.own = lax.dynamic_index_in_dim(column, z, 0, False)
        self.leave = [
            lax.dynamic_index_in_dim(column, z ^ k, 0, False) for k in range(1, self.grid.nz)
        ]

    def send_levels(self):
        self.arrive = [self.grid.swap_z(v, k) for k, v in enumerate(self.leave, 1)]

    def load_total(self):
        self.total = sum((v.astype(WIDE) for v in self.arrive), self.own.astype(WIDE)).astype(LOW)

    def send_total(self):
        self.other = self.grid.flip_x(self.total)


class Fold:
    def __init__(self, grid, parts):
        self.grid, self.parts = grid, parts

    def by_bits(self, dim):
        count = self.parts[0].shape[dim].bit_length() - 1
        self.parts = [v.reshape(v.shape[:dim] + (2,) * count + v.shape[dim + 1 :]) for v in self.parts]
        return count

    def leave(self, dim, mine):
        leave = sum(lax.dynamic_index_in_dim(v, 1 - mine, dim, False).astype(WIDE) for v in self.parts)
        self.parts = [lax.dynamic_index_in_dim(v, mine, dim, False) for v in self.parts]
        return leave.astype(LOW)

    def total(self):
        return sum(v.astype(WIDE) for v in self.parts).astype(LOW)


def total_of(grid, value):
    if not grid.cube:
        return lax.psum(value, "fsdp")
    value = value + grid.flip_core(value)
    value = value + grid.flip_x(value)
    value = value + grid.flip_y(value)
    bit = 1
    while bit < grid.nz:
        value = value + grid.swap_z(value, bit)
        bit *= 2
    return value


def split_columns(v):
    return jnp.stack(jnp.split(v, 2, -1))


def params(mib, semantics=None):
    return pltpu.CompilerParams(vmem_limit_bytes=mib * MIB, dimension_semantics=semantics)


def cost(microseconds):
    return pl.CostEstimate(flops=int(microseconds * 1e6), bytes_accessed=0, transcendentals=0)


def dot(a, b):
    return jnp.dot(a, b, preferred_element_type=WIDE)


def dot_nt(a, b):
    return lax.dot_general(a, b, (((1,), (1,)), ((), ())), preferred_element_type=WIDE)


def dot_tn(a, b):
    return lax.dot_general(a, b, (((0,), (0,)), ((), ())), preferred_element_type=WIDE)


class Source:
    def __init__(self, grid, arrays, whole=False):
        self.grid, self.arrays, self.whole = grid, arrays, whole
        self.specs = [ANYWHERE] * len(arrays)

    def copy(self, refs, low, rows, target, sem):
        grid = self.grid
        x, z, y, c = grid.place()
        for ref, spots in zip(refs, piece_places(grid)):
            for entry, (dx, dy, dc, level) in enumerate(spots):
                half = lax.rem(x + dx, 2)
                shard = ((z ^ level) * 2 + lax.rem(y + dy, 2)) * 2 + lax.rem(c + dc, 2)
                source = ref.at[entry, pl.ds(low, rows)]
                pltpu.make_async_copy(source, target(half, shard), sem).start()


def wait_all(ref, sem):
    pltpu.make_async_copy(ref, ref, sem).wait()


def shard_target(matrix, rows):
    n = matrix.shape[-1] // 2

    def target(half, shard):
        return matrix.at[
            pl.ds(pl.multiple_of(shard * rows, 16), rows), pl.ds(pl.multiple_of(half * n, 128), n)
        ]

    return target


def start_load(source, refs, low, rows, matrix, sem, whole=0):
    if not source.whole:
        source.copy(refs, low, rows, shard_target(matrix, rows), sem)
    else:
        pltpu.make_async_copy(refs[whole], matrix, sem).start()


def load_rows(grid, refs, which, low, target, sem):
    source = refs[0].at[:, pl.ds(low, target.shape[1])] if grid.cube else refs[which]
    pltpu.make_async_copy(source, target, sem).start()


def store_grad(grid, refs, index, low, rows, value):
    lead, columns = index
    if not grid.cube:
        refs[0][lead, :, low : low + rows, columns] = value.astype(LOW).reshape(grid.fsdp, rows, -1)
        return
    c = lax.rem(lax.axis_index("fsdp"), 2)
    value = value.astype(LOW).reshape(grid.fsdp // 2, 2, rows, value.shape[-1])
    even, odd = value[:, 0], value[:, 1]
    refs[0][lead, :, low : low + rows, columns] = jnp.where(c == 0, even, odd)
    refs[1][lead, :, low : low + rows, columns] = jnp.where(c == 0, odd, even)


def grad_shapes(grid, rows, columns):
    if not grid.cube:
        return [jax.ShapeDtypeStruct((2, grid.fsdp, rows, columns // 2), LOW)]
    return [jax.ShapeDtypeStruct((2, grid.fsdp // 2, rows, columns // 2), LOW)] * 2


def norm_rows(values):
    return lax.rsqrt(jnp.mean(values * values, -1, keepdims=True) + NORM_EPS)


def norm_back(values, scale, gain, grad):
    y = values * scale
    c = grad * gain
    back = scale * (c - y * jnp.mean(c * y, -1, keepdims=True))
    return back, jnp.sum(grad * y, 0, keepdims=True)


def project_in(grid, source, image, gains):
    length, width = image.shape
    rows = width // grid.fsdp
    count = len(source.arrays)

    def body(*refs):
        image_ref, gains_ref, pieces = refs[0], refs[1], refs[2 : 2 + count]
        normed_ref, qkv_ref, gains_out, weights, slabs, sems = refs[2 + count :]
        for j in range(3):
            start_load(source, pieces, j * rows, rows, weights.at[j], sems.at[j], j)
        if grid.cube:
            source.copy(pieces, 3 * rows, SLAB, lambda h, f: slabs.at[h, f], sems.at[3])
        values = image_ref[...].astype(WIDE)
        scaled = values * norm_rows(values)
        if grid.cube:
            wait_all(slabs, sems.at[3])
            found = jnp.sum(slabs[...].astype(WIDE), 1)
            gain = jnp.concatenate([found[0], found[1]], -1)
        else:
            gain = gains_ref[...].astype(WIDE)
        gains_out[...] = gain
        normed = (scaled * gain[0:1]).astype(LOW)
        normed_ref[...] = normed
        for j in range(3):
            wait_all(weights.at[j], sems.at[j])
            qkv_ref[j] = dot(normed, weights[j]).astype(LOW)

    vmem = pl.BlockSpec(memory_space=pltpu.VMEM)
    return pl.pallas_call(
        body,
        out_shape=[
            jax.ShapeDtypeStruct((length, width), LOW),
            jax.ShapeDtypeStruct((3, length, width), LOW),
            jax.ShapeDtypeStruct((SLAB, width), WIDE),
        ],
        in_specs=[vmem, vmem] + source.specs,
        out_specs=[vmem] * 3,
        scratch_shapes=[
            pltpu.VMEM((3, width, width), LOW),
            pltpu.VMEM((2, grid.fsdp, SLAB, width // 2), LOW),
            pltpu.SemaphoreType.DMA((4,)),
        ],
        compiler_params=params(12),
        cost_estimate=cost(8),
        name="project_in",
    )(image, gains, *source.arrays)


def attend(qkv, counts):
    length, width = qkv.shape[1:]
    pair = 2 * HD

    def body(counts_ref, qkv_ref, context_ref):
        seen = lax.broadcasted_iota(jnp.int32, (1, length), 1) < counts_ref[0]
        first = lax.broadcasted_iota(jnp.int32, (1, pair), 1) < HD
        q, k, v = qkv_ref[0], qkv_ref[1], qkv_ref[2]
        found = []
        for head in range(2):
            own = first if head == 0 else jnp.logical_not(first)
            scores = dot_nt(jnp.where(own, q, jnp.zeros_like(q)), k)
            scores = jnp.where(seen, scores, MASKED)
            probs = jnp.exp(scores - jnp.max(scores, -1, keepdims=True))
            summed = dot(probs.astype(LOW), jnp.where(own, v, jnp.ones_like(v)))
            found.append(summed / pltpu.roll(summed, HD, 1))
        context_ref[...] = jnp.where(first, found[0], found[1]).astype(LOW)

    return pl.pallas_call(
        body,
        grid=(width // pair,),
        out_shape=jax.ShapeDtypeStruct((length, width), LOW),
        in_specs=[
            pl.BlockSpec(memory_space=pltpu.SMEM),
            pl.BlockSpec((3, length, pair), lambda i: (0, 0, i)),
        ],
        out_specs=pl.BlockSpec((length, pair), lambda i: (0, i)),
        compiler_params=params(8, ("arbitrary",)),
        cost_estimate=cost(9),
        name="attend",
    )(counts, qkv)


def attend_back(qkv, d_context, counts, low, steps):
    length = qkv.shape[1]
    pair = 2 * HD
    width = steps * pair

    def body(counts_ref, qkv_ref, d_ref, out_ref):
        seen = lax.broadcasted_iota(jnp.int32, (length, 1), 0) < counts_ref[0]
        first = lax.broadcasted_iota(jnp.int32, (1, pair), 1) < HD
        q, k, v, d = qkv_ref[0], qkv_ref[1], qkv_ref[2], d_ref[...]
        found = []
        for head in range(2):
            own = first if head == 0 else jnp.logical_not(first)
            scores = dot_nt(k, jnp.where(own, q, jnp.zeros_like(q)))
            scores = jnp.where(seen, scores, MASKED)
            probs = jnp.exp(scores - jnp.max(scores, 0, keepdims=True))
            probs = probs * (1.0 / jnp.sum(probs, 0, keepdims=True))
            d_probs = dot_nt(v, jnp.where(own, d, jnp.zeros_like(d)))
            weighed = probs * d_probs
            d_scores = (weighed - probs * jnp.sum(weighed, 0, keepdims=True)).astype(LOW)
            found.append((dot_tn(d_scores, k), dot(d_scores, q), dot(probs.astype(LOW), d)))
        for j in range(3):
            out_ref[j] = jnp.where(first, found[0][j], found[1][j]).astype(LOW)

    return pl.pallas_call(
        body,
        grid=(width // pair,),
        out_shape=jax.ShapeDtypeStruct((3, length, width), LOW),
        in_specs=[
            pl.BlockSpec(memory_space=pltpu.SMEM),
            pl.BlockSpec((3, length, pair), lambda i: (0, 0, low + i)),
            pl.BlockSpec((length, pair), lambda i: (0, low + i)),
        ],
        out_specs=pl.BlockSpec((3, length, pair), lambda i: (0, 0, i)),
        compiler_params=params(8, ("arbitrary",)),
        cost_estimate=cost(2.3 * steps + 2),
        name="attend_back",
    )(counts, qkv, d_context)


def feed_forward(grid, second, third, image, context, cotangent, counts, gains):
    length, width = image.shape
    rows = width // grid.fsdp
    down_rows = second.down_rows
    hidden_width = down_rows * grid.fsdp
    steps = 4
    chunk = hidden_width // steps
    n_second, n_third = len(second.arrays), len(third.arrays)
    n_refs = len(grad_shapes(grid, rows, width))

    def body(*refs):
        counts_ref, image_ref, context_ref, cotangent_ref, gains_ref = refs[:5]
        seconds, refs = refs[5 : 5 + n_second], refs[5 + n_second :]
        thirds, refs = refs[:n_third], refs[n_third:]
        output_ref, d_attended_ref, d_context_ref, d_gain_ref = refs[:4]
        out_grads, refs = refs[4 : 4 + n_refs], refs[4 + n_refs :]
        in_grads, refs = refs[:n_refs], refs[n_refs:]
        w_out, w_down, w_gate, w_up, attended, normed, normed_t, e_ref, total, d_normed, sems = refs
        step = pl.program_id(0)
        seen = lax.broadcasted_iota(jnp.int32, (length, 1), 0) < counts_ref[0]

        @pl.when(step == 0)
        def _():
            start_load(second, seconds, 0, rows, w_out, sems.at[0], 0)
            load_rows(grid, thirds, 0, 0, w_gate, sems.at[1])
            load_rows(grid, thirds, 1, rows, w_up, sems.at[2])
            start_load(second, seconds, rows, down_rows, w_down, sems.at[3], 1)
            e = cotangent_ref[...]
            e_ref[...] = jnp.where(seen, e, jnp.zeros_like(e))
            wait_all(w_out, sems.at[0])
            values = image_ref[...].astype(WIDE) + dot(context_ref[...], w_out[...])
            attended[...] = values
            low = (values * norm_rows(values) * gains_ref[1:2]).astype(LOW)
            normed[...] = low
            normed_t[...] = low.T
            total[...] = values
            d_normed[...] = jnp.zeros_like(d_normed)
            wait_all(w_gate, sems.at[1])
            wait_all(w_up, sems.at[2])
            wait_all(w_down, sems.at[3])

        columns = pl.ds(pl.multiple_of(step * chunk, chunk), chunk)
        gate_w, up_w = (w[:, :, columns].reshape(width, chunk) for w in (w_gate, w_up))
        down_w = w_down[columns]
        e = e_ref[...]
        gate, up = dot(normed[...], gate_w), dot(normed[...], up_w)
        square = gate * gate
        bend = jnp.tanh(0.7978845608 * (gate + 0.044715 * square * gate))
        half_up = 0.5 * (1.0 + bend)
        gelu = gate * half_up
        slope = half_up + 0.5 * gate * (1.0 - bend * bend) * (
            0.7978845608 * (1.0 + 3.0 * 0.044715 * square)
        )
        hidden = (gelu * up).astype(LOW)
        total[...] += dot(hidden, down_w)
        d_hidden = dot_nt(e, down_w)
        d_gate = (d_hidden * up * slope).astype(LOW)
        d_up = (d_hidden * gelu).astype(LOW)
        g_down = dot_tn(hidden, e)
        shards = chunk // down_rows
        if grid.cube:
            c = lax.rem(lax.axis_index("fsdp"), 2)
            g_down = g_down.astype(LOW).reshape(shards // 2, 2, down_rows, width)
            even, odd = g_down[:, 0], g_down[:, 1]
            g_down = [jnp.where(c == 0, even, odd), jnp.where(c == 0, odd, even)]
            lead = pl.ds(step * (shards // 2), shards // 2)
        else:
            g_down = [g_down.astype(LOW).reshape(shards, down_rows, width)]
            lead = pl.ds(step * shards, shards)
        for ref, value in zip(out_grads, g_down):
            for h in range(2):
                ref[h, lead, rows:] = value[:, :, h * (width // 2) : (h + 1) * (width // 2)]
        everything = (0, slice(None))
        store_grad(grid, in_grads, everything, 0, rows, dot(normed_t[...], d_gate))
        store_grad(grid, in_grads, everything, rows, rows, dot(normed_t[...], d_up))
        d_normed[...] += dot_nt(d_gate, gate_w) + dot_nt(d_up, up_w)

        @pl.when(step == steps - 1)
        def _():
            output_ref[...] = jnp.where(seen, total[...], 0.0).astype(LOW)
            values = attended[...]
            back, d_gain = norm_back(values, norm_rows(values), gains_ref[1:2], d_normed[...])
            d_gain_ref[...] = jnp.broadcast_to(d_gain, d_gain_ref.shape)
            d_attended = e_ref[...].astype(WIDE) + back
            d_attended_ref[...] = d_attended
            low = d_attended.astype(LOW)
            d_context_ref[...] = dot_nt(low, w_out[...]).astype(LOW)
            g_out = dot_tn(context_ref[...], low)
            for h in range(2):
                part = g_out[:, h * (width // 2) : (h + 1) * (width // 2)]
                store_grad(grid, out_grads, (h, slice(None)), 0, rows, part)

    vmem = pl.BlockSpec(memory_space=pltpu.VMEM)
    per_half = steps // 2
    out_grads = grad_shapes(grid, rows + down_rows, width)
    in_grads = grad_shapes(grid, 2 * rows, hidden_width)
    block = (1,) + in_grads[0].shape[1:3] + (chunk,)
    in_block = pl.BlockSpec(block, lambda i: (i // per_half, 0, 0, lax.rem(i, per_half)))
    results = pl.pallas_call(
        body,
        grid=(steps,),
        out_shape=[
            jax.ShapeDtypeStruct((length, width), LOW),
            jax.ShapeDtypeStruct((length, width), WIDE),
            jax.ShapeDtypeStruct((length, width), LOW),
            jax.ShapeDtypeStruct((8, width), WIDE),
        ]
        + out_grads
        + in_grads,
        in_specs=[pl.BlockSpec(memory_space=pltpu.SMEM)] + [vmem] * 4 + second.specs + third.specs,
        out_specs=[vmem] * (4 + n_refs) + [in_block] * n_refs,
        scratch_shapes=[
            pltpu.VMEM((width, width), LOW),
            pltpu.VMEM((hidden_width, width), LOW),
            pltpu.VMEM((grid.fsdp, rows, hidden_width), LOW),
            pltpu.VMEM((grid.fsdp, rows, hidden_width), LOW),
            pltpu.VMEM((length, width), WIDE),
            pltpu.VMEM((length, width), LOW),
            pltpu.VMEM((width, length), LOW),
            pltpu.VMEM((length, width), LOW),
            pltpu.VMEM((length, width), WIDE),
            pltpu.VMEM((length, width), WIDE),
            pltpu.SemaphoreType.DMA((4,)),
        ],
        compiler_params=params(56, ("arbitrary",)),
        cost_estimate=cost(28),
        name="feed_forward",
    )(counts, image, context, cotangent, gains, *second.arrays, *third.arrays)
    return results[:4], results[4 : 4 + n_refs], results[4 + n_refs :]


def project_back(grid, source, image, normed, d_qkv, d_attended, gains, d_gain_two):
    length, width = image.shape
    rows = width // grid.fsdp
    count, parts = len(source.arrays), len(d_qkv)
    shapes = grad_shapes(grid, 3 * rows + SLAB, width)

    def body(*refs):
        image_ref, normed_ref, d_attended_ref, gains_ref, d_gain_ref = refs[:5]
        d_refs, refs = refs[5 : 5 + parts], refs[5 + parts :]
        pieces, refs = refs[:count], refs[count:]
        input_grad_ref, grads, (weights, sems) = refs[0], refs[1 : 1 + len(shapes)], refs[-2:]
        for j in range(3):
            start_load(source, pieces, j * rows, rows, weights.at[j], sems.at[j], j)
        normed_t = normed_ref[...].T
        d_parts = [jnp.concatenate([d_ref[j] for d_ref in d_refs], -1) for j in range(3)]
        for j in range(3):
            g = dot(normed_t, d_parts[j])
            for h in range(2):
                part = g[:, h * (width // 2) : (h + 1) * (width // 2)]
                store_grad(grid, grads, (h, slice(None)), j * rows, rows, part)
        d_normed = jnp.zeros((length, width), WIDE)
        for j in range(3):
            wait_all(weights.at[j], sems.at[j])
            d_normed = d_normed + dot_nt(d_parts[j], weights[j])
        values = image_ref[...].astype(WIDE)
        back, d_gain = norm_back(values, norm_rows(values), gains_ref[0:1], d_normed)
        input_grad_ref[...] = (d_attended_ref[...] + back).astype(LOW)
        slab = jnp.concatenate(
            [d_gain, d_gain_ref[0:1], jnp.zeros((SLAB - 2, width), WIDE)], 0
        ).astype(LOW)
        for h in range(2):
            part = slab[:, h * (width // 2) : (h + 1) * (width // 2)]
            for ref in grads:
                ref[h, :, 3 * rows :] = jnp.broadcast_to(part[None], (ref.shape[1],) + part.shape)

    vmem = pl.BlockSpec(memory_space=pltpu.VMEM)
    results = pl.pallas_call(
        body,
        out_shape=[jax.ShapeDtypeStruct((length, width), LOW)] + shapes,
        in_specs=[vmem] * (5 + parts) + source.specs,
        out_specs=[vmem] * (1 + len(shapes)),
        scratch_shapes=[
            pltpu.VMEM((3, width, width), LOW),
            pltpu.SemaphoreType.DMA((3,)),
        ],
        compiler_params=params(12),
        cost_estimate=cost(11),
        name="project_back",
    )(image, normed, d_attended, gains, d_gain_two, *d_qkv, *source.arrays)
    return results[0], results[1:]


def fold_column(reduce):
    grid = reduce.grid
    rows, columns = reduce.keep.shape[2:]
    half = grid.nz // 2

    def level(i):
        return jnp.where(i < half, 2 * i + 1, 2 * (i - half))

    def body(place_ref, keep_ref, got_ref, *refs):
        sides, (leave_ref, rest_ref) = refs[:-2], refs[-2:]
        total = keep_ref[0, 0].astype(WIDE) + got_ref[0, 0].astype(WIDE)
        for ref in sides:
            total = total + ref[0].astype(WIDE)
        total = total.astype(LOW)

        @pl.when(pl.program_id(0) < half)
        def _():
            leave_ref[0] = total

        @pl.when(pl.program_id(0) >= half)
        def _():
            rest_ref[0] = total

    def own(i, place):
        return place[0], (place[1] ^ level(i)) * 2 + place[2], 0, 0

    block = (1, rows, columns)
    whole = pl.BlockSpec((1,) + block, own)
    side = pl.BlockSpec(block, lambda i, place: (place[1] ^ level(i), 0, 0))
    shape = jax.ShapeDtypeStruct((half, rows, columns), LOW)
    x, z, y, _ = grid.place()
    return pl.pallas_call(
        body,
        grid_spec=pltpu.PrefetchScalarGridSpec(
            num_scalar_prefetch=1,
            grid=(grid.nz,),
            in_specs=[whole, whole] + [side] * len(reduce.sides),
            out_specs=[
                pl.BlockSpec(block, lambda i, place: (jnp.minimum(i, half - 1), 0, 0)),
                pl.BlockSpec(block, lambda i, place: (jnp.maximum(i - half, 0), 0, 0)),
            ],
        ),
        out_shape=[shape, shape],
        compiler_params=params(16, ("arbitrary",)),
        cost_estimate=cost(6e7),
        name="fold_column",
    )(jnp.stack([x, z, y]).astype(jnp.int32), reduce.keep, reduce.got, *reduce.sides)


def adamw(param, first, second, grad, rate, decay):
    first = BETA_ONE * first + (1.0 - BETA_ONE) * grad
    second = BETA_TWO * second + (1.0 - BETA_TWO) * grad * grad
    update = first / (1.0 - BETA_ONE**STEP) / (jnp.sqrt(second / (1.0 - BETA_TWO**STEP)) + ADAM_EPS)
    return (param - rate * (update + decay * param), first, second)


def finish(grid, own, arrive, totals, slab_rows):
    rows, columns = own.shape
    per_shard = 2 * columns // grid.fsdp

    def body(*refs):
        others, refs, (total_ref, sum_ref) = refs[: len(totals)], refs[len(totals) : -2], refs[-2:]
        total = sum(ref[...].astype(WIDE) for ref in refs)
        total = total.astype(LOW)
        total_ref[...] = total
        column = lax.broadcasted_iota(jnp.int32, (rows, columns), 1) + lax.axis_index("dp") * columns
        row = lax.broadcasted_iota(jnp.int32, (rows, columns), 0)
        first = lax.axis_index("fsdp") * per_shard
        mine = jnp.logical_and(column >= first, column < first + per_shard)
        counted = jnp.where(jnp.logical_or(row < rows - slab_rows, mine), total.astype(WIDE), 0.0)
        squared = jnp.sum(counted * counted)
        for ref in others:
            value = ref[...].astype(WIDE)
            squared = squared + jnp.sum(value * value)
        sum_ref[0] = squared

    vmem, smem = (pl.BlockSpec(memory_space=m) for m in (pltpu.VMEM, pltpu.SMEM))
    return pl.pallas_call(
        body,
        out_shape=[jax.ShapeDtypeStruct((rows, columns), LOW), jax.ShapeDtypeStruct((1,), WIDE)],
        in_specs=[vmem] * (1 + len(arrive) + len(totals)),
        out_specs=[vmem, smem],
        compiler_params=params(8),
        cost_estimate=cost(1),
        name="finish",
    )(*totals, own, *arrive)


def update(grid, grad_norm, x, weights, firsts, seconds, grads):
    rows = weights[0].shape[1]
    per_half = grid.fsdp // 2
    columns = weights[0].shape[2] // 2
    rates = (MATRIX_RATE, MATRIX_RATE, MATRIX_RATE, GAIN_RATE)
    decays = (MATRIX_DECAY, MATRIX_DECAY, MATRIX_DECAY, 0.0)

    def body(*refs):
        norm_ref, x_ref = refs[:2]
        weight_refs, first_refs, second_refs = refs[8:12], refs[12:16], refs[16:20]
        outs = refs[20:]
        half = pl.program_id(0)
        factor = jnp.minimum(1.0, CLIP_AT / (norm_ref[0] + 1e-06))
        group_one, group_two, group_three = (
            jnp.where(x_ref[0] == half, mine[...], other[...])
            for mine, other in zip(refs[2:8:2], refs[3:8:2])
        )

        def one(n, index, grad):
            taken = [r[n][index] for r in (weight_refs, first_refs, second_refs)]
            results = adamw(*taken, grad.astype(WIDE) * factor, rates[n], decays[n])
            for k, value in enumerate(results):
                outs[4 * k + n][index] = value

        for j in range(3):
            one(0, j, group_one[j * rows : (j + 1) * rows])
        one(0, 3, group_two[:rows])
        for j in range(2):
            one(1, j, group_three[j * rows : (j + 1) * rows])
        one(2, slice(None), group_two[rows:])
        shard = lax.axis_index("fsdp")

        @pl.when(shard // per_half == half)
        def _():
            shape = (columns, rows)
            place = lax.broadcasted_iota(jnp.int32, shape, 0) - lax.rem(shard, per_half) * rows
            pick = (place == lax.broadcasted_iota(jnp.int32, shape, 1)).astype(WIDE).astype(LOW)
            one(3, slice(None), dot(group_one[3 * rows :], pick)[:2])

    def halves(shape):
        block = shape[:-1] + (shape[-1] // 2,)
        return pl.BlockSpec(block, lambda i: (0,) * (len(shape) - 1) + (i,))

    smem, vmem = (pl.BlockSpec(memory_space=m) for m in (pltpu.SMEM, pltpu.VMEM))
    own = [halves(w.shape) for w in weights[:3]]
    own.append(pl.BlockSpec(weights[3].shape, lambda i: (0, 0)))
    return pl.pallas_call(
        body,
        grid=(2,),
        out_shape=[jax.ShapeDtypeStruct(w.shape, WIDE) for w in weights] * 3,
        in_specs=[smem, smem] + [vmem] * 6 + own * 3,
        out_specs=own * 3,
        compiler_params=params(56, ("arbitrary",)),
        cost_estimate=cost(4),
        name="update",
    )(grad_norm.reshape(1), x.reshape(1), *(v for g in grads for v in g), *weights, *firsts, *seconds)


def squares(v):
    return jnp.sum(jnp.square(v.astype(WIDE)))


def on_device(
    grid,
    patches,
    counts,
    cotangent,
    w_attn,
    w_in,
    w_down,
    gains,
    m_attn,
    m_in,
    m_down,
    m_gains,
    v_attn,
    v_in,
    v_down,
    v_gains,
):
    image, e = patches[0], cotangent[0]
    width = image.shape[1]
    rows, down_rows = w_attn.shape[1], w_down.shape[0]
    shard = lax.axis_index("fsdp")
    low_attn, low_in, low_down, low_gains = (
        w.astype(LOW) for w in (w_attn, w_in, w_down, gains)
    )
    owned = lax.broadcasted_iota(jnp.int32, (1, width), 1) // rows == shard
    slab = jnp.where(owned, jnp.tile(low_gains, (1, grid.fsdp)), jnp.zeros((), LOW))
    slab = jnp.pad(slab, ((0, SLAB - 2), (0, 0)))
    groups = [
        split_columns(g)
        for g in (
            jnp.concatenate([low_attn[0], low_attn[1], low_attn[2], slab], 0),
            jnp.concatenate([low_attn[3], low_down], 0),
        )
    ]
    pairs = width // (2 * HD)
    in_full = lax.all_gather(low_in.reshape(2 * rows, -1), "fsdp")
    in_full = [in_full] if grid.cube else [in_full[:, :rows], in_full[:, rows:]]
    third = Source(grid, in_full, True)

    if grid.cube:
        x = lax.axis_index("dp")
        parts = [lax.dynamic_index_in_dim(g, x, 0, False) for g in groups]
        one, two = Spread(grid, parts[0]), Spread(grid, parts[1])
        one.send_levels()
        one.levels, two.part = after(one.levels, two.part)
        one.load_column()
        one.send_sides()
        two.send_levels()
        (one.side, one.across), two.levels = after((one.side, one.across), two.levels)
        one.send_corners()
        two.load_column()
        two.send_sides()
        one.finish()
        first = Source(grid, one.pieces)
        normed, qkv, full_gains = project_in(grid, first, image, jnp.zeros((SLAB, width), WIDE))
        context = attend(qkv, counts)
        context, two.side, two.across = lax.optimization_barrier((context, two.side, two.across))
        two.send_corners()
        two.finish()
        second = Source(grid, two.pieces)
        second.down_rows = down_rows

        (output, d_attended, d_context, d_gain_two), out_grads, in_grads = feed_forward(
            grid, second, third, image, context, e, counts, full_gains
        )
        three = Reduce(grid, *in_grads)
        three.send_core()
        two_keep, two_sent = out_grads
        two_got = grid.flip_core(two_sent)
        cut = pairs // 3
        d_qkv = [attend_back(qkv, d_context, counts, 0, cut)]
        three.got, d_qkv = after(three.got, d_qkv)
        sides = three.load_sides()
        three.send_sides(sides)
        _, (two_got, d_context) = after(sides, (two_got, d_context))
        shape = (2, grid.nz, 2) + two_keep.shape[2:]
        two = Fold(grid, [two_keep.reshape(shape), two_got.reshape(shape)])
        bits = two.by_bits(1)
        x, z, y, c = grid.place()
        leave = two.leave(bits, lax.rem(z, 2))
        leave, d_context = after([leave[0], leave[1]], d_context)
        arrived = [grid.swap_z(v, 1) for v in leave]
        d_qkv.append(attend_back(qkv, d_context, counts, cut, pairs - cut))
        input_grad, grads = project_back(
            grid, first, image, normed, d_qkv, d_attended, full_gains, d_gain_two
        )
        for bit in range(1, bits):
            grads, arrived = after(grads, arrived)
            two.parts.append(jnp.stack(arrived) if bit == 1 else arrived)
            leave, three.sides = after(two.leave(bits - bit, lax.rem(z >> bit, 2)), three.sides)
            arrived = grid.swap_z(leave, 1 << bit)
        one = Reduce(grid, *grads)
        one.send_core()
        leave, rest = fold_column(three)
        in_three = grid.swap_z(leave, 1)
        leave, one.got = after(leave, one.got)
        sides = one.load_sides()
        one.send_sides(sides)
        _, (arrived, in_three) = after(sides, (arrived, in_three))
        two.parts.append(arrived)
        arrived = grid.flip_y(two.leave(1, y))
        three = Fold(grid, [rest, in_three])
        bits = three.by_bits(0)
        for bit in range(1, bits + 1):
            in_three = grid.swap_z(three.leave(bits - bit, 0), 1 << bit)
            three.parts.append(in_three)
        one.load_levels()
        one.send_levels()
        _, arrived = after(one.leave, arrived)
        two.parts.append(arrived)
        leave = two.leave(0, x)
        arrived = grid.flip_x(leave)
        two.parts.append(arrived)
        _, in_three = after(leave, in_three)
        three.parts[-1] = in_three
        three.total = three.total()
        three.other = grid.flip_x(three.total)
        two.total = two.total()
        two.other = grid.flip_x(two.total)
        totals = (three.total, two.total)
        one.total, squared = finish(grid, one.own, one.arrive, totals, SLAB)
        one.send_total()
        grad_norm = jnp.sqrt(total_of(grid, squared[0]))
        reduced = [(g.total, g.other) for g in (one, two, three)]
    else:
        groups = [lax.all_gather(g, "fsdp", axis=1) for g in groups]

        def whole(full, low, n):
            full = full[:, :, low : low + n].reshape(2, grid.fsdp * n, full.shape[3])
            return jnp.concatenate([full[0], full[1]], -1)

        slabs = jnp.sum(groups[0][:, :, 3 * rows :].astype(WIDE), 1)
        first = Source(grid, [whole(groups[0], j * rows, rows) for j in range(3)], True)
        second = Source(
            grid, [whole(groups[1], 0, rows), whole(groups[1], rows, down_rows)], True
        )
        second.down_rows = down_rows
        normed, qkv, full_gains = project_in(
            grid, first, image, jnp.concatenate([slabs[0], slabs[1]], -1)
        )
        context = attend(qkv, counts)
        (output, d_attended, d_context, d_gain_two), out_grads, in_grads = feed_forward(
            grid, second, third, image, context, e, counts, full_gains
        )
        d_qkv = [attend_back(qkv, d_context, counts, 0, pairs)]
        input_grad, grads = project_back(
            grid, first, image, normed, d_qkv, d_attended, full_gains, d_gain_two
        )

        reduced = []
        for (g,) in (grads, out_grads, in_grads):
            total = lax.psum_scatter(g.astype(WIDE), "fsdp", scatter_dimension=1)
            reduced.append(lax.psum(total.astype(LOW), "dp"))
        x = jnp.int32(0)
        mine = owned.reshape(2, 1, width // 2)
        slabs = jnp.where(mine, reduced[0][:, 3 * rows :], jnp.zeros((), LOW))
        squared = squares(reduced[0][:, : 3 * rows]) + squares(slabs)
        squared = squared + squares(reduced[1]) + squares(reduced[2])
        grad_norm = jnp.sqrt(total_of(grid, squared))

    updated = update(
        grid,
        grad_norm,
        x,
        (w_attn, w_in, w_down, gains),
        (m_attn, m_in, m_down, m_gains),
        (v_attn, v_in, v_down, v_gains),
        reduced,
    )
    return (output[None], input_grad[None], grad_norm, *updated)


def solution(mesh):
    placed = (
        P(("dp", "fsdp"), None, None),
        P(("dp", "fsdp")),
        P(("dp", "fsdp"), None, None),
        P(None, "fsdp", None),
        P(None, "fsdp", None),
        P("fsdp", None),
        P(None, "fsdp"),
        P(None, "fsdp", None),
        P(None, "fsdp", None),
        P("fsdp", None),
        P(None, "fsdp"),
        P(None, "fsdp", None),
        P(None, "fsdp", None),
        P("fsdp", None),
        P(None, "fsdp"),
    )
    grid = Grid(mesh.shape["dp"], mesh.shape["fsdp"])
    return jax.shard_map(
        functools.partial(on_device, grid),
        mesh=mesh,
        in_specs=placed,
        out_specs=(
            P(("dp", "fsdp"), None, None),
            P(("dp", "fsdp"), None, None),
            P(),
            P(None, "fsdp", None),
            P(None, "fsdp", None),
            P("fsdp", None),
            P(None, "fsdp"),
            P(None, "fsdp", None),
            P(None, "fsdp", None),
            P("fsdp", None),
            P(None, "fsdp"),
            P(None, "fsdp", None),
            P(None, "fsdp", None),
            P("fsdp", None),
            P(None, "fsdp"),
        ),
        check_vma=False,
    )
```

```python
import functools
import math

import jax
import jax.numpy as jnp
from jax import lax
from jax.experimental import pallas as pl
from jax.experimental.pallas import tpu as pltpu
from jax.sharding import PartitionSpec as P

HD = 64
STEP = 10


NORM_EPS = 1e-06
MASKED = -1000000000.0
BETA_ONE = 0.9
BETA_TWO = 0.999
ADAM_EPS = 1e-08
CLIP_AT = 1.0
MATRIX_RATE = 0.04
MATRIX_DECAY = 0.1
GAIN_RATE = 0.8

EVERY = ("dp", "fsdp")
LOW = jnp.bfloat16
WIDE = jnp.float32
SLAB = 16
MIB = 1024 * 1024
ANYWHERE = pl.BlockSpec(memory_space=pl.ANY)


class Grid:
    def __init__(self, dp, fsdp):
        self.dp, self.fsdp = dp, fsdp
        self.nz = fsdp // 4
        power = self.nz & (self.nz - 1) == 0
        self.cube = dp == 2 and fsdp % 4 == 0 and self.nz % 2 == 0 and power

    def move(self, step):
        pairs = []
        for source in range(self.dp * self.fsdp):
            x, rest = divmod(source, self.fsdp)
            z, rest = divmod(rest, 4)
            y, core = divmod(rest, 2)
            x, z, y, core = step(x, z, y, core)
            pairs.append((source, x * self.fsdp + (z * 2 + y) * 2 + core))
        return pairs

    def flip_x(self, v):
        return lax.ppermute(v, EVERY, self.move(lambda x, z, y, c: (1 - x, z, y, c)))

    def flip_y(self, v):
        return lax.ppermute(v, EVERY, self.move(lambda x, z, y, c: (x, z, 1 - y, c)))

    def flip_xy(self, v):
        return lax.ppermute(v, EVERY, self.move(lambda x, z, y, c: (1 - x, z, 1 - y, c)))

    def flip_core(self, v):
        return lax.ppermute(v, EVERY, self.move(lambda x, z, y, c: (x, z, y, 1 - c)))

    def swap_z(self, v, bit):
        return lax.ppermute(v, EVERY, self.move(lambda x, z, y, c: (x, z ^ bit, y, c)))

    def place(self):
        x, f = lax.axis_index("dp"), lax.axis_index("fsdp")
        return x, f // 4, lax.rem(f // 2, 2), lax.rem(f, 2)


def after(first, then):
    return lax.optimization_barrier((first, then))


class Spread:
    def __init__(self, grid, part):
        self.grid, self.part = grid, part

    def send_levels(self):
        self.levels = [self.grid.swap_z(self.part, k) for k in range(1, self.grid.nz)]

    def load_column(self):
        self.column = jnp.stack([self.part] + self.levels)

    def send_sides(self):
        self.side = self.grid.flip_x(self.column)
        self.across = self.grid.flip_y(self.column)

    def send_corners(self):
        self.corner = self.grid.flip_x(self.across)
        self.most = jnp.concatenate([self.column, self.side, self.across])
        self.other_most = self.grid.flip_core(self.most)

    def finish(self):
        self.other_rest = self.grid.flip_core(self.corner)

    @property
    def pieces(self):
        return [self.most, self.corner, self.other_most, self.other_rest]


def piece_places(grid):
    nz = grid.nz
    most = [(x, y, level) for x, y in ((0, 0), (1, 0), (0, 1)) for level in range(nz)]
    rest = [(1, 1, level) for level in range(nz)]
    return [[(x, y, core, n) for x, y, n in spots] for core in (0, 1) for spots in (most, rest)]


class Reduce:
    def __init__(self, grid, keep, sent):
        self.grid, self.keep, self.sent = grid, keep, sent

    def send_core(self):
        self.got = self.grid.flip_core(self.sent)

    def split(self, array):
        return array.reshape((2, self.grid.nz, 2) + array.shape[2:])

    def block(self, h, at_y):
        total = 0.0
        for array in (self.keep, self.got):
            array = array.reshape((2, self.grid.nz, 2) + array.shape[2:])
            part = lax.dynamic_index_in_dim(array, h, 0, False)
            total = total + lax.dynamic_index_in_dim(part, at_y, 1, False).astype(WIDE)
        return total

    def load_sides(self):
        x, z, y, c = self.grid.place()
        places = ((1 - x, y), (x, 1 - y), (1 - x, 1 - y))
        return [self.block(h, at_y).astype(LOW) for h, at_y in places]

    def send_sides(self, sides):
        sends = (self.grid.flip_x, self.grid.flip_y, self.grid.flip_xy)
        self.sides = [send(v) for send, v in zip(sends, sides)]

    def load_levels(self):
        x, z, y, c = self.grid.place()
        column = self.block(x, y) + sum(v.astype(WIDE) for v in self.sides)
        column = column.astype(LOW)
        self.own = lax.dynamic_index_in_dim(column, z, 0, False)
        self.leave = [
            lax.dynamic_index_in_dim(column, z ^ k, 0, False) for k in range(1, self.grid.nz)
        ]

    def send_levels(self):
        self.arrive = [self.grid.swap_z(v, k) for k, v in enumerate(self.leave, 1)]

    def load_total(self):
        self.total = sum((v.astype(WIDE) for v in self.arrive), self.own.astype(WIDE)).astype(LOW)

    def send_total(self):
        self.other = self.grid.flip_x(self.total)


class Fold:
    def __init__(self, grid, parts):
        self.grid, self.parts = grid, parts

    def by_bits(self, dim):
        count = self.parts[0].shape[dim].bit_length() - 1
        self.parts = [v.reshape(v.shape[:dim] + (2,) * count + v.shape[dim + 1 :]) for v in self.parts]
        return count

    def leave(self, dim, mine):
        leave = sum(lax.dynamic_index_in_dim(v, 1 - mine, dim, False).astype(WIDE) for v in self.parts)
        self.parts = [lax.dynamic_index_in_dim(v, mine, dim, False) for v in self.parts]
        return leave.astype(LOW)

    def total(self):
        return sum(v.astype(WIDE) for v in self.parts).astype(LOW)


def total_of(grid, value):
    if not grid.cube:
        return lax.psum(value, "fsdp")
    value = value + grid.flip_core(value)
    value = value + grid.flip_x(value)
    value = value + grid.flip_y(value)
    bit = 1
    while bit < grid.nz:
        value = value + grid.swap_z(value, bit)
        bit *= 2
    return value


def split_columns(v):
    return jnp.stack(jnp.split(v, 2, -1))


def params(mib, semantics=None):
    return pltpu.CompilerParams(vmem_limit_bytes=mib * MIB, dimension_semantics=semantics)


def cost(microseconds):
    return pl.CostEstimate(flops=int(microseconds * 1e6), bytes_accessed=0, transcendentals=0)


def dot(a, b):
    return jnp.dot(a, b, preferred_element_type=WIDE)


def dot_nt(a, b):
    return lax.dot_general(a, b, (((1,), (1,)), ((), ())), preferred_element_type=WIDE)


def dot_tn(a, b):
    return lax.dot_general(a, b, (((0,), (0,)), ((), ())), preferred_element_type=WIDE)


class Source:
    def __init__(self, grid, arrays, whole=False):
        self.grid, self.arrays, self.whole = grid, arrays, whole
        self.specs = [ANYWHERE] * len(arrays)

    def copy(self, refs, low, rows, target, sem):
        grid = self.grid
        x, z, y, c = grid.place()
        for ref, spots in zip(refs, piece_places(grid)):
            for entry, (dx, dy, dc, level) in enumerate(spots):
                half = lax.rem(x + dx, 2)
                shard = ((z ^ level) * 2 + lax.rem(y + dy, 2)) * 2 + lax.rem(c + dc, 2)
                source = ref.at[entry, pl.ds(low, rows)]
                pltpu.make_async_copy(source, target(half, shard), sem).start()


def wait_all(ref, sem):
    pltpu.make_async_copy(ref, ref, sem).wait()


def shard_target(matrix, rows):
    n = matrix.shape[-1] // 2

    def target(half, shard):
        return matrix.at[
            pl.ds(pl.multiple_of(shard * rows, 16), rows), pl.ds(pl.multiple_of(half * n, 128), n)
        ]

    return target


def start_load(source, refs, low, rows, matrix, sem, whole=0):
    if not source.whole:
        source.copy(refs, low, rows, shard_target(matrix, rows), sem)
    else:
        pltpu.make_async_copy(refs[whole], matrix, sem).start()


def load_rows(grid, refs, which, low, target, sem):
    source = refs[0].at[:, pl.ds(low, target.shape[1])] if grid.cube else refs[which]
    pltpu.make_async_copy(source, target, sem).start()


def store_grad(grid, refs, index, low, rows, value):
    lead, columns = index
    if not grid.cube:
        refs[0][lead, :, low : low + rows, columns] = value.astype(LOW).reshape(grid.fsdp, rows, -1)
        return
    c = lax.rem(lax.axis_index("fsdp"), 2)
    value = value.astype(LOW).reshape(grid.fsdp // 2, 2, rows, value.shape[-1])
    even, odd = value[:, 0], value[:, 1]
    refs[0][lead, :, low : low + rows, columns] = jnp.where(c == 0, even, odd)
    refs[1][lead, :, low : low + rows, columns] = jnp.where(c == 0, odd, even)


def grad_shapes(grid, rows, columns):
    if not grid.cube:
        return [jax.ShapeDtypeStruct((2, grid.fsdp, rows, columns // 2), LOW)]
    return [jax.ShapeDtypeStruct((2, grid.fsdp // 2, rows, columns // 2), LOW)] * 2


def norm_rows(values):
    return lax.rsqrt(jnp.mean(values * values, -1, keepdims=True) + NORM_EPS)


def norm_back(values, scale, gain, grad):
    y = values * scale
    c = grad * gain
    back = scale * (c - y * jnp.mean(c * y, -1, keepdims=True))
    return back, jnp.sum(grad * y, 0, keepdims=True)


def project_in(grid, source, image, gains):
    length, width = image.shape
    rows = width // grid.fsdp
    count = len(source.arrays)

    def body(*refs):
        image_ref, gains_ref, pieces = refs[0], refs[1], refs[2 : 2 + count]
        normed_ref, qkv_ref, gains_out, weights, slabs, sems = refs[2 + count :]
        for j in range(3):
            start_load(source, pieces, j * rows, rows, weights.at[j], sems.at[j], j)
        if grid.cube:
            source.copy(pieces, 3 * rows, SLAB, lambda h, f: slabs.at[h, f], sems.at[3])
        values = image_ref[...].astype(WIDE)
        scaled = values * norm_rows(values)
        if grid.cube:
            wait_all(slabs, sems.at[3])
            found = jnp.sum(slabs[...].astype(WIDE), 1)
            gain = jnp.concatenate([found[0], found[1]], -1)
        else:
            gain = gains_ref[...].astype(WIDE)
        gains_out[...] = gain
        normed = (scaled * gain[0:1]).astype(LOW)
        normed_ref[...] = normed
        for j in range(3):
            wait_all(weights.at[j], sems.at[j])
            qkv_ref[j] = dot(normed, weights[j]).astype(LOW)

    vmem = pl.BlockSpec(memory_space=pltpu.VMEM)
    return pl.pallas_call(
        body,
        out_shape=[
            jax.ShapeDtypeStruct((length, width), LOW),
            jax.ShapeDtypeStruct((3, length, width), LOW),
            jax.ShapeDtypeStruct((SLAB, width), WIDE),
        ],
        in_specs=[vmem, vmem] + source.specs,
        out_specs=[vmem] * 3,
        scratch_shapes=[
            pltpu.VMEM((3, width, width), LOW),
            pltpu.VMEM((2, grid.fsdp, SLAB, width // 2), LOW),
            pltpu.SemaphoreType.DMA((4,)),
        ],
        compiler_params=params(12),
        cost_estimate=cost(8),
        name="project_in",
    )(image, gains, *source.arrays)


def attend(qkv, counts):
    length, width = qkv.shape[1:]
    pair = 2 * HD

    def body(counts_ref, qkv_ref, context_ref):
        seen = lax.broadcasted_iota(jnp.int32, (1, length), 1) < counts_ref[0]
        first = lax.broadcasted_iota(jnp.int32, (1, pair), 1) < HD
        q, k, v = qkv_ref[0], qkv_ref[1], qkv_ref[2]
        found = []
        for head in range(2):
            own = first if head == 0 else jnp.logical_not(first)
            scores = dot_nt(jnp.where(own, q, jnp.zeros_like(q)), k)
            scores = jnp.where(seen, scores, MASKED)
            probs = jnp.exp(scores - jnp.max(scores, -1, keepdims=True))
            summed = dot(probs.astype(LOW), jnp.where(own, v, jnp.ones_like(v)))
            found.append(summed / pltpu.roll(summed, HD, 1))
        context_ref[...] = jnp.where(first, found[0], found[1]).astype(LOW)

    return pl.pallas_call(
        body,
        grid=(width // pair,),
        out_shape=jax.ShapeDtypeStruct((length, width), LOW),
        in_specs=[
            pl.BlockSpec(memory_space=pltpu.SMEM),
            pl.BlockSpec((3, length, pair), lambda i: (0, 0, i)),
        ],
        out_specs=pl.BlockSpec((length, pair), lambda i: (0, i)),
        compiler_params=params(8, ("arbitrary",)),
        cost_estimate=cost(9),
        name="attend",
    )(counts, qkv)


def attend_back(qkv, d_context, counts, low, steps):
    length = qkv.shape[1]
    pair = 2 * HD
    width = steps * pair

    def body(counts_ref, qkv_ref, d_ref, out_ref):
        seen = lax.broadcasted_iota(jnp.int32, (length, 1), 0) < counts_ref[0]
        first = lax.broadcasted_iota(jnp.int32, (1, pair), 1) < HD
        q, k, v, d = qkv_ref[0], qkv_ref[1], qkv_ref[2], d_ref[...]
        found = []
        for head in range(2):
            own = first if head == 0 else jnp.logical_not(first)
            scores = dot_nt(k, jnp.where(own, q, jnp.zeros_like(q)))
            scores = jnp.where(seen, scores, MASKED)
            probs = jnp.exp(scores - jnp.max(scores, 0, keepdims=True))
            probs = probs * (1.0 / jnp.sum(probs, 0, keepdims=True))
            d_probs = dot_nt(v, jnp.where(own, d, jnp.zeros_like(d)))
            weighed = probs * d_probs
            d_scores = (weighed - probs * jnp.sum(weighed, 0, keepdims=True)).astype(LOW)
            found.append((dot_tn(d_scores, k), dot(d_scores, q), dot(probs.astype(LOW), d)))
        for j in range(3):
            out_ref[j] = jnp.where(first, found[0][j], found[1][j]).astype(LOW)

    return pl.pallas_call(
        body,
        grid=(width // pair,),
        out_shape=jax.ShapeDtypeStruct((3, length, width), LOW),
        in_specs=[
            pl.BlockSpec(memory_space=pltpu.SMEM),
            pl.BlockSpec((3, length, pair), lambda i: (0, 0, low + i)),
            pl.BlockSpec((length, pair), lambda i: (0, low + i)),
        ],
        out_specs=pl.BlockSpec((3, length, pair), lambda i: (0, 0, i)),
        compiler_params=params(8, ("arbitrary",)),
        cost_estimate=cost(2.3 * steps + 2),
        name="attend_back",
    )(counts, qkv, d_context)


def feed_forward(grid, second, third, image, context, cotangent, counts, gains):
    length, width = image.shape
    rows = width // grid.fsdp
    down_rows = second.down_rows
    hidden_width = down_rows * grid.fsdp
    steps = 4
    chunk = hidden_width // steps
    n_second, n_third = len(second.arrays), len(third.arrays)
    n_refs = len(grad_shapes(grid, rows, width))

    def body(*refs):
        counts_ref, image_ref, context_ref, cotangent_ref, gains_ref = refs[:5]
        seconds, refs = refs[5 : 5 + n_second], refs[5 + n_second :]
        thirds, refs = refs[:n_third], refs[n_third:]
        output_ref, d_attended_ref, d_context_ref, d_gain_ref = refs[:4]
        out_grads, refs = refs[4 : 4 + n_refs], refs[4 + n_refs :]
        in_grads, refs = refs[:n_refs], refs[n_refs:]
        w_out, w_down, w_gate, w_up, attended, normed, normed_t, e_ref, total, d_normed, sems = refs
        step = pl.program_id(0)
        seen = lax.broadcasted_iota(jnp.int32, (length, 1), 0) < counts_ref[0]

        @pl.when(step == 0)
        def _():
            start_load(second, seconds, 0, rows, w_out, sems.at[0], 0)
            load_rows(grid, thirds, 0, 0, w_gate, sems.at[1])
            load_rows(grid, thirds, 1, rows, w_up, sems.at[2])
            start_load(second, seconds, rows, down_rows, w_down, sems.at[3], 1)
            e = cotangent_ref[...]
            e_ref[...] = jnp.where(seen, e, jnp.zeros_like(e))
            wait_all(w_out, sems.at[0])
            values = image_ref[...].astype(WIDE) + dot(context_ref[...], w_out[...])
            attended[...] = values
            low = (values * norm_rows(values) * gains_ref[1:2]).astype(LOW)
            normed[...] = low
            normed_t[...] = low.T
            total[...] = values
            d_normed[...] = jnp.zeros_like(d_normed)

        def one_chunk(first):
            columns = pl.ds(pl.multiple_of(step * chunk, chunk), chunk)
            if first:
                wait_all(w_gate, sems.at[1])
            gate_w = w_gate[:, :, columns].reshape(width, chunk)
            gate = dot(normed[...], gate_w)
            if first:
                wait_all(w_up, sems.at[2])
            up_w = w_up[:, :, columns].reshape(width, chunk)
            up = dot(normed[...], up_w)
            if first:
                wait_all(w_down, sems.at[3])
            down_w = w_down[columns]
            e = e_ref[...]
            square = gate * gate
            bend = jnp.tanh(0.7978845608 * (gate + 0.044715 * square * gate))
            half_up = 0.5 * (1.0 + bend)
            gelu = gate * half_up
            slope = half_up + 0.5 * gate * (1.0 - bend * bend) * (
                0.7978845608 * (1.0 + 3.0 * 0.044715 * square)
            )
            hidden = (gelu * up).astype(LOW)
            total[...] += dot(hidden, down_w)
            d_hidden = dot_nt(e, down_w)
            d_gate = (d_hidden * up * slope).astype(LOW)
            d_up = (d_hidden * gelu).astype(LOW)
            g_down = dot_tn(hidden, e)
            shards = chunk // down_rows
            if grid.cube:
                c = lax.rem(lax.axis_index("fsdp"), 2)
                g_down = g_down.astype(LOW).reshape(shards // 2, 2, down_rows, width)
                even, odd = g_down[:, 0], g_down[:, 1]
                g_down = [jnp.where(c == 0, even, odd), jnp.where(c == 0, odd, even)]
                lead = pl.ds(step * (shards // 2), shards // 2)
            else:
                g_down = [g_down.astype(LOW).reshape(shards, down_rows, width)]
                lead = pl.ds(step * shards, shards)
            for ref, value in zip(out_grads, g_down):
                for h in range(2):
                    ref[h, lead, rows:] = value[:, :, h * (width // 2) : (h + 1) * (width // 2)]
            everything = (0, slice(None))
            store_grad(grid, in_grads, everything, 0, rows, dot(normed_t[...], d_gate))
            store_grad(grid, in_grads, everything, rows, rows, dot(normed_t[...], d_up))
            d_normed[...] += dot_nt(d_gate, gate_w) + dot_nt(d_up, up_w)

        @pl.when(step == 0)
        def _():
            one_chunk(True)

        @pl.when(step > 0)
        def _():
            one_chunk(False)

        @pl.when(step == steps - 1)
        def _():
            output_ref[...] = jnp.where(seen, total[...], 0.0).astype(LOW)
            values = attended[...]
            back, d_gain = norm_back(values, norm_rows(values), gains_ref[1:2], d_normed[...])
            d_gain_ref[...] = jnp.broadcast_to(d_gain, d_gain_ref.shape)
            d_attended = e_ref[...].astype(WIDE) + back
            d_attended_ref[...] = d_attended
            low = d_attended.astype(LOW)
            d_context_ref[...] = dot_nt(low, w_out[...]).astype(LOW)
            g_out = dot_tn(context_ref[...], low)
            for h in range(2):
                part = g_out[:, h * (width // 2) : (h + 1) * (width // 2)]
                store_grad(grid, out_grads, (h, slice(None)), 0, rows, part)

    vmem = pl.BlockSpec(memory_space=pltpu.VMEM)
    per_half = steps // 2
    out_grads = grad_shapes(grid, rows + down_rows, width)
    in_grads = grad_shapes(grid, 2 * rows, hidden_width)
    block = (1,) + in_grads[0].shape[1:3] + (chunk,)
    in_block = pl.BlockSpec(block, lambda i: (i // per_half, 0, 0, lax.rem(i, per_half)))
    results = pl.pallas_call(
        body,
        grid=(steps,),
        out_shape=[
            jax.ShapeDtypeStruct((length, width), LOW),
            jax.ShapeDtypeStruct((length, width), WIDE),
            jax.ShapeDtypeStruct((length, width), LOW),
            jax.ShapeDtypeStruct((8, width), WIDE),
        ]
        + out_grads
        + in_grads,
        in_specs=[pl.BlockSpec(memory_space=pltpu.SMEM)] + [vmem] * 4 + second.specs + third.specs,
        out_specs=[vmem] * (4 + n_refs) + [in_block] * n_refs,
        scratch_shapes=[
            pltpu.VMEM((width, width), LOW),
            pltpu.VMEM((hidden_width, width), LOW),
            pltpu.VMEM((grid.fsdp, rows, hidden_width), LOW),
            pltpu.VMEM((grid.fsdp, rows, hidden_width), LOW),
            pltpu.VMEM((length, width), WIDE),
            pltpu.VMEM((length, width), LOW),
            pltpu.VMEM((width, length), LOW),
            pltpu.VMEM((length, width), LOW),
            pltpu.VMEM((length, width), WIDE),
            pltpu.VMEM((length, width), WIDE),
            pltpu.SemaphoreType.DMA((4,)),
        ],
        compiler_params=params(56, ("arbitrary",)),
        cost_estimate=cost(28),
        name="feed_forward",
    )(counts, image, context, cotangent, gains, *second.arrays, *third.arrays)
    return results[:4], results[4 : 4 + n_refs], results[4 + n_refs :]


def project_back(grid, source, image, normed, d_qkv, d_attended, gains, d_gain_two):
    length, width = image.shape
    rows = width // grid.fsdp
    count, parts = len(source.arrays), len(d_qkv)
    shapes = grad_shapes(grid, 3 * rows + SLAB, width)

    def body(*refs):
        image_ref, normed_ref, d_attended_ref, gains_ref, d_gain_ref = refs[:5]
        d_refs, refs = refs[5 : 5 + parts], refs[5 + parts :]
        pieces, refs = refs[:count], refs[count:]
        input_grad_ref, grads, (weights, sems) = refs[0], refs[1 : 1 + len(shapes)], refs[-2:]
        for j in range(3):
            start_load(source, pieces, j * rows, rows, weights.at[j], sems.at[j], j)
        normed_t = normed_ref[...].T
        d_parts = [jnp.concatenate([d_ref[j] for d_ref in d_refs], -1) for j in range(3)]
        for j in range(3):
            g = dot(normed_t, d_parts[j])
            for h in range(2):
                part = g[:, h * (width // 2) : (h + 1) * (width // 2)]
                store_grad(grid, grads, (h, slice(None)), j * rows, rows, part)
        d_normed = jnp.zeros((length, width), WIDE)
        for j in range(3):
            wait_all(weights.at[j], sems.at[j])
            d_normed = d_normed + dot_nt(d_parts[j], weights[j])
        values = image_ref[...].astype(WIDE)
        back, d_gain = norm_back(values, norm_rows(values), gains_ref[0:1], d_normed)
        input_grad_ref[...] = (d_attended_ref[...] + back).astype(LOW)
        slab = jnp.concatenate(
            [d_gain, d_gain_ref[0:1], jnp.zeros((SLAB - 2, width), WIDE)], 0
        ).astype(LOW)
        for h in range(2):
            part = slab[:, h * (width // 2) : (h + 1) * (width // 2)]
            for ref in grads:
                ref[h, :, 3 * rows :] = jnp.broadcast_to(part[None], (ref.shape[1],) + part.shape)

    vmem = pl.BlockSpec(memory_space=pltpu.VMEM)
    results = pl.pallas_call(
        body,
        out_shape=[jax.ShapeDtypeStruct((length, width), LOW)] + shapes,
        in_specs=[vmem] * (5 + parts) + source.specs,
        out_specs=[vmem] * (1 + len(shapes)),
        scratch_shapes=[
            pltpu.VMEM((3, width, width), LOW),
            pltpu.SemaphoreType.DMA((3,)),
        ],
        compiler_params=params(12),
        cost_estimate=cost(11),
        name="project_back",
    )(image, normed, d_attended, gains, d_gain_two, *d_qkv, *source.arrays)
    return results[0], results[1:]


def fold_column(reduce):
    grid = reduce.grid
    rows, columns = reduce.keep.shape[2:]
    half = grid.nz // 2

    def body(place_ref, keep_ref, got_ref, *refs):
        total = keep_ref[0, 0].astype(WIDE) + got_ref[0, 0].astype(WIDE)
        for ref in refs[:-1]:
            total = total + ref[0].astype(WIDE)
        refs[-1][0] = total.astype(LOW)

    def level(i, place):
        return place[1] ^ (2 * i + 1)

    block = (1, rows, columns)
    whole = pl.BlockSpec(
        (1,) + block, lambda i, place: (place[0], level(i, place) * 2 + place[2], 0, 0)
    )
    side = pl.BlockSpec(block, lambda i, place: (level(i, place), 0, 0))
    x, z, y, _ = grid.place()
    return pl.pallas_call(
        body,
        grid_spec=pltpu.PrefetchScalarGridSpec(
            num_scalar_prefetch=1,
            grid=(half,),
            in_specs=[whole, whole] + [side] * len(reduce.sides),
            out_specs=pl.BlockSpec(block, lambda i, place: (i, 0, 0)),
        ),
        out_shape=jax.ShapeDtypeStruct((half, rows, columns), LOW),
        compiler_params=params(16, ("arbitrary",)),
        cost_estimate=cost(6e7),
        name="fold_column",
    )(jnp.stack([x, z, y]).astype(jnp.int32), reduce.keep, reduce.got, *reduce.sides)


def adamw(param, first, second, grad, rate, decay):
    first = BETA_ONE * first + (1.0 - BETA_ONE) * grad
    second = BETA_TWO * second + (1.0 - BETA_TWO) * grad * grad
    update = first / (1.0 - BETA_ONE**STEP) / (jnp.sqrt(second / (1.0 - BETA_TWO**STEP)) + ADAM_EPS)
    return (param - rate * (update + decay * param), first, second)


def finish(grid, own, arrive, totals, slab_rows):
    rows, columns = own.shape
    per_shard = 2 * columns // grid.fsdp

    def body(*refs):
        others, refs, (total_ref, sum_ref) = refs[: len(totals)], refs[len(totals) : -2], refs[-2:]
        total = sum(ref[...].astype(WIDE) for ref in refs)
        total = total.astype(LOW)
        total_ref[...] = total
        column = lax.broadcasted_iota(jnp.int32, (rows, columns), 1) + lax.axis_index("dp") * columns
        row = lax.broadcasted_iota(jnp.int32, (rows, columns), 0)
        first = lax.axis_index("fsdp") * per_shard
        mine = jnp.logical_and(column >= first, column < first + per_shard)
        counted = jnp.where(jnp.logical_or(row < rows - slab_rows, mine), total.astype(WIDE), 0.0)
        squared = jnp.sum(counted * counted)
        for ref in others:
            value = ref[...].astype(WIDE)
            squared = squared + jnp.sum(value * value)
        sum_ref[0] = squared

    vmem, smem = (pl.BlockSpec(memory_space=m) for m in (pltpu.VMEM, pltpu.SMEM))
    return pl.pallas_call(
        body,
        out_shape=[jax.ShapeDtypeStruct((rows, columns), LOW), jax.ShapeDtypeStruct((1,), WIDE)],
        in_specs=[vmem] * (1 + len(arrive) + len(totals)),
        out_specs=[vmem, smem],
        compiler_params=params(8),
        cost_estimate=cost(1),
        name="finish",
    )(*totals, own, *arrive)


def update(grid, grad_norm, x, weights, firsts, seconds, grads):
    rows = weights[0].shape[1]
    per_half = grid.fsdp // 2
    columns = weights[0].shape[2] // 2
    rates = (MATRIX_RATE, MATRIX_RATE, MATRIX_RATE, GAIN_RATE)
    decays = (MATRIX_DECAY, MATRIX_DECAY, MATRIX_DECAY, 0.0)

    def body(*refs):
        norm_ref, x_ref = refs[:2]
        weight_refs, first_refs, second_refs = refs[8:12], refs[12:16], refs[16:20]
        outs = refs[20:]
        half = pl.program_id(0)
        factor = jnp.minimum(1.0, CLIP_AT / (norm_ref[0] + 1e-06))
        group_one, group_two, group_three = (
            jnp.where(x_ref[0] == half, mine[...], other[...])
            for mine, other in zip(refs[2:8:2], refs[3:8:2])
        )

        def one(n, index, grad):
            taken = [r[n][index] for r in (weight_refs, first_refs, second_refs)]
            results = adamw(*taken, grad.astype(WIDE) * factor, rates[n], decays[n])
            for k, value in enumerate(results):
                outs[4 * k + n][index] = value

        for j in range(3):
            one(0, j, group_one[j * rows : (j + 1) * rows])
        one(0, 3, group_two[:rows])
        for j in range(2):
            one(1, j, group_three[j * rows : (j + 1) * rows])
        one(2, slice(None), group_two[rows:])
        shard = lax.axis_index("fsdp")

        @pl.when(shard // per_half == half)
        def _():
            shape = (columns, rows)
            place = lax.broadcasted_iota(jnp.int32, shape, 0) - lax.rem(shard, per_half) * rows
            pick = (place == lax.broadcasted_iota(jnp.int32, shape, 1)).astype(WIDE).astype(LOW)
            one(3, slice(None), dot(group_one[3 * rows :], pick)[:2])

    def halves(shape):
        block = shape[:-1] + (shape[-1] // 2,)
        return pl.BlockSpec(block, lambda i: (0,) * (len(shape) - 1) + (i,))

    smem, vmem = (pl.BlockSpec(memory_space=m) for m in (pltpu.SMEM, pltpu.VMEM))
    own = [halves(w.shape) for w in weights[:3]]
    own.append(pl.BlockSpec(weights[3].shape, lambda i: (0, 0)))
    return pl.pallas_call(
        body,
        grid=(2,),
        out_shape=[jax.ShapeDtypeStruct(w.shape, WIDE) for w in weights] * 3,
        in_specs=[smem, smem] + [vmem] * 6 + own * 3,
        out_specs=own * 3,
        compiler_params=params(56, ("arbitrary",)),
        cost_estimate=cost(4),
        name="update",
    )(grad_norm.reshape(1), x.reshape(1), *(v for g in grads for v in g), *weights, *firsts, *seconds)


def squares(v):
    return jnp.sum(jnp.square(v.astype(WIDE)))


def on_device(
    grid,
    patches,
    counts,
    cotangent,
    w_attn,
    w_in,
    w_down,
    gains,
    m_attn,
    m_in,
    m_down,
    m_gains,
    v_attn,
    v_in,
    v_down,
    v_gains,
):
    image, e = patches[0], cotangent[0]
    width = image.shape[1]
    rows, down_rows = w_attn.shape[1], w_down.shape[0]
    shard = lax.axis_index("fsdp")
    low_attn, low_in, low_down, low_gains = (
        w.astype(LOW) for w in (w_attn, w_in, w_down, gains)
    )
    owned = lax.broadcasted_iota(jnp.int32, (1, width), 1) // rows == shard
    slab = jnp.where(owned, jnp.tile(low_gains, (1, grid.fsdp)), jnp.zeros((), LOW))
    slab = jnp.pad(slab, ((0, SLAB - 2), (0, 0)))
    groups = [
        split_columns(g)
        for g in (
            jnp.concatenate([low_attn[0], low_attn[1], low_attn[2], slab], 0),
            jnp.concatenate([low_attn[3], low_down], 0),
        )
    ]
    pairs = width // (2 * HD)
    in_full = lax.all_gather(low_in.reshape(2 * rows, -1), "fsdp")
    in_full = [in_full] if grid.cube else [in_full[:, :rows], in_full[:, rows:]]
    third = Source(grid, in_full, True)

    if grid.cube:
        x = lax.axis_index("dp")
        parts = [lax.dynamic_index_in_dim(g, x, 0, False) for g in groups]
        one, two = Spread(grid, parts[0]), Spread(grid, parts[1])
        one.send_levels()
        one.levels, two.part = after(one.levels, two.part)
        one.load_column()
        one.send_sides()
        two.send_levels()
        (one.side, one.across), two.levels = after((one.side, one.across), two.levels)
        one.send_corners()
        two.load_column()
        two.send_sides()
        one.finish()
        first = Source(grid, one.pieces)
        normed, qkv, full_gains = project_in(grid, first, image, jnp.zeros((SLAB, width), WIDE))
        context = attend(qkv, counts)
        context, two.side, two.across = lax.optimization_barrier((context, two.side, two.across))
        two.send_corners()
        two.finish()
        second = Source(grid, two.pieces)
        second.down_rows = down_rows

        (output, d_attended, d_context, d_gain_two), out_grads, in_grads = feed_forward(
            grid, second, third, image, context, e, counts, full_gains
        )
        three = Reduce(grid, *in_grads)
        three.send_core()
        two_keep, two_sent = out_grads
        two_got = grid.flip_core(two_sent)
        cut = pairs // 3
        d_qkv = [attend_back(qkv, d_context, counts, 0, cut)]
        three.got, d_qkv = after(three.got, d_qkv)
        sides = three.load_sides()
        three.send_sides(sides)
        _, (two_got, d_context) = after(sides, (two_got, d_context))
        shape = (2, grid.nz, 2) + two_keep.shape[2:]
        two = Fold(grid, [two_keep.reshape(shape), two_got.reshape(shape)])
        bits = two.by_bits(1)
        x, z, y, c = grid.place()
        leave = two.leave(bits, lax.rem(z, 2))
        leave, d_context = after([leave[0], leave[1]], d_context)
        arrived = [grid.swap_z(v, 1) for v in leave]
        d_qkv.append(attend_back(qkv, d_context, counts, cut, pairs - cut))
        input_grad, grads = project_back(
            grid, first, image, normed, d_qkv, d_attended, full_gains, d_gain_two
        )
        for bit in range(1, bits):
            grads, arrived = after(grads, arrived)
            two.parts.append(jnp.stack(arrived) if bit == 1 else arrived)
            leave, three.sides = after(two.leave(bits - bit, lax.rem(z >> bit, 2)), three.sides)
            arrived = grid.swap_z(leave, 1 << bit)
        one = Reduce(grid, *grads)
        one.send_core()
        leave = fold_column(three)
        in_three = grid.swap_z(leave, 1)
        leave, one.got = after(leave, one.got)
        sides = one.load_sides()
        one.send_sides(sides)
        _, (arrived, in_three) = after(sides, (arrived, in_three))
        two.parts.append(arrived)
        arrived = grid.flip_y(two.leave(1, y))
        rest = [z ^ k for k in range(0, grid.nz, 2)]
        kept = [lax.dynamic_index_in_dim(three.split(v), x, 0, False) for v in (three.keep, three.got)]
        kept = [lax.dynamic_index_in_dim(v, y, 1, False) for v in kept] + three.sides
        kept = [jnp.stack([lax.dynamic_index_in_dim(v, k, 0, False) for k in rest]) for v in kept]
        three = Fold(grid, kept + [in_three])
        bits = three.by_bits(0)
        for bit in range(1, bits + 1):
            in_three = grid.swap_z(three.leave(bits - bit, 0), 1 << bit)
            three.parts.append(in_three)
        one.load_levels()
        one.send_levels()
        _, arrived = after(one.leave, arrived)
        two.parts.append(arrived)
        leave = two.leave(0, x)
        arrived = grid.flip_x(leave)
        two.parts.append(arrived)
        _, in_three = after(leave, in_three)
        three.parts[-1] = in_three
        three.total = three.total()
        three.other = grid.flip_x(three.total)
        two.total = two.total()
        two.other = grid.flip_x(two.total)
        totals = (three.total, two.total)
        one.total, squared = finish(grid, one.own, one.arrive, totals, SLAB)
        one.send_total()
        grad_norm = jnp.sqrt(total_of(grid, squared[0]))
        reduced = [(g.total, g.other) for g in (one, two, three)]
    else:
        groups = [lax.all_gather(g, "fsdp", axis=1) for g in groups]

        def whole(full, low, n):
            full = full[:, :, low : low + n].reshape(2, grid.fsdp * n, full.shape[3])
            return jnp.concatenate([full[0], full[1]], -1)

        slabs = jnp.sum(groups[0][:, :, 3 * rows :].astype(WIDE), 1)
        first = Source(grid, [whole(groups[0], j * rows, rows) for j in range(3)], True)
        second = Source(
            grid, [whole(groups[1], 0, rows), whole(groups[1], rows, down_rows)], True
        )
        second.down_rows = down_rows
        normed, qkv, full_gains = project_in(
            grid, first, image, jnp.concatenate([slabs[0], slabs[1]], -1)
        )
        context = attend(qkv, counts)
        (output, d_attended, d_context, d_gain_two), out_grads, in_grads = feed_forward(
            grid, second, third, image, context, e, counts, full_gains
        )
        d_qkv = [attend_back(qkv, d_context, counts, 0, pairs)]
        input_grad, grads = project_back(
            grid, first, image, normed, d_qkv, d_attended, full_gains, d_gain_two
        )

        reduced = []
        for (g,) in (grads, out_grads, in_grads):
            total = lax.psum_scatter(g.astype(WIDE), "fsdp", scatter_dimension=1)
            reduced.append(lax.psum(total.astype(LOW), "dp"))
        x = jnp.int32(0)
        mine = owned.reshape(2, 1, width // 2)
        slabs = jnp.where(mine, reduced[0][:, 3 * rows :], jnp.zeros((), LOW))
        squared = squares(reduced[0][:, : 3 * rows]) + squares(slabs)
        squared = squared + squares(reduced[1]) + squares(reduced[2])
        grad_norm = jnp.sqrt(total_of(grid, squared))

    updated = update(
        grid,
        grad_norm,
        x,
        (w_attn, w_in, w_down, gains),
        (m_attn, m_in, m_down, m_gains),
        (v_attn, v_in, v_down, v_gains),
        reduced,
    )
    return (output[None], input_grad[None], grad_norm, *updated)


def solution(mesh):
    placed = (
        P(("dp", "fsdp"), None, None),
        P(("dp", "fsdp")),
        P(("dp", "fsdp"), None, None),
        P(None, "fsdp", None),
        P(None, "fsdp", None),
        P("fsdp", None),
        P(None, "fsdp"),
        P(None, "fsdp", None),
        P(None, "fsdp", None),
        P("fsdp", None),
        P(None, "fsdp"),
        P(None, "fsdp", None),
        P(None, "fsdp", None),
        P("fsdp", None),
        P(None, "fsdp"),
    )
    grid = Grid(mesh.shape["dp"], mesh.shape["fsdp"])
    return jax.shard_map(
        functools.partial(on_device, grid),
        mesh=mesh,
        in_specs=placed,
        out_specs=(
            P(("dp", "fsdp"), None, None),
            P(("dp", "fsdp"), None, None),
            P(),
            P(None, "fsdp", None),
            P(None, "fsdp", None),
            P("fsdp", None),
            P(None, "fsdp"),
            P(None, "fsdp", None),
            P(None, "fsdp", None),
            P("fsdp", None),
            P(None, "fsdp"),
            P(None, "fsdp", None),
            P(None, "fsdp", None),
            P("fsdp", None),
            P(None, "fsdp"),
        ),
        check_vma=False,
    )
```

```python
import functools
import math

import jax
import jax.numpy as jnp
from jax import lax
from jax.experimental import pallas as pl
from jax.experimental.pallas import tpu as pltpu
from jax.sharding import PartitionSpec as P

HD = 64
STEP = 10


NORM_EPS = 1e-06
MASKED = -1000000000.0
BETA_ONE = 0.9
BETA_TWO = 0.999
ADAM_EPS = 1e-08
CLIP_AT = 1.0
MATRIX_RATE = 0.04
MATRIX_DECAY = 0.1
GAIN_RATE = 0.8

EVERY = ("dp", "fsdp")
LOW = jnp.bfloat16
WIDE = jnp.float32
SLAB = 16
MIB = 1024 * 1024
ANYWHERE = pl.BlockSpec(memory_space=pl.ANY)


class Grid:
    def __init__(self, dp, fsdp):
        self.dp, self.fsdp = dp, fsdp
        self.nz = fsdp // 4
        power = self.nz & (self.nz - 1) == 0
        self.cube = dp == 2 and fsdp % 4 == 0 and self.nz % 2 == 0 and power

    def move(self, step):
        pairs = []
        for source in range(self.dp * self.fsdp):
            x, rest = divmod(source, self.fsdp)
            z, rest = divmod(rest, 4)
            y, core = divmod(rest, 2)
            x, z, y, core = step(x, z, y, core)
            pairs.append((source, x * self.fsdp + (z * 2 + y) * 2 + core))
        return pairs

    def flip_x(self, v):
        return lax.ppermute(v, EVERY, self.move(lambda x, z, y, c: (1 - x, z, y, c)))

    def flip_y(self, v):
        return lax.ppermute(v, EVERY, self.move(lambda x, z, y, c: (x, z, 1 - y, c)))

    def flip_xy(self, v):
        return lax.ppermute(v, EVERY, self.move(lambda x, z, y, c: (1 - x, z, 1 - y, c)))

    def flip_core(self, v):
        return lax.ppermute(v, EVERY, self.move(lambda x, z, y, c: (x, z, y, 1 - c)))

    def swap_z(self, v, bit):
        return lax.ppermute(v, EVERY, self.move(lambda x, z, y, c: (x, z ^ bit, y, c)))

    def place(self):
        x, f = lax.axis_index("dp"), lax.axis_index("fsdp")
        return x, f // 4, lax.rem(f // 2, 2), lax.rem(f, 2)


def after(first, then):
    return lax.optimization_barrier((first, then))


class Spread:
    def __init__(self, grid, part):
        self.grid, self.part = grid, part

    def send_levels(self):
        self.levels = [self.grid.swap_z(self.part, k) for k in range(1, self.grid.nz)]

    def load_column(self):
        self.column = jnp.stack([self.part] + self.levels)

    def send_sides(self):
        self.side = self.grid.flip_x(self.column)
        self.across = self.grid.flip_y(self.column)

    def send_corners(self):
        self.corner = self.grid.flip_x(self.across)
        self.most = jnp.concatenate([self.column, self.side, self.across])
        self.other_most = self.grid.flip_core(self.most)

    def finish(self):
        self.other_rest = self.grid.flip_core(self.corner)

    @property
    def pieces(self):
        return [self.most, self.corner, self.other_most, self.other_rest]


def piece_places(grid):
    nz = grid.nz
    most = [(x, y, level) for x, y in ((0, 0), (1, 0), (0, 1)) for level in range(nz)]
    rest = [(1, 1, level) for level in range(nz)]
    return [[(x, y, core, n) for x, y, n in spots] for core in (0, 1) for spots in (most, rest)]


class Reduce:
    def __init__(self, grid, keep, sent):
        self.grid, self.keep, self.sent = grid, keep, sent

    def send_core(self):
        self.got = self.grid.flip_core(self.sent)

    def split(self, array):
        return array.reshape((2, self.grid.nz, 2) + array.shape[2:])

    def block(self, h, at_y):
        total = 0.0
        for array in (self.keep, self.got):
            array = array.reshape((2, self.grid.nz, 2) + array.shape[2:])
            part = lax.dynamic_index_in_dim(array, h, 0, False)
            total = total + lax.dynamic_index_in_dim(part, at_y, 1, False).astype(WIDE)
        return total

    def load_sides(self):
        x, z, y, c = self.grid.place()
        places = ((1 - x, y), (x, 1 - y), (1 - x, 1 - y))
        return [self.block(h, at_y).astype(LOW) for h, at_y in places]

    def send_sides(self, sides):
        sends = (self.grid.flip_x, self.grid.flip_y, self.grid.flip_xy)
        self.sides = [send(v) for send, v in zip(sends, sides)]

    def load_levels(self):
        x, z, y, c = self.grid.place()
        column = self.block(x, y) + sum(v.astype(WIDE) for v in self.sides)
        column = column.astype(LOW)
        self.own = lax.dynamic_index_in_dim(column, z, 0, False)
        self.leave = [
            lax.dynamic_index_in_dim(column, z ^ k, 0, False) for k in range(1, self.grid.nz)
        ]

    def send_levels(self):
        self.arrive = [self.grid.swap_z(v, k) for k, v in enumerate(self.leave, 1)]

    def load_total(self):
        self.total = sum((v.astype(WIDE) for v in self.arrive), self.own.astype(WIDE)).astype(LOW)

    def send_total(self):
        self.other = self.grid.flip_x(self.total)


class Fold:
    def __init__(self, grid, parts):
        self.grid, self.parts = grid, parts

    def by_bits(self, dim):
        count = self.parts[0].shape[dim].bit_length() - 1
        self.parts = [v.reshape(v.shape[:dim] + (2,) * count + v.shape[dim + 1 :]) for v in self.parts]
        return count

    def leave(self, dim, mine):
        leave = sum(lax.dynamic_index_in_dim(v, 1 - mine, dim, False).astype(WIDE) for v in self.parts)
        self.parts = [lax.dynamic_index_in_dim(v, mine, dim, False) for v in self.parts]
        return leave.astype(LOW)

    def total(self):
        return sum(v.astype(WIDE) for v in self.parts).astype(LOW)


def total_of(grid, value):
    if not grid.cube:
        return lax.psum(value, "fsdp")
    value = value + grid.flip_core(value)
    value = value + grid.flip_x(value)
    value = value + grid.flip_y(value)
    bit = 1
    while bit < grid.nz:
        value = value + grid.swap_z(value, bit)
        bit *= 2
    return value


def split_columns(v):
    return jnp.stack(jnp.split(v, 2, -1))


def params(mib, semantics=None):
    return pltpu.CompilerParams(vmem_limit_bytes=mib * MIB, dimension_semantics=semantics)


def cost(microseconds):
    return pl.CostEstimate(flops=int(microseconds * 1e6), bytes_accessed=0, transcendentals=0)


def dot(a, b):
    return jnp.dot(a, b, preferred_element_type=WIDE)


def dot_nt(a, b):
    return lax.dot_general(a, b, (((1,), (1,)), ((), ())), preferred_element_type=WIDE)


def dot_tn(a, b):
    return lax.dot_general(a, b, (((0,), (0,)), ((), ())), preferred_element_type=WIDE)


class Source:
    def __init__(self, grid, arrays, whole=False):
        self.grid, self.arrays, self.whole = grid, arrays, whole
        self.specs = [ANYWHERE] * len(arrays)

    def copy(self, refs, low, rows, target, sem):
        grid = self.grid
        x, z, y, c = grid.place()
        for ref, spots in zip(refs, piece_places(grid)):
            for entry, (dx, dy, dc, level) in enumerate(spots):
                half = lax.rem(x + dx, 2)
                shard = ((z ^ level) * 2 + lax.rem(y + dy, 2)) * 2 + lax.rem(c + dc, 2)
                source = ref.at[entry, pl.ds(low, rows)]
                pltpu.make_async_copy(source, target(half, shard), sem).start()


def wait_all(ref, sem):
    pltpu.make_async_copy(ref, ref, sem).wait()


def shard_target(matrix, rows):
    n = matrix.shape[-1] // 2

    def target(half, shard):
        return matrix.at[
            pl.ds(pl.multiple_of(shard * rows, 16), rows), pl.ds(pl.multiple_of(half * n, 128), n)
        ]

    return target


def start_load(source, refs, low, rows, matrix, sem, whole=0):
    if not source.whole:
        source.copy(refs, low, rows, shard_target(matrix, rows), sem)
    else:
        pltpu.make_async_copy(refs[whole], matrix, sem).start()


def load_rows(grid, refs, which, low, target, sem):
    source = refs[0].at[:, pl.ds(low, target.shape[1])] if grid.cube else refs[which]
    pltpu.make_async_copy(source, target, sem).start()


def store_grad(grid, refs, index, low, rows, value):
    lead, columns = index
    if not grid.cube:
        refs[0][lead, :, low : low + rows, columns] = value.astype(LOW).reshape(grid.fsdp, rows, -1)
        return
    c = lax.rem(lax.axis_index("fsdp"), 2)
    value = value.astype(LOW).reshape(grid.fsdp // 2, 2, rows, value.shape[-1])
    even, odd = value[:, 0], value[:, 1]
    refs[0][lead, :, low : low + rows, columns] = jnp.where(c == 0, even, odd)
    refs[1][lead, :, low : low + rows, columns] = jnp.where(c == 0, odd, even)


def grad_shapes(grid, rows, columns):
    if not grid.cube:
        return [jax.ShapeDtypeStruct((2, grid.fsdp, rows, columns // 2), LOW)]
    return [jax.ShapeDtypeStruct((2, grid.fsdp // 2, rows, columns // 2), LOW)] * 2


def norm_rows(values):
    return lax.rsqrt(jnp.mean(values * values, -1, keepdims=True) + NORM_EPS)


def norm_back(values, scale, gain, grad):
    y = values * scale
    c = grad * gain
    back = scale * (c - y * jnp.mean(c * y, -1, keepdims=True))
    return back, jnp.sum(grad * y, 0, keepdims=True)


def project_in(grid, source, image, gains):
    length, width = image.shape
    rows = width // grid.fsdp
    count = len(source.arrays)

    def body(*refs):
        image_ref, gains_ref, pieces = refs[0], refs[1], refs[2 : 2 + count]
        normed_ref, qkv_ref, gains_out, weights, slabs, sems = refs[2 + count :]
        for j in range(3):
            start_load(source, pieces, j * rows, rows, weights.at[j], sems.at[j], j)
        if grid.cube:
            source.copy(pieces, 3 * rows, SLAB, lambda h, f: slabs.at[h, f], sems.at[3])
        values = image_ref[...].astype(WIDE)
        scaled = values * norm_rows(values)
        if grid.cube:
            wait_all(slabs, sems.at[3])
            found = jnp.sum(slabs[...].astype(WIDE), 1)
            gain = jnp.concatenate([found[0], found[1]], -1)
        else:
            gain = gains_ref[...].astype(WIDE)
        gains_out[...] = gain
        normed = (scaled * gain[0:1]).astype(LOW)
        normed_ref[...] = normed
        for j in range(3):
            wait_all(weights.at[j], sems.at[j])
            qkv_ref[j] = dot(normed, weights[j]).astype(LOW)

    vmem = pl.BlockSpec(memory_space=pltpu.VMEM)
    return pl.pallas_call(
        body,
        out_shape=[
            jax.ShapeDtypeStruct((length, width), LOW),
            jax.ShapeDtypeStruct((3, length, width), LOW),
            jax.ShapeDtypeStruct((SLAB, width), WIDE),
        ],
        in_specs=[vmem, vmem] + source.specs,
        out_specs=[vmem] * 3,
        scratch_shapes=[
            pltpu.VMEM((3, width, width), LOW),
            pltpu.VMEM((2, grid.fsdp, SLAB, width // 2), LOW),
            pltpu.SemaphoreType.DMA((4,)),
        ],
        compiler_params=params(12),
        cost_estimate=cost(8),
        name="project_in",
    )(image, gains, *source.arrays)


def attend(qkv, counts):
    length, width = qkv.shape[1:]
    pair = 2 * HD

    def body(counts_ref, qkv_ref, context_ref):
        seen = lax.broadcasted_iota(jnp.int32, (1, length), 1) < counts_ref[0]
        first = lax.broadcasted_iota(jnp.int32, (1, pair), 1) < HD
        q, k, v = qkv_ref[0], qkv_ref[1], qkv_ref[2]
        found = []
        for head in range(2):
            own = first if head == 0 else jnp.logical_not(first)
            scores = dot_nt(jnp.where(own, q, jnp.zeros_like(q)), k)
            scores = jnp.where(seen, scores, MASKED)
            probs = jnp.exp(scores - jnp.max(scores, -1, keepdims=True))
            summed = dot(probs.astype(LOW), jnp.where(own, v, jnp.ones_like(v)))
            found.append(summed / pltpu.roll(summed, HD, 1))
        context_ref[...] = jnp.where(first, found[0], found[1]).astype(LOW)

    return pl.pallas_call(
        body,
        grid=(width // pair,),
        out_shape=jax.ShapeDtypeStruct((length, width), LOW),
        in_specs=[
            pl.BlockSpec(memory_space=pltpu.SMEM),
            pl.BlockSpec((3, length, pair), lambda i: (0, 0, i)),
        ],
        out_specs=pl.BlockSpec((length, pair), lambda i: (0, i)),
        compiler_params=params(8, ("arbitrary",)),
        cost_estimate=cost(9),
        name="attend",
    )(counts, qkv)


def attend_back(qkv, d_context, counts, low, steps):
    length = qkv.shape[1]
    pair = 2 * HD
    width = steps * pair

    def body(counts_ref, qkv_ref, d_ref, out_ref):
        seen = lax.broadcasted_iota(jnp.int32, (length, 1), 0) < counts_ref[0]
        first = lax.broadcasted_iota(jnp.int32, (1, pair), 1) < HD
        q, k, v, d = qkv_ref[0], qkv_ref[1], qkv_ref[2], d_ref[...]
        found = []
        for head in range(2):
            own = first if head == 0 else jnp.logical_not(first)
            scores = dot_nt(k, jnp.where(own, q, jnp.zeros_like(q)))
            scores = jnp.where(seen, scores, MASKED)
            probs = jnp.exp(scores - jnp.max(scores, 0, keepdims=True))
            probs = probs * (1.0 / jnp.sum(probs, 0, keepdims=True))
            d_probs = dot_nt(v, jnp.where(own, d, jnp.zeros_like(d)))
            weighed = probs * d_probs
            d_scores = (weighed - probs * jnp.sum(weighed, 0, keepdims=True)).astype(LOW)
            found.append((dot_tn(d_scores, k), dot(d_scores, q), dot(probs.astype(LOW), d)))
        for j in range(3):
            out_ref[j] = jnp.where(first, found[0][j], found[1][j]).astype(LOW)

    return pl.pallas_call(
        body,
        grid=(width // pair,),
        out_shape=jax.ShapeDtypeStruct((3, length, width), LOW),
        in_specs=[
            pl.BlockSpec(memory_space=pltpu.SMEM),
            pl.BlockSpec((3, length, pair), lambda i: (0, 0, low + i)),
            pl.BlockSpec((length, pair), lambda i: (0, low + i)),
        ],
        out_specs=pl.BlockSpec((3, length, pair), lambda i: (0, 0, i)),
        compiler_params=params(8, ("arbitrary",)),
        cost_estimate=cost(2.3 * steps + 2),
        name="attend_back",
    )(counts, qkv, d_context)


def feed_forward(grid, second, third, image, context, cotangent, counts, gains):
    length, width = image.shape
    rows = width // grid.fsdp
    down_rows = second.down_rows
    hidden_width = down_rows * grid.fsdp
    steps = 4
    chunk = hidden_width // steps
    n_second, n_third = len(second.arrays), len(third.arrays)
    n_refs = len(grad_shapes(grid, rows, width))

    def body(*refs):
        counts_ref, image_ref, context_ref, cotangent_ref, gains_ref = refs[:5]
        seconds, refs = refs[5 : 5 + n_second], refs[5 + n_second :]
        thirds, refs = refs[:n_third], refs[n_third:]
        output_ref, d_attended_ref, d_context_ref, d_gain_ref = refs[:4]
        out_grads, refs = refs[4 : 4 + n_refs], refs[4 + n_refs :]
        in_grads, refs = refs[:n_refs], refs[n_refs:]
        w_out, w_down, w_gate, w_up, attended, normed, normed_t, e_ref, total, d_normed, sems = refs
        step = pl.program_id(0)
        seen = lax.broadcasted_iota(jnp.int32, (length, 1), 0) < counts_ref[0]

        @pl.when(step == 0)
        def _():
            start_load(second, seconds, 0, rows, w_out, sems.at[0], 0)
            load_rows(grid, thirds, 0, 0, w_gate, sems.at[1])
            load_rows(grid, thirds, 1, rows, w_up, sems.at[2])
            start_load(second, seconds, rows, down_rows, w_down, sems.at[3], 1)
            e = cotangent_ref[...]
            e_ref[...] = jnp.where(seen, e, jnp.zeros_like(e))
            wait_all(w_out, sems.at[0])
            values = image_ref[...].astype(WIDE) + dot(context_ref[...], w_out[...])
            attended[...] = values
            low = (values * norm_rows(values) * gains_ref[1:2]).astype(LOW)
            normed[...] = low
            normed_t[...] = low.T
            total[...] = values
            d_normed[...] = jnp.zeros_like(d_normed)

        def one_chunk(first):
            columns = pl.ds(pl.multiple_of(step * chunk, chunk), chunk)
            if first:
                wait_all(w_gate, sems.at[1])
            gate_w = w_gate[:, :, columns].reshape(width, chunk)
            gate = dot(normed[...], gate_w)
            if first:
                wait_all(w_up, sems.at[2])
            up_w = w_up[:, :, columns].reshape(width, chunk)
            up = dot(normed[...], up_w)
            if first:
                wait_all(w_down, sems.at[3])
            down_w = w_down[columns]
            e = e_ref[...]
            square = gate * gate
            bend = jnp.tanh(0.7978845608 * (gate + 0.044715 * square * gate))
            half_up = 0.5 * (1.0 + bend)
            gelu = gate * half_up
            slope = half_up + 0.5 * gate * (1.0 - bend * bend) * (
                0.7978845608 * (1.0 + 3.0 * 0.044715 * square)
            )
            hidden = (gelu * up).astype(LOW)
            total[...] += dot(hidden, down_w)
            d_hidden = dot_nt(e, down_w)
            d_gate = (d_hidden * up * slope).astype(LOW)
            d_up = (d_hidden * gelu).astype(LOW)
            g_down = dot_tn(hidden, e)
            shards = chunk // down_rows
            if grid.cube:
                c = lax.rem(lax.axis_index("fsdp"), 2)
                g_down = g_down.astype(LOW).reshape(shards // 2, 2, down_rows, width)
                even, odd = g_down[:, 0], g_down[:, 1]
                g_down = [jnp.where(c == 0, even, odd), jnp.where(c == 0, odd, even)]
                lead = pl.ds(step * (shards // 2), shards // 2)
            else:
                g_down = [g_down.astype(LOW).reshape(shards, down_rows, width)]
                lead = pl.ds(step * shards, shards)
            for ref, value in zip(out_grads, g_down):
                for h in range(2):
                    ref[h, lead, rows:] = value[:, :, h * (width // 2) : (h + 1) * (width // 2)]
            everything = (0, slice(None))
            store_grad(grid, in_grads, everything, 0, rows, dot(normed_t[...], d_gate))
            store_grad(grid, in_grads, everything, rows, rows, dot(normed_t[...], d_up))
            d_normed[...] += dot_nt(d_gate, gate_w) + dot_nt(d_up, up_w)

        @pl.when(step == 0)
        def _():
            one_chunk(True)

        @pl.when(step > 0)
        def _():
            one_chunk(False)

        @pl.when(step == steps - 1)
        def _():
            output_ref[...] = jnp.where(seen, total[...], 0.0).astype(LOW)
            values = attended[...]
            back, d_gain = norm_back(values, norm_rows(values), gains_ref[1:2], d_normed[...])
            d_gain_ref[...] = jnp.broadcast_to(d_gain, d_gain_ref.shape)
            d_attended = e_ref[...].astype(WIDE) + back
            d_attended_ref[...] = d_attended
            low = d_attended.astype(LOW)
            d_context_ref[...] = dot_nt(low, w_out[...]).astype(LOW)
            g_out = dot_tn(context_ref[...], low)
            for h in range(2):
                part = g_out[:, h * (width // 2) : (h + 1) * (width // 2)]
                store_grad(grid, out_grads, (h, slice(None)), 0, rows, part)

    vmem = pl.BlockSpec(memory_space=pltpu.VMEM)
    per_half = steps // 2
    out_grads = grad_shapes(grid, rows + down_rows, width)
    in_grads = grad_shapes(grid, 2 * rows, hidden_width)
    block = (1,) + in_grads[0].shape[1:3] + (chunk,)
    in_block = pl.BlockSpec(block, lambda i: (i // per_half, 0, 0, lax.rem(i, per_half)))
    results = pl.pallas_call(
        body,
        grid=(steps,),
        out_shape=[
            jax.ShapeDtypeStruct((length, width), LOW),
            jax.ShapeDtypeStruct((length, width), WIDE),
            jax.ShapeDtypeStruct((length, width), LOW),
            jax.ShapeDtypeStruct((8, width), WIDE),
        ]
        + out_grads
        + in_grads,
        in_specs=[pl.BlockSpec(memory_space=pltpu.SMEM)] + [vmem] * 4 + second.specs + third.specs,
        out_specs=[vmem] * (4 + n_refs) + [in_block] * n_refs,
        scratch_shapes=[
            pltpu.VMEM((width, width), LOW),
            pltpu.VMEM((hidden_width, width), LOW),
            pltpu.VMEM((grid.fsdp, rows, hidden_width), LOW),
            pltpu.VMEM((grid.fsdp, rows, hidden_width), LOW),
            pltpu.VMEM((length, width), WIDE),
            pltpu.VMEM((length, width), LOW),
            pltpu.VMEM((width, length), LOW),
            pltpu.VMEM((length, width), LOW),
            pltpu.VMEM((length, width), WIDE),
            pltpu.VMEM((length, width), WIDE),
            pltpu.SemaphoreType.DMA((4,)),
        ],
        compiler_params=params(56, ("arbitrary",)),
        cost_estimate=cost(28),
        name="feed_forward",
    )(counts, image, context, cotangent, gains, *second.arrays, *third.arrays)
    return results[:4], results[4 : 4 + n_refs], results[4 + n_refs :]


def project_back(grid, source, image, normed, d_qkv, d_attended, gains, d_gain_two):
    length, width = image.shape
    rows = width // grid.fsdp
    count, parts = len(source.arrays), len(d_qkv)
    shapes = grad_shapes(grid, 3 * rows + SLAB, width)

    def body(*refs):
        image_ref, normed_ref, d_attended_ref, gains_ref, d_gain_ref = refs[:5]
        d_refs, refs = refs[5 : 5 + parts], refs[5 + parts :]
        pieces, refs = refs[:count], refs[count:]
        input_grad_ref, grads, (weights, sems) = refs[0], refs[1 : 1 + len(shapes)], refs[-2:]
        for j in range(3):
            start_load(source, pieces, j * rows, rows, weights.at[j], sems.at[j], j)
        normed_t = normed_ref[...].T
        d_parts = [jnp.concatenate([d_ref[j] for d_ref in d_refs], -1) for j in range(3)]
        for j in range(3):
            g = dot(normed_t, d_parts[j])
            for h in range(2):
                part = g[:, h * (width // 2) : (h + 1) * (width // 2)]
                store_grad(grid, grads, (h, slice(None)), j * rows, rows, part)
        d_normed = jnp.zeros((length, width), WIDE)
        for j in range(3):
            wait_all(weights.at[j], sems.at[j])
            d_normed = d_normed + dot_nt(d_parts[j], weights[j])
        values = image_ref[...].astype(WIDE)
        back, d_gain = norm_back(values, norm_rows(values), gains_ref[0:1], d_normed)
        input_grad_ref[...] = (d_attended_ref[...] + back).astype(LOW)
        slab = jnp.concatenate(
            [d_gain, d_gain_ref[0:1], jnp.zeros((SLAB - 2, width), WIDE)], 0
        ).astype(LOW)
        for h in range(2):
            part = slab[:, h * (width // 2) : (h + 1) * (width // 2)]
            for ref in grads:
                ref[h, :, 3 * rows :] = jnp.broadcast_to(part[None], (ref.shape[1],) + part.shape)

    vmem = pl.BlockSpec(memory_space=pltpu.VMEM)
    results = pl.pallas_call(
        body,
        out_shape=[jax.ShapeDtypeStruct((length, width), LOW)] + shapes,
        in_specs=[vmem] * (5 + parts) + source.specs,
        out_specs=[vmem] * (1 + len(shapes)),
        scratch_shapes=[
            pltpu.VMEM((3, width, width), LOW),
            pltpu.SemaphoreType.DMA((3,)),
        ],
        compiler_params=params(12),
        cost_estimate=cost(11),
        name="project_back",
    )(image, normed, d_attended, gains, d_gain_two, *d_qkv, *source.arrays)
    return results[0], results[1:]


def fold_column(reduce):
    grid = reduce.grid
    rows, columns = reduce.keep.shape[2:]
    half = grid.nz // 2

    def body(place_ref, keep_ref, got_ref, *refs):
        total = keep_ref[0, 0].astype(WIDE) + got_ref[0, 0].astype(WIDE)
        for ref in refs[:-1]:
            total = total + ref[0].astype(WIDE)
        refs[-1][0] = total.astype(LOW)

    def level(i, place):
        return place[1] ^ (2 * i + 1)

    block = (1, rows, columns)
    whole = pl.BlockSpec(
        (1,) + block, lambda i, place: (place[0], level(i, place) * 2 + place[2], 0, 0)
    )
    side = pl.BlockSpec(block, lambda i, place: (level(i, place), 0, 0))
    x, z, y, _ = grid.place()
    return pl.pallas_call(
        body,
        grid_spec=pltpu.PrefetchScalarGridSpec(
            num_scalar_prefetch=1,
            grid=(half,),
            in_specs=[whole, whole] + [side] * len(reduce.sides),
            out_specs=pl.BlockSpec(block, lambda i, place: (i, 0, 0)),
        ),
        out_shape=jax.ShapeDtypeStruct((half, rows, columns), LOW),
        compiler_params=params(16, ("arbitrary",)),
        cost_estimate=cost(6e7),
        name="fold_column",
    )(jnp.stack([x, z, y]).astype(jnp.int32), reduce.keep, reduce.got, *reduce.sides)


def adamw(param, first, second, grad, rate, decay):
    first = BETA_ONE * first + (1.0 - BETA_ONE) * grad
    second = BETA_TWO * second + (1.0 - BETA_TWO) * grad * grad
    update = first / (1.0 - BETA_ONE**STEP) / (jnp.sqrt(second / (1.0 - BETA_TWO**STEP)) + ADAM_EPS)
    return (param - rate * (update + decay * param), first, second)


def finish(grid, own, arrive, totals, slab_rows):
    rows, columns = own.shape
    per_shard = 2 * columns // grid.fsdp

    def body(*refs):
        others, refs, (total_ref, sum_ref) = refs[: len(totals)], refs[len(totals) : -2], refs[-2:]
        total = sum(ref[...].astype(WIDE) for ref in refs)
        total = total.astype(LOW)
        total_ref[...] = total
        column = lax.broadcasted_iota(jnp.int32, (rows, columns), 1) + lax.axis_index("dp") * columns
        row = lax.broadcasted_iota(jnp.int32, (rows, columns), 0)
        first = lax.axis_index("fsdp") * per_shard
        mine = jnp.logical_and(column >= first, column < first + per_shard)
        counted = jnp.where(jnp.logical_or(row < rows - slab_rows, mine), total.astype(WIDE), 0.0)
        squared = jnp.sum(counted * counted)
        for ref in others:
            value = ref[...].astype(WIDE)
            squared = squared + jnp.sum(value * value)
        sum_ref[0] = squared

    vmem, smem = (pl.BlockSpec(memory_space=m) for m in (pltpu.VMEM, pltpu.SMEM))
    return pl.pallas_call(
        body,
        out_shape=[jax.ShapeDtypeStruct((rows, columns), LOW), jax.ShapeDtypeStruct((1,), WIDE)],
        in_specs=[vmem] * (1 + len(arrive) + len(totals)),
        out_specs=[vmem, smem],
        compiler_params=params(8),
        cost_estimate=cost(1),
        name="finish",
    )(*totals, own, *arrive)


def update(grid, grad_norm, x, weights, firsts, seconds, grads):
    rows = weights[0].shape[1]
    per_half = grid.fsdp // 2
    columns = weights[0].shape[2] // 2
    rates = (MATRIX_RATE, MATRIX_RATE, MATRIX_RATE, GAIN_RATE)
    decays = (MATRIX_DECAY, MATRIX_DECAY, MATRIX_DECAY, 0.0)

    def body(*refs):
        norm_ref, x_ref = refs[:2]
        weight_refs, first_refs, second_refs = refs[8:12], refs[12:16], refs[16:20]
        outs = refs[20:]
        half = pl.program_id(0)
        factor = jnp.minimum(1.0, CLIP_AT / (norm_ref[0] + 1e-06))
        group_one, group_two, group_three = (
            jnp.where(x_ref[0] == half, mine[...], other[...])
            for mine, other in zip(refs[2:8:2], refs[3:8:2])
        )

        def one(n, index, grad):
            taken = [r[n][index] for r in (weight_refs, first_refs, second_refs)]
            results = adamw(*taken, grad.astype(WIDE) * factor, rates[n], decays[n])
            for k, value in enumerate(results):
                outs[4 * k + n][index] = value

        for j in range(3):
            one(0, j, group_one[j * rows : (j + 1) * rows])
        one(0, 3, group_two[:rows])
        for j in range(2):
            one(1, j, group_three[j * rows : (j + 1) * rows])
        one(2, slice(None), group_two[rows:])
        shard = lax.axis_index("fsdp")

        @pl.when(shard // per_half == half)
        def _():
            shape = (columns, rows)
            place = lax.broadcasted_iota(jnp.int32, shape, 0) - lax.rem(shard, per_half) * rows
            pick = (place == lax.broadcasted_iota(jnp.int32, shape, 1)).astype(WIDE).astype(LOW)
            one(3, slice(None), dot(group_one[3 * rows :], pick)[:2])

    def halves(shape):
        block = shape[:-1] + (shape[-1] // 2,)
        return pl.BlockSpec(block, lambda i: (0,) * (len(shape) - 1) + (i,))

    smem, vmem = (pl.BlockSpec(memory_space=m) for m in (pltpu.SMEM, pltpu.VMEM))
    own = [halves(w.shape) for w in weights[:3]]
    own.append(pl.BlockSpec(weights[3].shape, lambda i: (0, 0)))
    return pl.pallas_call(
        body,
        grid=(2,),
        out_shape=[jax.ShapeDtypeStruct(w.shape, WIDE) for w in weights] * 3,
        in_specs=[smem, smem] + [vmem] * 6 + own * 3,
        out_specs=own * 3,
        compiler_params=params(56, ("arbitrary",)),
        cost_estimate=cost(4),
        name="update",
    )(grad_norm.reshape(1), x.reshape(1), *(v for g in grads for v in g), *weights, *firsts, *seconds)


def squares(v):
    return jnp.sum(jnp.square(v.astype(WIDE)))


def on_device(
    grid,
    patches,
    counts,
    cotangent,
    w_attn,
    w_in,
    w_down,
    gains,
    m_attn,
    m_in,
    m_down,
    m_gains,
    v_attn,
    v_in,
    v_down,
    v_gains,
):
    image, e = patches[0], cotangent[0]
    width = image.shape[1]
    rows, down_rows = w_attn.shape[1], w_down.shape[0]
    shard = lax.axis_index("fsdp")
    low_attn, low_in, low_down, low_gains = (
        w.astype(LOW) for w in (w_attn, w_in, w_down, gains)
    )
    owned = lax.broadcasted_iota(jnp.int32, (1, width), 1) // rows == shard
    slab = jnp.where(owned, jnp.tile(low_gains, (1, grid.fsdp)), jnp.zeros((), LOW))
    slab = jnp.pad(slab, ((0, SLAB - 2), (0, 0)))
    groups = [
        split_columns(g)
        for g in (
            jnp.concatenate([low_attn[0], low_attn[1], low_attn[2], slab], 0),
            jnp.concatenate([low_attn[3], low_down], 0),
        )
    ]
    pairs = width // (2 * HD)
    in_full = lax.all_gather(low_in.reshape(2 * rows, -1), "fsdp")
    in_full = [in_full] if grid.cube else [in_full[:, :rows], in_full[:, rows:]]
    third = Source(grid, in_full, True)

    if grid.cube:
        x = lax.axis_index("dp")
        parts = [lax.dynamic_index_in_dim(g, x, 0, False) for g in groups]
        one, two = Spread(grid, parts[0]), Spread(grid, parts[1])
        one.send_levels()
        one.levels, two.part = after(one.levels, two.part)
        one.load_column()
        one.send_sides()
        two.send_levels()
        (one.side, one.across), two.levels = after((one.side, one.across), two.levels)
        one.send_corners()
        two.load_column()
        two.send_sides()
        one.finish()
        first = Source(grid, one.pieces)
        normed, qkv, full_gains = project_in(grid, first, image, jnp.zeros((SLAB, width), WIDE))
        context = attend(qkv, counts)
        context, two.side, two.across = lax.optimization_barrier((context, two.side, two.across))
        two.send_corners()
        two.finish()
        second = Source(grid, two.pieces)
        second.down_rows = down_rows

        (output, d_attended, d_context, d_gain_two), out_grads, in_grads = feed_forward(
            grid, second, third, image, context, e, counts, full_gains
        )
        three = Reduce(grid, *in_grads)
        three.send_core()
        two_keep, two_sent = out_grads
        two_got = grid.flip_core(two_sent)
        cut = max(1, pairs // 6)
        d_qkv = [attend_back(qkv, d_context, counts, 0, cut)]
        three.got, d_qkv = after(three.got, d_qkv)
        sides = three.load_sides()
        three.send_sides(sides)
        _, (two_got, d_context) = after(sides, (two_got, d_context))
        shape = (2, grid.nz, 2) + two_keep.shape[2:]
        two = Fold(grid, [two_keep.reshape(shape), two_got.reshape(shape)])
        bits = two.by_bits(1)
        x, z, y, c = grid.place()
        leave = two.leave(bits, lax.rem(z, 2))
        leave, d_context = after([leave[0], leave[1]], d_context)
        arrived = [grid.swap_z(v, 1) for v in leave]
        d_qkv.append(attend_back(qkv, d_context, counts, cut, pairs - cut))
        input_grad, grads = project_back(
            grid, first, image, normed, d_qkv, d_attended, full_gains, d_gain_two
        )
        for bit in range(1, bits):
            grads, arrived = after(grads, arrived)
            two.parts.append(jnp.stack(arrived) if bit == 1 else arrived)
            leave, three.sides = after(two.leave(bits - bit, lax.rem(z >> bit, 2)), three.sides)
            arrived = grid.swap_z(leave, 1 << bit)
        one = Reduce(grid, *grads)
        one.send_core()
        leave = fold_column(three)
        in_three = grid.swap_z(leave, 1)
        leave, one.got = after(leave, one.got)
        sides = one.load_sides()
        one.send_sides(sides)
        _, (arrived, in_three) = after(sides, (arrived, in_three))
        two.parts.append(arrived)
        arrived = grid.flip_y(two.leave(1, y))
        rest = [z ^ k for k in range(0, grid.nz, 2)]
        kept = [lax.dynamic_index_in_dim(three.split(v), x, 0, False) for v in (three.keep, three.got)]
        kept = [lax.dynamic_index_in_dim(v, y, 1, False) for v in kept] + three.sides
        kept = [jnp.stack([lax.dynamic_index_in_dim(v, k, 0, False) for k in rest]) for v in kept]
        three = Fold(grid, kept + [in_three])
        bits = three.by_bits(0)
        for bit in range(1, bits + 1):
            in_three = grid.swap_z(three.leave(bits - bit, 0), 1 << bit)
            three.parts.append(in_three)
        one.load_levels()
        one.send_levels()
        _, arrived = after(one.leave, arrived)
        two.parts.append(arrived)
        leave = two.leave(0, x)
        arrived = grid.flip_x(leave)
        two.parts.append(arrived)
        _, in_three = after(leave, in_three)
        three.parts[-1] = in_three
        three.total = three.total()
        three.other = grid.flip_x(three.total)
        two.total = two.total()
        two.other = grid.flip_x(two.total)
        totals = (three.total, two.total)
        one.total, squared = finish(grid, one.own, one.arrive, totals, SLAB)
        one.send_total()
        grad_norm = jnp.sqrt(total_of(grid, squared[0]))
        reduced = [(g.total, g.other) for g in (one, two, three)]
    else:
        groups = [lax.all_gather(g, "fsdp", axis=1) for g in groups]

        def whole(full, low, n):
            full = full[:, :, low : low + n].reshape(2, grid.fsdp * n, full.shape[3])
            return jnp.concatenate([full[0], full[1]], -1)

        slabs = jnp.sum(groups[0][:, :, 3 * rows :].astype(WIDE), 1)
        first = Source(grid, [whole(groups[0], j * rows, rows) for j in range(3)], True)
        second = Source(
            grid, [whole(groups[1], 0, rows), whole(groups[1], rows, down_rows)], True
        )
        second.down_rows = down_rows
        normed, qkv, full_gains = project_in(
            grid, first, image, jnp.concatenate([slabs[0], slabs[1]], -1)
        )
        context = attend(qkv, counts)
        (output, d_attended, d_context, d_gain_two), out_grads, in_grads = feed_forward(
            grid, second, third, image, context, e, counts, full_gains
        )
        d_qkv = [attend_back(qkv, d_context, counts, 0, pairs)]
        input_grad, grads = project_back(
            grid, first, image, normed, d_qkv, d_attended, full_gains, d_gain_two
        )

        reduced = []
        for (g,) in (grads, out_grads, in_grads):
            total = lax.psum_scatter(g.astype(WIDE), "fsdp", scatter_dimension=1)
            reduced.append(lax.psum(total.astype(LOW), "dp"))
        x = jnp.int32(0)
        mine = owned.reshape(2, 1, width // 2)
        slabs = jnp.where(mine, reduced[0][:, 3 * rows :], jnp.zeros((), LOW))
        squared = squares(reduced[0][:, : 3 * rows]) + squares(slabs)
        squared = squared + squares(reduced[1]) + squares(reduced[2])
        grad_norm = jnp.sqrt(total_of(grid, squared))

    updated = update(
        grid,
        grad_norm,
        x,
        (w_attn, w_in, w_down, gains),
        (m_attn, m_in, m_down, m_gains),
        (v_attn, v_in, v_down, v_gains),
        reduced,
    )
    return (output[None], input_grad[None], grad_norm, *updated)


def solution(mesh):
    placed = (
        P(("dp", "fsdp"), None, None),
        P(("dp", "fsdp")),
        P(("dp", "fsdp"), None, None),
        P(None, "fsdp", None),
        P(None, "fsdp", None),
        P("fsdp", None),
        P(None, "fsdp"),
        P(None, "fsdp", None),
        P(None, "fsdp", None),
        P("fsdp", None),
        P(None, "fsdp"),
        P(None, "fsdp", None),
        P(None, "fsdp", None),
        P("fsdp", None),
        P(None, "fsdp"),
    )
    grid = Grid(mesh.shape["dp"], mesh.shape["fsdp"])
    return jax.shard_map(
        functools.partial(on_device, grid),
        mesh=mesh,
        in_specs=placed,
        out_specs=(
            P(("dp", "fsdp"), None, None),
            P(("dp", "fsdp"), None, None),
            P(),
            P(None, "fsdp", None),
            P(None, "fsdp", None),
            P("fsdp", None),
            P(None, "fsdp"),
            P(None, "fsdp", None),
            P(None, "fsdp", None),
            P("fsdp", None),
            P(None, "fsdp"),
            P(None, "fsdp", None),
            P(None, "fsdp", None),
            P("fsdp", None),
            P(None, "fsdp"),
        ),
        check_vma=False,
    )
```

```python
import functools
import math

import jax
import jax.numpy as jnp
from jax import lax
from jax.experimental import pallas as pl
from jax.experimental.pallas import tpu as pltpu
from jax.sharding import PartitionSpec as P

HD = 64
STEP = 10


NORM_EPS = 1e-06
MASKED = -1000000000.0
BETA_ONE = 0.9
BETA_TWO = 0.999
ADAM_EPS = 1e-08
CLIP_AT = 1.0
MATRIX_RATE = 0.04
MATRIX_DECAY = 0.1
GAIN_RATE = 0.8

EVERY = ("dp", "fsdp")
LOW = jnp.bfloat16
WIDE = jnp.float32
SLAB = 16
MIB = 1024 * 1024
ANYWHERE = pl.BlockSpec(memory_space=pl.ANY)


class Grid:
    def __init__(self, dp, fsdp):
        self.dp, self.fsdp = dp, fsdp
        self.nz = fsdp // 4
        power = self.nz & (self.nz - 1) == 0
        self.cube = dp == 2 and fsdp % 4 == 0 and self.nz % 2 == 0 and power

    def move(self, step):
        pairs = []
        for source in range(self.dp * self.fsdp):
            x, rest = divmod(source, self.fsdp)
            z, rest = divmod(rest, 4)
            y, core = divmod(rest, 2)
            x, z, y, core = step(x, z, y, core)
            pairs.append((source, x * self.fsdp + (z * 2 + y) * 2 + core))
        return pairs

    def flip_x(self, v):
        return lax.ppermute(v, EVERY, self.move(lambda x, z, y, c: (1 - x, z, y, c)))

    def flip_y(self, v):
        return lax.ppermute(v, EVERY, self.move(lambda x, z, y, c: (x, z, 1 - y, c)))

    def flip_xy(self, v):
        return lax.ppermute(v, EVERY, self.move(lambda x, z, y, c: (1 - x, z, 1 - y, c)))

    def flip_core(self, v):
        return lax.ppermute(v, EVERY, self.move(lambda x, z, y, c: (x, z, y, 1 - c)))

    def swap_z(self, v, bit):
        return lax.ppermute(v, EVERY, self.move(lambda x, z, y, c: (x, z ^ bit, y, c)))

    def place(self):
        x, f = lax.axis_index("dp"), lax.axis_index("fsdp")
        return x, f // 4, lax.rem(f // 2, 2), lax.rem(f, 2)


def after(first, then):
    return lax.optimization_barrier((first, then))


class Spread:
    def __init__(self, grid, part):
        self.grid, self.part = grid, part

    def send_levels(self):
        self.levels = [self.grid.swap_z(self.part, k) for k in range(1, self.grid.nz)]

    def load_column(self):
        self.column = jnp.stack([self.part] + self.levels)

    def send_sides(self):
        self.side = self.grid.flip_x(self.column)
        self.across = self.grid.flip_y(self.column)

    def send_corners(self):
        self.corner = self.grid.flip_x(self.across)
        self.most = jnp.concatenate([self.column, self.side, self.across])
        self.other_most = self.grid.flip_core(self.most)

    def finish(self):
        self.other_rest = self.grid.flip_core(self.corner)

    @property
    def pieces(self):
        return [self.most, self.corner, self.other_most, self.other_rest]


def piece_places(grid):
    nz = grid.nz
    most = [(x, y, level) for x, y in ((0, 0), (1, 0), (0, 1)) for level in range(nz)]
    rest = [(1, 1, level) for level in range(nz)]
    return [[(x, y, core, n) for x, y, n in spots] for core in (0, 1) for spots in (most, rest)]


class Reduce:
    def __init__(self, grid, keep, sent):
        self.grid, self.keep, self.sent = grid, keep, sent

    def send_core(self):
        self.got = self.grid.flip_core(self.sent)

    def split(self, array):
        return array.reshape((2, self.grid.nz, 2) + array.shape[2:])

    def block(self, h, at_y):
        total = 0.0
        for array in (self.keep, self.got):
            array = array.reshape((2, self.grid.nz, 2) + array.shape[2:])
            part = lax.dynamic_index_in_dim(array, h, 0, False)
            total = total + lax.dynamic_index_in_dim(part, at_y, 1, False).astype(WIDE)
        return total

    def load_sides(self):
        x, z, y, c = self.grid.place()
        places = ((1 - x, y), (x, 1 - y), (1 - x, 1 - y))
        return [self.block(h, at_y).astype(LOW) for h, at_y in places]

    def send_sides(self, sides):
        sends = (self.grid.flip_x, self.grid.flip_y, self.grid.flip_xy)
        self.sides = [send(v) for send, v in zip(sends, sides)]

    def load_levels(self):
        x, z, y, c = self.grid.place()
        column = self.block(x, y) + sum(v.astype(WIDE) for v in self.sides)
        column = column.astype(LOW)
        self.own = lax.dynamic_index_in_dim(column, z, 0, False)
        self.leave = [
            lax.dynamic_index_in_dim(column, z ^ k, 0, False) for k in range(1, self.grid.nz)
        ]

    def send_levels(self):
        self.arrive = [self.grid.swap_z(v, k) for k, v in enumerate(self.leave, 1)]

    def load_total(self):
        self.total = sum((v.astype(WIDE) for v in self.arrive), self.own.astype(WIDE)).astype(LOW)

    def send_total(self):
        self.other = self.grid.flip_x(self.total)


class Fold:
    def __init__(self, grid, parts):
        self.grid, self.parts = grid, parts

    def by_bits(self, dim):
        count = self.parts[0].shape[dim].bit_length() - 1
        self.parts = [v.reshape(v.shape[:dim] + (2,) * count + v.shape[dim + 1 :]) for v in self.parts]
        return count

    def leave(self, dim, mine):
        leave = sum(lax.dynamic_index_in_dim(v, 1 - mine, dim, False).astype(WIDE) for v in self.parts)
        self.parts = [lax.dynamic_index_in_dim(v, mine, dim, False) for v in self.parts]
        return leave.astype(LOW)

    def total(self):
        return sum(v.astype(WIDE) for v in self.parts).astype(LOW)


def total_of(grid, value):
    if not grid.cube:
        return lax.psum(value, "fsdp")
    value = value + grid.flip_core(value)
    value = value + grid.flip_x(value)
    value = value + grid.flip_y(value)
    bit = 1
    while bit < grid.nz:
        value = value + grid.swap_z(value, bit)
        bit *= 2
    return value


def split_columns(v):
    return jnp.stack(jnp.split(v, 2, -1))


def params(mib, semantics=None):
    return pltpu.CompilerParams(vmem_limit_bytes=mib * MIB, dimension_semantics=semantics)


def cost(microseconds):
    return pl.CostEstimate(flops=int(microseconds * 1e6), bytes_accessed=0, transcendentals=0)


def dot(a, b):
    return jnp.dot(a, b, preferred_element_type=WIDE)


def dot_nt(a, b):
    return lax.dot_general(a, b, (((1,), (1,)), ((), ())), preferred_element_type=WIDE)


def dot_tn(a, b):
    return lax.dot_general(a, b, (((0,), (0,)), ((), ())), preferred_element_type=WIDE)


class Source:
    def __init__(self, grid, arrays, whole=False):
        self.grid, self.arrays, self.whole = grid, arrays, whole
        self.specs = [ANYWHERE] * len(arrays)

    def copy(self, refs, low, rows, target, sem):
        grid = self.grid
        x, z, y, c = grid.place()
        for ref, spots in zip(refs, piece_places(grid)):
            for entry, (dx, dy, dc, level) in enumerate(spots):
                half = lax.rem(x + dx, 2)
                shard = ((z ^ level) * 2 + lax.rem(y + dy, 2)) * 2 + lax.rem(c + dc, 2)
                source = ref.at[entry, pl.ds(low, rows)]
                pltpu.make_async_copy(source, target(half, shard), sem).start()


def wait_all(ref, sem):
    pltpu.make_async_copy(ref, ref, sem).wait()


def shard_target(matrix, rows):
    n = matrix.shape[-1] // 2

    def target(half, shard):
        return matrix.at[
            pl.ds(pl.multiple_of(shard * rows, 16), rows), pl.ds(pl.multiple_of(half * n, 128), n)
        ]

    return target


def start_load(source, refs, low, rows, matrix, sem, whole=0):
    if not source.whole:
        source.copy(refs, low, rows, shard_target(matrix, rows), sem)
    else:
        pltpu.make_async_copy(refs[whole], matrix, sem).start()


def load_rows(grid, refs, which, low, target, sem):
    source = refs[0].at[:, pl.ds(low, target.shape[1])] if grid.cube else refs[which]
    pltpu.make_async_copy(source, target, sem).start()


def store_grad(grid, refs, index, low, rows, value):
    lead, columns = index
    if not grid.cube:
        refs[0][lead, :, low : low + rows, columns] = value.astype(LOW).reshape(grid.fsdp, rows, -1)
        return
    c = lax.rem(lax.axis_index("fsdp"), 2)
    value = value.astype(LOW).reshape(grid.fsdp // 2, 2, rows, value.shape[-1])
    even, odd = value[:, 0], value[:, 1]
    refs[0][lead, :, low : low + rows, columns] = jnp.where(c == 0, even, odd)
    refs[1][lead, :, low : low + rows, columns] = jnp.where(c == 0, odd, even)


def grad_shapes(grid, rows, columns):
    if not grid.cube:
        return [jax.ShapeDtypeStruct((2, grid.fsdp, rows, columns // 2), LOW)]
    return [jax.ShapeDtypeStruct((2, grid.fsdp // 2, rows, columns // 2), LOW)] * 2


def norm_rows(values):
    return lax.rsqrt(jnp.mean(values * values, -1, keepdims=True) + NORM_EPS)


def norm_back(values, scale, gain, grad):
    y = values * scale
    c = grad * gain
    back = scale * (c - y * jnp.mean(c * y, -1, keepdims=True))
    return back, jnp.sum(grad * y, 0, keepdims=True)


def project_in(grid, source, image, gains):
    length, width = image.shape
    rows = width // grid.fsdp
    count = len(source.arrays)

    def body(*refs):
        image_ref, gains_ref, pieces = refs[0], refs[1], refs[2 : 2 + count]
        normed_ref, qkv_ref, gains_out, weights, slabs, sems = refs[2 + count :]
        for j in range(3):
            start_load(source, pieces, j * rows, rows, weights.at[j], sems.at[j], j)
        if grid.cube:
            source.copy(pieces, 3 * rows, SLAB, lambda h, f: slabs.at[h, f], sems.at[3])
        values = image_ref[...].astype(WIDE)
        scaled = values * norm_rows(values)
        if grid.cube:
            wait_all(slabs, sems.at[3])
            found = jnp.sum(slabs[...].astype(WIDE), 1)
            gain = jnp.concatenate([found[0], found[1]], -1)
        else:
            gain = gains_ref[...].astype(WIDE)
        gains_out[...] = gain
        normed = (scaled * gain[0:1]).astype(LOW)
        normed_ref[...] = normed
        for j in range(3):
            wait_all(weights.at[j], sems.at[j])
            qkv_ref[j] = dot(normed, weights[j]).astype(LOW)

    vmem = pl.BlockSpec(memory_space=pltpu.VMEM)
    return pl.pallas_call(
        body,
        out_shape=[
            jax.ShapeDtypeStruct((length, width), LOW),
            jax.ShapeDtypeStruct((3, length, width), LOW),
            jax.ShapeDtypeStruct((SLAB, width), WIDE),
        ],
        in_specs=[vmem, vmem] + source.specs,
        out_specs=[vmem] * 3,
        scratch_shapes=[
            pltpu.VMEM((3, width, width), LOW),
            pltpu.VMEM((2, grid.fsdp, SLAB, width // 2), LOW),
            pltpu.SemaphoreType.DMA((4,)),
        ],
        compiler_params=params(12),
        cost_estimate=cost(8),
        name="project_in",
    )(image, gains, *source.arrays)


def attend(qkv, counts):
    length, width = qkv.shape[1:]
    pair = 2 * HD

    def body(counts_ref, qkv_ref, context_ref):
        seen = lax.broadcasted_iota(jnp.int32, (1, length), 1) < counts_ref[0]
        first = lax.broadcasted_iota(jnp.int32, (1, pair), 1) < HD
        q, k, v = qkv_ref[0], qkv_ref[1], qkv_ref[2]
        found = []
        for head in range(2):
            own = first if head == 0 else jnp.logical_not(first)
            scores = dot_nt(jnp.where(own, q, jnp.zeros_like(q)), k)
            scores = jnp.where(seen, scores, MASKED)
            probs = jnp.exp(scores - jnp.max(scores, -1, keepdims=True))
            summed = dot(probs.astype(LOW), jnp.where(own, v, jnp.ones_like(v)))
            found.append(summed / pltpu.roll(summed, HD, 1))
        context_ref[...] = jnp.where(first, found[0], found[1]).astype(LOW)

    return pl.pallas_call(
        body,
        grid=(width // pair,),
        out_shape=jax.ShapeDtypeStruct((length, width), LOW),
        in_specs=[
            pl.BlockSpec(memory_space=pltpu.SMEM),
            pl.BlockSpec((3, length, pair), lambda i: (0, 0, i)),
        ],
        out_specs=pl.BlockSpec((length, pair), lambda i: (0, i)),
        compiler_params=params(8, ("arbitrary",)),
        cost_estimate=cost(9),
        name="attend",
    )(counts, qkv)


def attend_back(qkv, d_context, counts, low, steps):
    length = qkv.shape[1]
    pair = 2 * HD
    width = steps * pair

    def body(counts_ref, qkv_ref, d_ref, out_ref):
        seen = lax.broadcasted_iota(jnp.int32, (length, 1), 0) < counts_ref[0]
        first = lax.broadcasted_iota(jnp.int32, (1, pair), 1) < HD
        q, k, v, d = qkv_ref[0], qkv_ref[1], qkv_ref[2], d_ref[...]
        found = []
        for head in range(2):
            own = first if head == 0 else jnp.logical_not(first)
            scores = dot_nt(k, jnp.where(own, q, jnp.zeros_like(q)))
            scores = jnp.where(seen, scores, MASKED)
            probs = jnp.exp(scores - jnp.max(scores, 0, keepdims=True))
            probs = probs * (1.0 / jnp.sum(probs, 0, keepdims=True))
            d_probs = dot_nt(v, jnp.where(own, d, jnp.zeros_like(d)))
            weighed = probs * d_probs
            d_scores = (weighed - probs * jnp.sum(weighed, 0, keepdims=True)).astype(LOW)
            found.append((dot_tn(d_scores, k), dot(d_scores, q), dot(probs.astype(LOW), d)))
        for j in range(3):
            out_ref[j] = jnp.where(first, found[0][j], found[1][j]).astype(LOW)

    return pl.pallas_call(
        body,
        grid=(width // pair,),
        out_shape=jax.ShapeDtypeStruct((3, length, width), LOW),
        in_specs=[
            pl.BlockSpec(memory_space=pltpu.SMEM),
            pl.BlockSpec((3, length, pair), lambda i: (0, 0, low + i)),
            pl.BlockSpec((length, pair), lambda i: (0, low + i)),
        ],
        out_specs=pl.BlockSpec((3, length, pair), lambda i: (0, 0, i)),
        compiler_params=params(8, ("arbitrary",)),
        cost_estimate=cost(2.3 * steps + 2),
        name="attend_back",
    )(counts, qkv, d_context)


def feed_forward(grid, second, third, image, context, cotangent, counts, gains):
    length, width = image.shape
    rows = width // grid.fsdp
    down_rows = second.down_rows
    hidden_width = down_rows * grid.fsdp
    steps = 4
    chunk = hidden_width // steps
    n_second, n_third = len(second.arrays), len(third.arrays)
    n_refs = len(grad_shapes(grid, rows, width))

    def body(*refs):
        counts_ref, image_ref, context_ref, cotangent_ref, gains_ref = refs[:5]
        seconds, refs = refs[5 : 5 + n_second], refs[5 + n_second :]
        thirds, refs = refs[:n_third], refs[n_third:]
        output_ref, d_attended_ref, d_context_ref, d_gain_ref = refs[:4]
        out_grads, refs = refs[4 : 4 + n_refs], refs[4 + n_refs :]
        in_grads, refs = refs[:n_refs], refs[n_refs:]
        w_out, w_down, w_gate, w_up, attended, normed, normed_t, e_ref, total, d_normed, sems = refs
        step = pl.program_id(0)
        seen = lax.broadcasted_iota(jnp.int32, (length, 1), 0) < counts_ref[0]

        @pl.when(step == 0)
        def _():
            start_load(second, seconds, 0, rows, w_out, sems.at[0], 0)
            load_rows(grid, thirds, 0, 0, w_gate, sems.at[1])
            load_rows(grid, thirds, 1, rows, w_up, sems.at[2])
            start_load(second, seconds, rows, down_rows, w_down, sems.at[3], 1)
            e = cotangent_ref[...]
            e_ref[...] = jnp.where(seen, e, jnp.zeros_like(e))
            wait_all(w_out, sems.at[0])
            values = image_ref[...].astype(WIDE) + dot(context_ref[...], w_out[...])
            attended[...] = values
            low = (values * norm_rows(values) * gains_ref[1:2]).astype(LOW)
            normed[...] = low
            normed_t[...] = low.T
            total[...] = values
            d_normed[...] = jnp.zeros_like(d_normed)

        def one_chunk(first):
            columns = pl.ds(pl.multiple_of(step * chunk, chunk), chunk)
            if first:
                wait_all(w_gate, sems.at[1])
            gate_w = w_gate[:, :, columns].reshape(width, chunk)
            gate = dot(normed[...], gate_w)
            if first:
                wait_all(w_up, sems.at[2])
            up_w = w_up[:, :, columns].reshape(width, chunk)
            up = dot(normed[...], up_w)
            if first:
                wait_all(w_down, sems.at[3])
            down_w = w_down[columns]
            e = e_ref[...]
            square = gate * gate
            bend = jnp.tanh(0.7978845608 * (gate + 0.044715 * square * gate))
            half_up = 0.5 * (1.0 + bend)
            gelu = gate * half_up
            slope = half_up + 0.5 * gate * (1.0 - bend * bend) * (
                0.7978845608 * (1.0 + 3.0 * 0.044715 * square)
            )
            hidden = (gelu * up).astype(LOW)
            total[...] += dot(hidden, down_w)
            d_hidden = dot_nt(e, down_w)
            d_gate = (d_hidden * up * slope).astype(LOW)
            d_up = (d_hidden * gelu).astype(LOW)
            g_down = dot_tn(hidden, e)
            shards = chunk // down_rows
            if grid.cube:
                c = lax.rem(lax.axis_index("fsdp"), 2)
                g_down = g_down.astype(LOW).reshape(shards // 2, 2, down_rows, width)
                even, odd = g_down[:, 0], g_down[:, 1]
                g_down = [jnp.where(c == 0, even, odd), jnp.where(c == 0, odd, even)]
                lead = pl.ds(step * (shards // 2), shards // 2)
            else:
                g_down = [g_down.astype(LOW).reshape(shards, down_rows, width)]
                lead = pl.ds(step * shards, shards)
            for ref, value in zip(out_grads, g_down):
                for h in range(2):
                    ref[h, lead, rows:] = value[:, :, h * (width // 2) : (h + 1) * (width // 2)]
            everything = (0, slice(None))
            store_grad(grid, in_grads, everything, 0, rows, dot(normed_t[...], d_gate))
            store_grad(grid, in_grads, everything, rows, rows, dot(normed_t[...], d_up))
            d_normed[...] += dot_nt(d_gate, gate_w) + dot_nt(d_up, up_w)

        @pl.when(step == 0)
        def _():
            one_chunk(True)

        @pl.when(step > 0)
        def _():
            one_chunk(False)

        @pl.when(step == steps - 1)
        def _():
            output_ref[...] = jnp.where(seen, total[...], 0.0).astype(LOW)
            values = attended[...]
            back, d_gain = norm_back(values, norm_rows(values), gains_ref[1:2], d_normed[...])
            d_gain_ref[...] = jnp.broadcast_to(d_gain, d_gain_ref.shape)
            d_attended = e_ref[...].astype(WIDE) + back
            d_attended_ref[...] = d_attended
            low = d_attended.astype(LOW)
            d_context_ref[...] = dot_nt(low, w_out[...]).astype(LOW)
            g_out = dot_tn(context_ref[...], low)
            for h in range(2):
                part = g_out[:, h * (width // 2) : (h + 1) * (width // 2)]
                store_grad(grid, out_grads, (h, slice(None)), 0, rows, part)

    vmem = pl.BlockSpec(memory_space=pltpu.VMEM)
    per_half = steps // 2
    out_grads = grad_shapes(grid, rows + down_rows, width)
    in_grads = grad_shapes(grid, 2 * rows, hidden_width)
    block = (1,) + in_grads[0].shape[1:3] + (chunk,)
    in_block = pl.BlockSpec(block, lambda i: (i // per_half, 0, 0, lax.rem(i, per_half)))
    results = pl.pallas_call(
        body,
        grid=(steps,),
        out_shape=[
            jax.ShapeDtypeStruct((length, width), LOW),
            jax.ShapeDtypeStruct((length, width), WIDE),
            jax.ShapeDtypeStruct((length, width), LOW),
            jax.ShapeDtypeStruct((8, width), WIDE),
        ]
        + out_grads
        + in_grads,
        in_specs=[pl.BlockSpec(memory_space=pltpu.SMEM)] + [vmem] * 4 + second.specs + third.specs,
        out_specs=[vmem] * (4 + n_refs) + [in_block] * n_refs,
        scratch_shapes=[
            pltpu.VMEM((width, width), LOW),
            pltpu.VMEM((hidden_width, width), LOW),
            pltpu.VMEM((grid.fsdp, rows, hidden_width), LOW),
            pltpu.VMEM((grid.fsdp, rows, hidden_width), LOW),
            pltpu.VMEM((length, width), WIDE),
            pltpu.VMEM((length, width), LOW),
            pltpu.VMEM((width, length), LOW),
            pltpu.VMEM((length, width), LOW),
            pltpu.VMEM((length, width), WIDE),
            pltpu.VMEM((length, width), WIDE),
            pltpu.SemaphoreType.DMA((4,)),
        ],
        compiler_params=params(56, ("arbitrary",)),
        cost_estimate=cost(28),
        name="feed_forward",
    )(counts, image, context, cotangent, gains, *second.arrays, *third.arrays)
    return results[:4], results[4 : 4 + n_refs], results[4 + n_refs :]


def project_back(grid, source, image, normed, d_qkv, d_attended, gains, d_gain_two):
    length, width = image.shape
    rows = width // grid.fsdp
    count, parts = len(source.arrays), len(d_qkv)
    shapes = grad_shapes(grid, 3 * rows + SLAB, width)

    def body(*refs):
        image_ref, normed_ref, d_attended_ref, gains_ref, d_gain_ref = refs[:5]
        d_refs, refs = refs[5 : 5 + parts], refs[5 + parts :]
        pieces, refs = refs[:count], refs[count:]
        input_grad_ref, grads, (weights, sems) = refs[0], refs[1 : 1 + len(shapes)], refs[-2:]
        for j in range(3):
            start_load(source, pieces, j * rows, rows, weights.at[j], sems.at[j], j)
        normed_t = normed_ref[...].T
        d_parts = [jnp.concatenate([d_ref[j] for d_ref in d_refs], -1) for j in range(3)]
        for j in range(3):
            g = dot(normed_t, d_parts[j])
            for h in range(2):
                part = g[:, h * (width // 2) : (h + 1) * (width // 2)]
                store_grad(grid, grads, (h, slice(None)), j * rows, rows, part)
        d_normed = jnp.zeros((length, width), WIDE)
        for j in range(3):
            wait_all(weights.at[j], sems.at[j])
            d_normed = d_normed + dot_nt(d_parts[j], weights[j])
        values = image_ref[...].astype(WIDE)
        back, d_gain = norm_back(values, norm_rows(values), gains_ref[0:1], d_normed)
        input_grad_ref[...] = (d_attended_ref[...] + back).astype(LOW)
        slab = jnp.concatenate(
            [d_gain, d_gain_ref[0:1], jnp.zeros((SLAB - 2, width), WIDE)], 0
        ).astype(LOW)
        for h in range(2):
            part = slab[:, h * (width // 2) : (h + 1) * (width // 2)]
            for ref in grads:
                ref[h, :, 3 * rows :] = jnp.broadcast_to(part[None], (ref.shape[1],) + part.shape)

    vmem = pl.BlockSpec(memory_space=pltpu.VMEM)
    results = pl.pallas_call(
        body,
        out_shape=[jax.ShapeDtypeStruct((length, width), LOW)] + shapes,
        in_specs=[vmem] * (5 + parts) + source.specs,
        out_specs=[vmem] * (1 + len(shapes)),
        scratch_shapes=[
            pltpu.VMEM((3, width, width), LOW),
            pltpu.SemaphoreType.DMA((3,)),
        ],
        compiler_params=params(12),
        cost_estimate=cost(11),
        name="project_back",
    )(image, normed, d_attended, gains, d_gain_two, *d_qkv, *source.arrays)
    return results[0], results[1:]


def fold_column(reduce):
    grid = reduce.grid
    rows, columns = reduce.keep.shape[2:]
    half = grid.nz // 2

    def body(place_ref, keep_ref, got_ref, *refs):
        total = keep_ref[0, 0].astype(WIDE) + got_ref[0, 0].astype(WIDE)
        for ref in refs[:-1]:
            total = total + ref[0].astype(WIDE)
        refs[-1][0] = total.astype(LOW)

    def level(i, place):
        return place[1] ^ (2 * i + 1)

    block = (1, rows, columns)
    whole = pl.BlockSpec(
        (1,) + block, lambda i, place: (place[0], level(i, place) * 2 + place[2], 0, 0)
    )
    side = pl.BlockSpec(block, lambda i, place: (level(i, place), 0, 0))
    x, z, y, _ = grid.place()
    return pl.pallas_call(
        body,
        grid_spec=pltpu.PrefetchScalarGridSpec(
            num_scalar_prefetch=1,
            grid=(half,),
            in_specs=[whole, whole] + [side] * len(reduce.sides),
            out_specs=pl.BlockSpec(block, lambda i, place: (i, 0, 0)),
        ),
        out_shape=jax.ShapeDtypeStruct((half, rows, columns), LOW),
        compiler_params=params(16, ("arbitrary",)),
        cost_estimate=cost(6e7),
        name="fold_column",
    )(jnp.stack([x, z, y]).astype(jnp.int32), reduce.keep, reduce.got, *reduce.sides)


def adamw(param, first, second, grad, rate, decay):
    first = BETA_ONE * first + (1.0 - BETA_ONE) * grad
    second = BETA_TWO * second + (1.0 - BETA_TWO) * grad * grad
    update = first / (1.0 - BETA_ONE**STEP) / (jnp.sqrt(second / (1.0 - BETA_TWO**STEP)) + ADAM_EPS)
    return (param - rate * (update + decay * param), first, second)


def finish(grid, own, arrive, totals, slab_rows):
    rows, columns = own.shape
    per_shard = 2 * columns // grid.fsdp

    def body(*refs):
        others, refs, (total_ref, sum_ref) = refs[: len(totals)], refs[len(totals) : -2], refs[-2:]
        total = sum(ref[...].astype(WIDE) for ref in refs)
        total = total.astype(LOW)
        total_ref[...] = total
        column = lax.broadcasted_iota(jnp.int32, (rows, columns), 1) + lax.axis_index("dp") * columns
        row = lax.broadcasted_iota(jnp.int32, (rows, columns), 0)
        first = lax.axis_index("fsdp") * per_shard
        mine = jnp.logical_and(column >= first, column < first + per_shard)
        counted = jnp.where(jnp.logical_or(row < rows - slab_rows, mine), total.astype(WIDE), 0.0)
        squared = jnp.sum(counted * counted)
        for ref in others:
            value = ref[...].astype(WIDE)
            squared = squared + jnp.sum(value * value)
        sum_ref[0] = squared

    vmem, smem = (pl.BlockSpec(memory_space=m) for m in (pltpu.VMEM, pltpu.SMEM))
    return pl.pallas_call(
        body,
        out_shape=[jax.ShapeDtypeStruct((rows, columns), LOW), jax.ShapeDtypeStruct((1,), WIDE)],
        in_specs=[vmem] * (1 + len(arrive) + len(totals)),
        out_specs=[vmem, smem],
        compiler_params=params(8),
        cost_estimate=cost(1),
        name="finish",
    )(*totals, own, *arrive)


def update(grid, grad_norm, x, weights, firsts, seconds, grads):
    rows = weights[0].shape[1]
    per_half = grid.fsdp // 2
    columns = weights[0].shape[2] // 2
    rates = (MATRIX_RATE, MATRIX_RATE, MATRIX_RATE, GAIN_RATE)
    decays = (MATRIX_DECAY, MATRIX_DECAY, MATRIX_DECAY, 0.0)

    def body(*refs):
        norm_ref, x_ref = refs[:2]
        weight_refs, first_refs, second_refs = refs[8:12], refs[12:16], refs[16:20]
        outs = refs[20:]
        half = pl.program_id(0)
        factor = jnp.minimum(1.0, CLIP_AT / (norm_ref[0] + 1e-06))
        group_one, group_two, group_three = (
            jnp.where(x_ref[0] == half, mine[...], other[...])
            for mine, other in zip(refs[2:8:2], refs[3:8:2])
        )

        def one(n, index, grad):
            taken = [r[n][index] for r in (weight_refs, first_refs, second_refs)]
            results = adamw(*taken, grad.astype(WIDE) * factor, rates[n], decays[n])
            for k, value in enumerate(results):
                outs[4 * k + n][index] = value

        for j in range(3):
            one(0, j, group_one[j * rows : (j + 1) * rows])
        one(0, 3, group_two[:rows])
        for j in range(2):
            one(1, j, group_three[j * rows : (j + 1) * rows])
        one(2, slice(None), group_two[rows:])
        shard = lax.axis_index("fsdp")

        @pl.when(shard // per_half == half)
        def _():
            shape = (columns, rows)
            place = lax.broadcasted_iota(jnp.int32, shape, 0) - lax.rem(shard, per_half) * rows
            pick = (place == lax.broadcasted_iota(jnp.int32, shape, 1)).astype(WIDE).astype(LOW)
            one(3, slice(None), dot(group_one[3 * rows :], pick)[:2])

    def halves(shape):
        block = shape[:-1] + (shape[-1] // 2,)
        return pl.BlockSpec(block, lambda i: (0,) * (len(shape) - 1) + (i,))

    smem, vmem = (pl.BlockSpec(memory_space=m) for m in (pltpu.SMEM, pltpu.VMEM))
    own = [halves(w.shape) for w in weights[:3]]
    own.append(pl.BlockSpec(weights[3].shape, lambda i: (0, 0)))
    return pl.pallas_call(
        body,
        grid=(2,),
        out_shape=[jax.ShapeDtypeStruct(w.shape, WIDE) for w in weights] * 3,
        in_specs=[smem, smem] + [vmem] * 6 + own * 3,
        out_specs=own * 3,
        compiler_params=params(56, ("arbitrary",)),
        cost_estimate=cost(4),
        name="update",
    )(grad_norm.reshape(1), x.reshape(1), *(v for g in grads for v in g), *weights, *firsts, *seconds)


def squares(v):
    return jnp.sum(jnp.square(v.astype(WIDE)))


def on_device(
    grid,
    patches,
    counts,
    cotangent,
    w_attn,
    w_in,
    w_down,
    gains,
    m_attn,
    m_in,
    m_down,
    m_gains,
    v_attn,
    v_in,
    v_down,
    v_gains,
):
    image, e = patches[0], cotangent[0]
    width = image.shape[1]
    rows, down_rows = w_attn.shape[1], w_down.shape[0]
    shard = lax.axis_index("fsdp")
    low_attn, low_in, low_down, low_gains = (
        w.astype(LOW) for w in (w_attn, w_in, w_down, gains)
    )
    owned = lax.broadcasted_iota(jnp.int32, (1, width), 1) // rows == shard
    slab = jnp.where(owned, jnp.tile(low_gains, (1, grid.fsdp)), jnp.zeros((), LOW))
    slab = jnp.pad(slab, ((0, SLAB - 2), (0, 0)))
    groups = [
        split_columns(g)
        for g in (
            jnp.concatenate([low_attn[0], low_attn[1], low_attn[2], slab], 0),
            jnp.concatenate([low_attn[3], low_down], 0),
        )
    ]
    pairs = width // (2 * HD)
    in_full = lax.all_gather(low_in.reshape(2 * rows, -1), "fsdp")
    in_full = [in_full] if grid.cube else [in_full[:, :rows], in_full[:, rows:]]
    third = Source(grid, in_full, True)

    if grid.cube:
        x = lax.axis_index("dp")
        parts = [lax.dynamic_index_in_dim(g, x, 0, False) for g in groups]
        one, two = Spread(grid, parts[0]), Spread(grid, parts[1])
        one.send_levels()
        one.levels, two.part = after(one.levels, two.part)
        one.load_column()
        one.send_sides()
        two.send_levels()
        (one.side, one.across), two.levels = after((one.side, one.across), two.levels)
        one.send_corners()
        two.load_column()
        two.send_sides()
        one.finish()
        first = Source(grid, one.pieces)
        normed, qkv, full_gains = project_in(grid, first, image, jnp.zeros((SLAB, width), WIDE))
        context = attend(qkv, counts)
        context, two.side, two.across = lax.optimization_barrier((context, two.side, two.across))
        two.send_corners()
        two.finish()
        second = Source(grid, two.pieces)
        second.down_rows = down_rows

        (output, d_attended, d_context, d_gain_two), out_grads, in_grads = feed_forward(
            grid, second, third, image, context, e, counts, full_gains
        )
        three = Reduce(grid, *in_grads)
        three.send_core()
        two_keep, two_sent = out_grads
        two_got = grid.flip_core(two_sent)
        cut = max(1, pairs // 6)
        d_qkv = [attend_back(qkv, d_context, counts, 0, cut)]
        three.got, d_qkv = after(three.got, d_qkv)
        sides = three.load_sides()
        three.send_sides(sides)
        _, (two_got, d_context) = after(sides, (two_got, d_context))
        shape = (2, grid.nz, 2) + two_keep.shape[2:]
        two = Fold(grid, [two_keep.reshape(shape), two_got.reshape(shape)])
        bits = two.by_bits(1)
        x, z, y, c = grid.place()
        leave = two.leave(bits, lax.rem(z, 2))
        leave, d_context = after([leave[0], leave[1]], d_context)
        arrived = [grid.swap_z(v, 1) for v in leave]
        d_qkv.append(attend_back(qkv, d_context, counts, cut, pairs - cut))
        input_grad, grads = project_back(
            grid, first, image, normed, d_qkv, d_attended, full_gains, d_gain_two
        )
        for bit in range(1, bits):
            grads, arrived = after(grads, arrived)
            two.parts.append(jnp.stack(arrived) if bit == 1 else arrived)
            leave, three.sides = after(two.leave(bits - bit, lax.rem(z >> bit, 2)), three.sides)
            arrived = grid.swap_z(leave, 1 << bit)
        one = Reduce(grid, *grads)
        one.send_core()
        leave = fold_column(three)
        in_three = grid.swap_z(leave, 1)
        leave, one.got = after(leave, one.got)
        sides = one.load_sides()
        one.send_sides(sides)
        _, (arrived, in_three) = after(sides, (arrived, in_three))
        two.parts.append(arrived)
        arrived = grid.flip_y(two.leave(1, y))
        rest = [z ^ k for k in range(0, grid.nz, 2)]
        kept = [lax.dynamic_index_in_dim(three.split(v), x, 0, False) for v in (three.keep, three.got)]
        kept = [lax.dynamic_index_in_dim(v, y, 1, False) for v in kept] + three.sides
        kept = [jnp.stack([lax.dynamic_index_in_dim(v, k, 0, False) for k in rest]) for v in kept]
        three = Fold(grid, kept + [in_three])
        bits = three.by_bits(0)
        for bit in range(1, bits + 1):
            in_three = grid.swap_z(three.leave(bits - bit, 0), 1 << bit)
            three.parts.append(in_three)
        one.load_levels()
        one.send_levels()
        _, arrived = after(one.leave, arrived)
        two.parts.append(arrived)
        leave = two.leave(0, x)
        arrived = grid.flip_x(leave)
        two.parts.append(arrived)
        _, in_three = after(leave, in_three)
        three.parts[-1] = in_three
        three.total = three.total()
        two.total = two.total()
        totals = (three.total, two.total)
        one.total, squared = finish(grid, one.own, one.arrive, totals, SLAB)
        _, totals = after(squared, totals)
        three.other, two.other = (grid.flip_x(v) for v in totals)
        one.send_total()
        grad_norm = jnp.sqrt(total_of(grid, squared[0]))
        reduced = [(g.total, g.other) for g in (one, two, three)]
    else:
        groups = [lax.all_gather(g, "fsdp", axis=1) for g in groups]

        def whole(full, low, n):
            full = full[:, :, low : low + n].reshape(2, grid.fsdp * n, full.shape[3])
            return jnp.concatenate([full[0], full[1]], -1)

        slabs = jnp.sum(groups[0][:, :, 3 * rows :].astype(WIDE), 1)
        first = Source(grid, [whole(groups[0], j * rows, rows) for j in range(3)], True)
        second = Source(
            grid, [whole(groups[1], 0, rows), whole(groups[1], rows, down_rows)], True
        )
        second.down_rows = down_rows
        normed, qkv, full_gains = project_in(
            grid, first, image, jnp.concatenate([slabs[0], slabs[1]], -1)
        )
        context = attend(qkv, counts)
        (output, d_attended, d_context, d_gain_two), out_grads, in_grads = feed_forward(
            grid, second, third, image, context, e, counts, full_gains
        )
        d_qkv = [attend_back(qkv, d_context, counts, 0, pairs)]
        input_grad, grads = project_back(
            grid, first, image, normed, d_qkv, d_attended, full_gains, d_gain_two
        )

        reduced = []
        for (g,) in (grads, out_grads, in_grads):
            total = lax.psum_scatter(g.astype(WIDE), "fsdp", scatter_dimension=1)
            reduced.append(lax.psum(total.astype(LOW), "dp"))
        x = jnp.int32(0)
        mine = owned.reshape(2, 1, width // 2)
        slabs = jnp.where(mine, reduced[0][:, 3 * rows :], jnp.zeros((), LOW))
        squared = squares(reduced[0][:, : 3 * rows]) + squares(slabs)
        squared = squared + squares(reduced[1]) + squares(reduced[2])
        grad_norm = jnp.sqrt(total_of(grid, squared))

    updated = update(
        grid,
        grad_norm,
        x,
        (w_attn, w_in, w_down, gains),
        (m_attn, m_in, m_down, m_gains),
        (v_attn, v_in, v_down, v_gains),
        reduced,
    )
    return (output[None], input_grad[None], grad_norm, *updated)


def solution(mesh):
    placed = (
        P(("dp", "fsdp"), None, None),
        P(("dp", "fsdp")),
        P(("dp", "fsdp"), None, None),
        P(None, "fsdp", None),
        P(None, "fsdp", None),
        P("fsdp", None),
        P(None, "fsdp"),
        P(None, "fsdp", None),
        P(None, "fsdp", None),
        P("fsdp", None),
        P(None, "fsdp"),
        P(None, "fsdp", None),
        P(None, "fsdp", None),
        P("fsdp", None),
        P(None, "fsdp"),
    )
    grid = Grid(mesh.shape["dp"], mesh.shape["fsdp"])
    return jax.shard_map(
        functools.partial(on_device, grid),
        mesh=mesh,
        in_specs=placed,
        out_specs=(
            P(("dp", "fsdp"), None, None),
            P(("dp", "fsdp"), None, None),
            P(),
            P(None, "fsdp", None),
            P(None, "fsdp", None),
            P("fsdp", None),
            P(None, "fsdp"),
            P(None, "fsdp", None),
            P(None, "fsdp", None),
            P("fsdp", None),
            P(None, "fsdp"),
            P(None, "fsdp", None),
            P(None, "fsdp", None),
            P("fsdp", None),
            P(None, "fsdp"),
        ),
        check_vma=False,
    )
```
